256 devices in a mesh: rows: 32 (over z_hi, y, core), sub: 8 (over x, z_lo).
Axes of the slice: x: 4, y: 4, z: 8 (z_hi: 4, z_lo: 2; z = z_hi * 2 + z_lo), core: 2. Of those that a mesh axis runs over, the one named last changes fastest.
Arguments:
- features: bfloat16 [1048576, 512], P(('rows', 'sub')), may hold values from -16 to 16
- residual: float32 [1048576, 128], P(('rows', 'sub')), may hold values from -6 to 6
- coefficients: float32 [1048576, 128], P(('rows', 'sub')), may hold values from -6 to 6
- block_owner: int32 [2], replicated, may hold values from 0 to 255
- block_tiles: int32 [2, 4], replicated, may hold values from 0 to 31, as said below
Outputs:
- residual_out: float32 [1048576, 128], P(('rows', 'sub'))
- coefficients_out: float32 [1048576, 128], P(('rows', 'sub'))
The draws below stay inside these ranges and needn't reach their ends.
Inputs may be any that keep to these rules, and one draw needn't show every extreme that they name: `block_tiles`: in each step the tile numbers are distinct, and tiles 0 and 31 are among them.
All inputs are finite; a program needn't handle non-finite values.
Results may differ from the reference program's by a relative error of at most 0.0012.
Values may be sent and summed in bfloat16 or wider, within the bound.
A program may use at most 128 MiB of HBM per device.

```python
import math
import jax
import jax.numpy as jnp
from jax import lax

F = 512
C = 128
BLOCK = 512
TILE = 128
STEPS = 2
ROWS_DEV = 4096
NROWS = 1048576
DEVICES = 256


def draw_features(key, part):
    key = jax.random.fold_in(key, 11)
    latent_key, scale_key, random_key = jax.random.split(key, 3)
    latent_dims = 16
    latent = jax.random.normal(latent_key, (NROWS, latent_dims), jnp.float32)
    column_scale = jax.random.uniform(scale_key, (F,), jnp.float32, 0.8, 1.2)
    spread = 0.45
    random_part = jax.random.normal(random_key, (NROWS, F), jnp.float32)
    shared = jnp.tile(latent, (1, F // latent_dims))
    values = 1.1 * shared * column_scale[None, :] + spread * random_part
    return jnp.clip(values, -16.0, 16.0).astype(jnp.bfloat16)


def draw_block_tiles(key, part):
    key = jax.random.fold_in(key, 7)
    step_keys = jax.random.split(key, STEPS)
    tiles_dev = ROWS_DEV // TILE
    block_tiles = BLOCK // TILE

    def pick_tiles(one_key):
        first_key, second_key = jax.random.split(one_key)
        middle = jax.random.permutation(first_key, tiles_dev - 2)[:block_tiles - 2].astype(jnp.int32) + 1
        ends = jnp.array([0, tiles_dev - 1], dtype=jnp.int32)
        chosen = jnp.concatenate([ends, middle])
        order = jax.random.permutation(second_key, block_tiles)
        return chosen[order].astype(jnp.int32)
    return jax.vmap(pick_tiles)(step_keys)


def level_of(own_key, shape, pieces, least, largest):
    def one(dim, shards_of):
        draws = jax.random.uniform(jax.random.fold_in(jax.random.fold_in(own_key, 6), dim), (shards_of,), jnp.float32, least / len(pieces), largest / len(pieces))
        return jnp.repeat(jnp.exp(draws), shape[dim] // shards_of).reshape((-1,) + (1,) * (len(shape) - dim - 1))

    gain = one(*pieces[0])
    for cut in pieces[1:]:
        gain = gain * one(*cut)
    return gain


def normal_values(stream_key, shape, deviation, most, pieces=(), kind=jnp.bfloat16):
    loudness = level_of(stream_key, shape, pieces, -0.22, 0.18) if pieces else 1.0
    result = jax.random.normal(stream_key, shape, jnp.float32) * deviation * loudness
    return jnp.minimum(jnp.maximum(result, -most), most).astype(kind)


def setup_inputs(seed: int = 0) -> dict:
    key_of = jax.random.split(jax.random.key(seed), 6)
    features = draw_features(jax.random.fold_in(key_of[5], 71), 0)
    residual = normal_values(key_of[1], (NROWS, C), 1.0, 6.0, ((0, 256),), jnp.float32)
    coefficients = normal_values(key_of[2], (NROWS, C), 1.0, 6.0, ((0, 256),), jnp.float32)
    block_owner = jax.random.randint(key_of[3], (STEPS,), 0, DEVICES).astype(jnp.int32)
    block_tiles = draw_block_tiles(jax.random.fold_in(key_of[5], 71), 0)
    return {"features": features, "residual": residual, "coefficients": coefficients, "block_owner": block_owner, "block_tiles": block_tiles}


RIDGE = 0.5

def kernel_block(left_rows, right_rows, left_norm, right_norm, kernel_scale):
    cross_dot = jnp.dot(left_rows.astype(jnp.float32), right_rows.astype(jnp.float32).T)
    distance = left_norm[:, None] + right_norm[None, :] - 2.0 * cross_dot
    return jnp.exp(-kernel_scale * distance)

def block_solve(kernel_bb, gradient):
    size_now = kernel_bb.shape[0]
    system = kernel_bb + RIDGE * jnp.eye(size_now, dtype=jnp.float32)
    factor = jnp.linalg.cholesky(system)
    half_way = lax.linalg.triangular_solve(factor, gradient, left_side=True, lower=True)
    return lax.linalg.triangular_solve(factor, half_way, left_side=True, lower=True, transpose_a=True)

def reference(features, residual, coefficients, block_owner, block_tiles):
    devices = features.shape[0] // ROWS_DEV
    kernel_scale = 1.0 / F
    step_size = 1.0 / math.sqrt(ROWS_DEV * devices)
    shards = features.reshape(devices, ROWS_DEV, F)
    norms = lax.optimization_barrier(jnp.sum(jnp.square(features.astype(jnp.float32)), axis=1)).reshape(devices, ROWS_DEV)
    for step_index in range(STEPS):
        owner_now = block_owner[step_index]
        tile_ids = block_tiles[step_index]
        block_rows = shards[owner_now].reshape(ROWS_DEV // TILE, TILE, F)[tile_ids].reshape(BLOCK, F)
        block_norm = lax.optimization_barrier(jnp.sum(jnp.square(block_rows.astype(jnp.float32)), axis=1))
        weighted = (residual - RIDGE * coefficients).astype(jnp.bfloat16).reshape(devices, ROWS_DEV, C)

        def partial_term(inputs):
            shard_rows, shard_norm, shard_weight = inputs
            slab = kernel_block(shard_rows, block_rows, shard_norm, block_norm, kernel_scale).astype(jnp.bfloat16)
            return jnp.einsum('rb,rc->bc', slab.astype(jnp.float32), shard_weight.astype(jnp.float32))
        terms = lax.map(partial_term, (shards, norms, weighted))
        gradient = lax.optimization_barrier(jnp.sum(terms, axis=0))
        kernel_bb = kernel_block(block_rows, block_rows, block_norm, block_norm, kernel_scale)
        update = block_solve(kernel_bb, gradient) * step_size
        update_low = update.astype(jnp.bfloat16)

        def new_residual(inputs):
            shard_rows, shard_norm, shard_residual = inputs
            slab = kernel_block(shard_rows, block_rows, shard_norm, block_norm, kernel_scale).astype(jnp.bfloat16)
            return shard_residual - jnp.dot(slab.astype(jnp.float32), update_low.astype(jnp.float32))
        residual = lax.map(new_residual, (shards, norms, residual.reshape(devices, ROWS_DEV, C))).reshape(devices * ROWS_DEV, C)
        row_index = (owner_now * ROWS_DEV + tile_ids[:, None] * TILE + jnp.arange(TILE, dtype=jnp.int32)[None, :]).reshape(-1).astype(jnp.int32)
        coefficients = coefficients.at[row_index].add(update)
    return (residual, coefficients)
```

```python
import functools
import math

import jax
import jax.numpy as jnp
from jax import lax
from jax.experimental import pallas as pl
from jax.experimental.pallas import tpu as pltpu
from jax.sharding import PartitionSpec as P

MESH = pl.DeviceIdType.MESH
HI = lax.Precision.HIGHEST
F32 = jnp.float32
BF16 = jnp.bfloat16

BLOCK = 512
TILE = 128
STEPS = 2
RIDGE = 0.5
WIDTH = 512
TARGETS = 128
NX, NY, NZ = 4, 4, 8
NQ = NX * NY
CHUNK = 512
VMEM_BYTES = 56 << 20


def vmem():
    return pl.BlockSpec(memory_space=pltpu.VMEM)


def smem():
    return pl.BlockSpec(memory_space=pltpu.SMEM)


def dot(a, b, precision=None):
    return jnp.dot(a, b, precision=precision, preferred_element_type=F32)


def dot_nt(a, b, precision=None):
    return lax.dot_general(
        a, b, (((1,), (1,)), ((), ())), precision=precision, preferred_element_type=F32
    )


def place():
    across, within = lax.axis_index("rows"), lax.axis_index("sub")
    core = lax.rem(across, 2)
    y = lax.rem(lax.div(across, 2), NY)
    z = lax.div(across, 2 * NY) * 2 + lax.rem(within, 2)
    x = lax.div(within, 2)
    return x * NY + y, z, core


def device(q, z, core):
    x, y = lax.div(q, NY), lax.rem(q, NY)
    return (lax.div(z, 2) * (2 * NY) + y * 2 + core, x * 2 + lax.rem(z, 2))


def ring(start, step, size):
    return lax.rem(start + step, size)


def greet(q, z, core):
    barrier = pltpu.get_barrier_semaphore()
    pl.semaphore_signal(barrier, inc=1, device_id=device(q, z, 1 - core), device_id_type=MESH)

    @pl.loop(1, NQ)
    def _(i):
        pl.semaphore_signal(
            barrier, inc=1, device_id=device(ring(q, i, NQ), z, core), device_id_type=MESH
        )

    @pl.loop(1, NZ)
    def _(i):
        pl.semaphore_signal(
            barrier, inc=1, device_id=device(q, ring(z, i, NZ), core), device_id_type=MESH
        )

    pl.semaphore_wait(barrier, 1 + (NQ - 1) + (NZ - 1))


def remote(source, target, send_sem, recv_sem, where):
    return pltpu.make_async_remote_copy(
        src_ref=source,
        dst_ref=target,
        send_sem=send_sem,
        recv_sem=recv_sem,
        device_id=where,
        device_id_type=MESH,
    )


STAGE_SEMS = [
    pltpu.SemaphoreType.DMA((2, NQ)),
    pltpu.SemaphoreType.DMA((2, NQ)),
    pltpu.SemaphoreType.DMA((2, 2, NZ)),
    pltpu.SemaphoreType.DMA((2, 2, NZ)),
    pltpu.SemaphoreType.DMA((2, NQ)),
    pltpu.SemaphoreType.DMA((2, NQ)),
]


class Sum:
    def __init__(self, part, total, recv_a, half, recv_b, cut, recv_c, joined, sems, spot):
        self.part, self.total, self.recv_a, self.half = part, total, recv_a, half
        self.recv_b, self.cut, self.recv_c, self.joined = recv_b, cut, recv_c, joined
        self.sems = sems
        self.q, self.z, self.core = spot
        self.rows, self.lanes = half.shape[1], half.shape[2]
        self.high = cut.shape[1]
        self.tiles = cut.shape[0]
        self.rounds = 2 if self.tiles > NZ else 1

    def a_copy(self, i):
        q, z, core = self.q, self.z, self.core
        at = ring(q, i, NQ)
        sem = self.sems[0]
        return remote(
            self.part.at[1 - core, at],
            self.recv_a.at[at],
            sem.at[0, at],
            sem.at[1, at],
            device(q, z, 1 - core),
        )

    def start_a(self):
        @pl.loop(1, NQ + 1)
        def _(i):
            self.a_copy(i).start()

    def b_copy(self, i, arriving):
        q, z, core = self.q, self.z, self.core
        there = ring(q, i, NQ)
        sem = self.sems[1]
        slot = there if arriving else q
        return remote(
            self.half.at[there],
            self.recv_b.at[slot],
            sem.at[0, there],
            sem.at[1, slot],
            device(there, z, core),
        )

    def a_to_b(self):
        @pl.loop(1, NQ + 1)
        def _(i):
            at = ring(self.q, i, NQ)
            self.a_copy(i).wait_recv()
            self.half[at] = self.part[self.core, at] + self.recv_a[at]

            @pl.when(i < NQ)
            def _():
                self.b_copy(i, False).start()

    def tile_of(self, z, turn):
        return z if turn == 0 else NZ + lax.rem(z, 4)

    def c_copy(self, i, turn, arriving):
        q, z, core = self.q, self.z, self.core
        there = ring(z, i, NZ)
        sem = self.sems[2]
        slot = there if arriving else z
        return remote(
            self.cut.at[self.tile_of(there, turn)],
            self.recv_c.at[turn, slot],
            sem.at[0, turn, there],
            sem.at[1, turn, slot],
            device(q, there, core),
        )

    def b_to_c(self):
        self.recv_b[self.q] = self.half[self.q]

        @pl.loop(1, NQ)
        def _(i):
            self.b_copy(i, True).wait_recv()

        chunk = self.recv_b[0]
        for i in range(1, NQ):
            chunk = chunk + self.recv_b[i]
        across = self.lanes // 128
        for t in range(self.tiles):
            down, along = t // across, t % across
            self.cut[t] = chunk[
                down * self.high : (down + 1) * self.high, along * 128 : (along + 1) * 128
            ]

        @pl.loop(1, NZ)
        def _(i):
            for turn in range(self.rounds):
                self.c_copy(i, turn, False).start()

    def d_copy(self, i, turn, arriving):
        q, z, core = self.q, self.z, self.core
        sem = self.sems[3]
        if turn == 0:
            there = ring(z, i, NZ)
        else:
            there = lax.div(z, 4) * 4 + lax.rem(lax.rem(z, 4) + i, 4)
        slot = there if arriving else z
        tile = self.tile_of(slot, turn)
        return remote(
            self.joined.at[self.tile_of(z, turn)],
            self.joined.at[tile],
            sem.at[0, turn, there],
            sem.at[1, turn, slot],
            device(q, there, core),
        )

    def c_to_d(self):
        for turn in range(self.rounds):
            self.recv_c[turn, self.z] = self.cut[self.tile_of(self.z, turn)]

            @pl.loop(1, NZ)
            def _(i):
                self.c_copy(i, turn, True).wait_recv()

            tile = self.recv_c[turn, 0]
            for i in range(1, NZ):
                tile = tile + self.recv_c[turn, i]
            self.joined[self.tile_of(self.z, turn)] = tile

            @pl.loop(1, NZ if turn == 0 else 4)
            def _(i):
                self.d_copy(i, turn, False).start()

    def e_copy(self, i, arriving):
        q, z, core = self.q, self.z, self.core
        there = ring(q, i, NQ)
        sem = self.sems[4]
        slot = there if arriving else q
        return remote(
            self.total.at[core, q],
            self.total.at[core, slot],
            sem.at[0, there],
            sem.at[1, slot],
            device(there, z, core),
        )

    def f_copy(self, i, arriving):
        q, z, core = self.q, self.z, self.core
        at = ring(q, i, NQ)
        sem = self.sems[5]
        return remote(
            self.total.at[core, at],
            self.total.at[1 - core if arriving else core, at],
            sem.at[0, at],
            sem.at[1, at],
            device(q, z, 1 - core),
        )

    def d_to_e(self):
        for turn in range(self.rounds):

            @pl.loop(1, NZ if turn == 0 else 4)
            def _(i):
                self.d_copy(i, turn, True).wait_recv()

        across = self.lanes // 128
        for t in range(self.tiles):
            down, along = t // across, t % across
            self.total[
                self.core,
                self.q,
                down * self.high : (down + 1) * self.high,
                along * 128 : (along + 1) * 128,
            ] = self.joined[t]

        @pl.loop(1, NQ)
        def _(i):
            self.e_copy(i, False).start()

        self.f_copy(0, False).start()

    def e_to_f(self):
        @pl.loop(1, NQ)
        def _(i):
            self.e_copy(i, True).wait_recv()
            self.f_copy(i, False).start()

    def finish(self):
        @pl.loop(0, NQ)
        def _(i):
            self.f_copy(i, True).wait_recv()
            self.f_copy(i, False).wait_send()
            self.a_copy(i).wait_send()

        @pl.loop(1, NQ)
        def _(i):
            self.b_copy(i, False).wait_send()
            self.e_copy(i, False).wait_send()

        for turn in range(self.rounds):

            @pl.loop(1, NZ)
            def _(i):
                self.c_copy(i, turn, False).wait_send()

            @pl.loop(1, NZ if turn == 0 else 4)
            def _(i):
                self.d_copy(i, turn, False).wait_send()


def sum_scratch(rows, lanes, dtype):
    high = 16 if dtype == BF16 else 8
    tiles = (rows // high) * (lanes // 128)
    rounds = 2 if tiles > NZ else 1
    return [
        pltpu.VMEM((NQ, rows, lanes), dtype),
        pltpu.VMEM((NQ, rows, lanes), dtype),
        pltpu.VMEM((NQ, rows, lanes), dtype),
        pltpu.VMEM((tiles, high, 128), dtype),
        pltpu.VMEM((rounds, NZ, high, 128), dtype),
        pltpu.VMEM((tiles, high, 128), dtype),
        *STAGE_SEMS,
    ]


def fetch_kernel(owner_ref, tiles_ref, feat_ref, out_ref, part, *scratch):
    q, z, core = place()
    me = lax.axis_index("rows") * lax.axis_size("sub") + lax.axis_index("sub")
    rows = part.shape[2]
    per_tile = TILE // rows
    for s in range(STEPS):
        mine = jnp.full((rows, WIDTH), (owner_ref[s] == me).astype(F32)).astype(BF16)
        for t in range(BLOCK // TILE):
            tile = feat_ref[tiles_ref[s, t]]
            for i in range(per_tile):
                part[s, t * per_tile + i] = tile[i * rows : (i + 1) * rows] * mine
    greet(q, z, core)
    run = Sum(part, out_ref, *scratch[:6], scratch[6:], (q, z, core))
    run.start_a()
    run.a_to_b()
    run.b_to_c()
    run.c_to_d()
    run.d_to_e()
    run.e_to_f()
    run.finish()


def fetch_blocks(block_owner, block_tiles, features):
    rows = BLOCK // NQ
    shape = (STEPS, NQ, rows, WIDTH)
    out = pl.pallas_call(
        fetch_kernel,
        out_shape=jax.ShapeDtypeStruct(shape, BF16),
        in_specs=[smem(), smem(), vmem()],
        out_specs=vmem(),
        scratch_shapes=[pltpu.VMEM(shape, BF16), *sum_scratch(rows, WIDTH, BF16)],
        compiler_params=pltpu.CompilerParams(
            collective_id=0, has_side_effects=True, vmem_limit_bytes=VMEM_BYTES
        ),
        name="fetch_blocks",
    )(block_owner, block_tiles, features.reshape(-1, TILE, WIDTH))
    return out.reshape(STEPS * BLOCK, WIDTH)


LOG2E_SCALED = math.log2(math.e) / WIDTH


def column_norms(rows):
    wide = rows.astype(F32)
    return jnp.sum(wide * wide, axis=1, keepdims=True)


def slab_kernel(block_ref, feat_ref, res_ref, coef_ref, slab_ref, part_ref, norm_ref):
    @pl.when(pl.program_id(0) == 0)
    def _():
        norm = column_norms(block_ref[...]) * LOG2E_SCALED
        norm_ref[...] = jnp.broadcast_to(norm, norm_ref.shape)
        part_ref[...] = jnp.zeros_like(part_ref)

    feat = feat_ref[...]
    norms = column_norms(feat) * LOG2E_SCALED
    along = jnp.transpose(jnp.broadcast_to(norms, (CHUNK, 128)))[0:1, :]
    weighted = (res_ref[...] - RIDGE * coef_ref[...]).astype(BF16)
    slabs = []
    for s in range(STEPS):
        at = pl.ds(s * BLOCK, BLOCK)
        cross = dot_nt(block_ref[at, :], feat)
        power = (2.0 * LOG2E_SCALED) * cross - along - norm_ref[at, 0:1]
        slab = jnp.exp2(power).astype(BF16)
        slab_ref[at, :] = slab
        slabs.append(slab)
        part_ref[:, s * TARGETS : (s + 1) * TARGETS] += dot(slab, weighted)
    part_ref[:, STEPS * TARGETS :] += dot_nt(slabs[1], slabs[0])


def slab_parts(blocks, features, residual, coefficients):
    rows = features.shape[0]
    return pl.pallas_call(
        slab_kernel,
        grid=(rows // CHUNK,),
        out_shape=(
            jax.ShapeDtypeStruct((STEPS * BLOCK, rows), BF16),
            jax.ShapeDtypeStruct((BLOCK, STEPS * TARGETS + BLOCK), F32),
        ),
        in_specs=[
            pl.BlockSpec((STEPS * BLOCK, WIDTH), lambda i: (0, 0)),
            pl.BlockSpec((CHUNK, WIDTH), lambda i: (i, 0)),
            pl.BlockSpec((CHUNK, TARGETS), lambda i: (i, 0)),
            pl.BlockSpec((CHUNK, TARGETS), lambda i: (i, 0)),
        ],
        out_specs=(
            pl.BlockSpec((STEPS * BLOCK, CHUNK), lambda i: (0, i)),
            pl.BlockSpec((BLOCK, STEPS * TARGETS + BLOCK), lambda i: (0, 0)),
        ),
        scratch_shapes=[pltpu.VMEM((STEPS * BLOCK, 128), F32)],
        compiler_params=pltpu.CompilerParams(vmem_limit_bytes=VMEM_BYTES),
        name="slab_parts",
    )(blocks, features, residual, coefficients)


PANEL = 4


def invert_tile(mats):
    n = TILE
    row = lax.broadcasted_iota(jnp.int32, (n, n), 0)
    lane = lax.broadcasted_iota(jnp.int32, (n, n), 1)
    mats = list(mats)
    for first in range(0, n, PANEL):
        columns = [
            [jnp.broadcast_to(a[:, first + j : first + j + 1], (n, n)) for j in range(PANEL)]
            for a in mats
        ]
        for j in range(PANEL):
            k = first + j
            for m, a in enumerate(mats):
                column = columns[m][j]
                inverse = 1.0 / column[k : k + 1, :]
                column = jnp.where(row == k, column - 1.0, column)
                a = jnp.where(lane == k, jnp.where(row == k, 1.0, 0.0), a)
                mats[m] = a - column * (a[k : k + 1, :] * inverse)
                for jj in range(j + 1, PANEL):
                    other = columns[m][jj]
                    columns[m][jj] = other - column * (other[k : k + 1, :] * inverse)
    return mats


def invert_kernel(block_ref, inv_ref, between_ref):
    blocks = block_ref[...]
    norms = column_norms(blocks) * LOG2E_SCALED
    along = jnp.transpose(jnp.broadcast_to(norms, (STEPS * BLOCK, 128)))[0:1, :]
    row = lax.broadcasted_iota(jnp.int32, (BLOCK, BLOCK), 0)
    lane = lax.broadcasted_iota(jnp.int32, (BLOCK, BLOCK), 1)

    def kernel(left, right):
        a, b = left * BLOCK, right * BLOCK
        cross = dot_nt(blocks[a : a + BLOCK], blocks[b : b + BLOCK])
        return jnp.exp2(
            (2.0 * LOG2E_SCALED) * cross - along[:, b : b + BLOCK] - norms[a : a + BLOCK]
        )

    for s in range(STEPS):
        inv_ref[s] = kernel(s, s) + jnp.where(row == lane, RIDGE, 0.0)
    between_ref[...] = kernel(1, 0).astype(BF16)

    def eliminate(k, carry):
        at = pl.ds(pl.multiple_of(k * TILE, TILE), TILE)
        tiles = invert_tile([inv_ref[s, at, at] for s in range(STEPS)])
        inside = lax.div(lax.broadcasted_iota(jnp.int32, (TILE, BLOCK), 1), TILE) == k
        for s in range(STEPS):
            lead = dot(tiles[s], inv_ref[s, at, :], HI)
            lead = jnp.where(inside, jnp.concatenate([tiles[s]] * (BLOCK // TILE), axis=1), lead)
            column = inv_ref[s, :, at]
            inv_ref[s, :, at] = jnp.zeros_like(column)
            inv_ref[s] -= dot(column, lead, HI)
            inv_ref[s, at, :] = lead
        return carry

    lax.fori_loop(0, BLOCK // TILE, eliminate, 0)


def invert_blocks(blocks):
    return pl.pallas_call(
        invert_kernel,
        out_shape=(
            jax.ShapeDtypeStruct((STEPS, BLOCK, BLOCK), F32),
            jax.ShapeDtypeStruct((BLOCK, BLOCK), BF16),
        ),
        in_specs=[vmem()],
        out_specs=(vmem(), vmem()),
        compiler_params=pltpu.CompilerParams(vmem_limit_bytes=VMEM_BYTES),
        name="invert_blocks",
    )(blocks)


def reduce_kernel(part_ref, out_ref, *scratch):
    spot = place()
    greet(*spot)
    run = Sum(part_ref, out_ref, *scratch[:6], scratch[6:], spot)
    run.start_a()
    run.a_to_b()
    run.b_to_c()
    run.c_to_d()
    run.d_to_e()
    run.e_to_f()
    run.finish()


def reduce_parts(parts):
    height, lanes = parts.shape
    rows = height // (2 * NQ)
    shape = (2, NQ, rows, lanes)
    out = pl.pallas_call(
        reduce_kernel,
        out_shape=jax.ShapeDtypeStruct(shape, F32),
        in_specs=[vmem()],
        out_specs=vmem(),
        scratch_shapes=sum_scratch(rows, lanes, F32),
        compiler_params=pltpu.CompilerParams(
            collective_id=1, has_side_effects=True, vmem_limit_bytes=VMEM_BYTES
        ),
        name="reduce_parts",
    )(parts.reshape(shape))
    return out.reshape(height, lanes)


def final_kernel(
    step_size,
    owner_ref,
    tiles_ref,
    sum_ref,
    inv_ref,
    between_ref,
    slab_ref,
    res_ref,
    coef_ref,
    res_out,
    coef_out,
    update_ref,
    low_ref,
):
    step = pl.program_id(0)

    @pl.when(step == 0)
    def _():
        first = dot(inv_ref[0], sum_ref[:, :TARGETS], HI) * step_size
        first_low = first.astype(BF16)
        gradient = (
            sum_ref[:, TARGETS : 2 * TARGETS]
            - dot(sum_ref[:, 2 * TARGETS :], first_low.astype(F32), HI)
            - RIDGE * dot(between_ref[...].astype(F32), first, HI)
        )
        second = dot(inv_ref[1], gradient, HI) * step_size
        update_ref[0:BLOCK] = first
        update_ref[BLOCK:] = second
        low_ref[...] = jnp.transpose(update_ref[...]).astype(BF16)

    res_out[...] = res_ref[...] - jnp.transpose(dot(low_ref[...], slab_ref[...]))
    coef_out[...] = coef_ref[...]
    me = lax.axis_index("rows") * lax.axis_size("sub") + lax.axis_index("sub")
    tiles_here = CHUNK // TILE
    for s in range(STEPS):
        for t in range(BLOCK // TILE):
            tile = tiles_ref[s, t]

            @pl.when((owner_ref[s] == me) & (lax.div(tile, tiles_here) == step))
            def _():
                at = pl.ds(pl.multiple_of(lax.rem(tile, tiles_here) * TILE, TILE), TILE)
                coef_out[at, :] += update_ref[pl.ds(s * BLOCK + t * TILE, TILE), :]


def final(step_size, owner, tiles, sums, inverses, between, slabs, residual, coefficients):
    rows = residual.shape[0]
    whole2 = lambda i: (0, 0)
    chunk = pl.BlockSpec((CHUNK, TARGETS), lambda i: (i, 0))
    return pl.pallas_call(
        functools.partial(final_kernel, step_size),
        grid=(rows // CHUNK,),
        out_shape=(
            jax.ShapeDtypeStruct(residual.shape, F32),
            jax.ShapeDtypeStruct(coefficients.shape, F32),
        ),
        in_specs=[
            smem(),
            smem(),
            pl.BlockSpec(sums.shape, whole2),
            pl.BlockSpec(inverses.shape, lambda i: (0, 0, 0)),
            pl.BlockSpec(between.shape, whole2),
            pl.BlockSpec((STEPS * BLOCK, CHUNK), lambda i: (0, i)),
            chunk,
            chunk,
        ],
        out_specs=(chunk, chunk),
        scratch_shapes=[
            pltpu.VMEM((STEPS * BLOCK, TARGETS), F32),
            pltpu.VMEM((TARGETS, STEPS * BLOCK), BF16),
        ],
        compiler_params=pltpu.CompilerParams(vmem_limit_bytes=VMEM_BYTES),
        name="final",
    )(owner, tiles, sums, inverses, between, slabs, residual, coefficients)


def local(features, residual, coefficients, block_owner, block_tiles):
    devices = lax.axis_size("rows") * lax.axis_size("sub")
    step_size = 1.0 / math.sqrt(features.shape[0] * devices)
    blocks = fetch_blocks(block_owner, block_tiles, features)
    slabs, parts = slab_parts(blocks, features, residual, coefficients)
    sums = reduce_parts(parts)
    inverses, between = invert_blocks(blocks)
    return final(
        step_size,
        block_owner,
        block_tiles,
        sums,
        inverses,
        between,
        slabs,
        residual,
        coefficients,
    )


def solution(mesh):
    in_specs = (
        P(("rows", "sub"), None),
        P(("rows", "sub"), None),
        P(("rows", "sub"), None),
        P(),
        P(),
    )
    out_specs = (P(("rows", "sub"), None), P(("rows", "sub"), None))
    return jax.shard_map(local, mesh=mesh, in_specs=in_specs, out_specs=out_specs, check_vma=False)
```

```python
import functools
import math

import jax
import jax.numpy as jnp
from jax import lax
from jax.experimental import pallas as pl
from jax.experimental.pallas import tpu as pltpu
from jax.sharding import PartitionSpec as P

MESH = pl.DeviceIdType.MESH
HI = lax.Precision.HIGHEST
F32 = jnp.float32
BF16 = jnp.bfloat16

BLOCK = 512
TILE = 128
STEPS = 2
RIDGE = 0.5
WIDTH = 512
TARGETS = 128
NX, NY, NZ = 4, 4, 8
NQ = NX * NY
CHUNK = 1024


def vmem():
    return pl.BlockSpec(memory_space=pltpu.VMEM)


def smem():
    return pl.BlockSpec(memory_space=pltpu.SMEM)


def dot(a, b, precision=None):
    return jnp.dot(a, b, precision=precision, preferred_element_type=F32)


def dot_nt(a, b, precision=None):
    return lax.dot_general(
        a, b, (((1,), (1,)), ((), ())), precision=precision, preferred_element_type=F32
    )


def place():
    across, within = lax.axis_index("rows"), lax.axis_index("sub")
    core = lax.rem(across, 2)
    y = lax.rem(lax.div(across, 2), NY)
    z = lax.div(across, 2 * NY) * 2 + lax.rem(within, 2)
    x = lax.div(within, 2)
    return x, y, z, core


def device(x, y, z, core):
    return (lax.div(z, 2) * (2 * NY) + y * 2 + core, x * 2 + lax.rem(z, 2))


def around(at, step, size):
    return lax.rem(at + step, size)


def hops(step, size):
    return min(step, size - step)


COLUMNS = sorted(
    [(i, j) for i in range(NX) for j in range(NY) if i or j],
    key=lambda s: -hops(s[0], NX) - hops(s[1], NY),
)
PLANES = sorted(range(1, NZ), key=lambda s: -hops(s, NZ))


def greet(spot):
    x, y, z, core = spot
    barrier = pltpu.get_barrier_semaphore()

    def signal(*where):
        pl.semaphore_signal(barrier, inc=1, device_id=device(*where), device_id_type=MESH)

    for i, j in COLUMNS:
        signal(around(x, i, NX), around(y, j, NY), z, core)
    for k in PLANES:
        signal(x, y, around(z, k, NZ), core)
    signal(x, y, z, 1 - core)
    pl.semaphore_wait(barrier, 1 + len(COLUMNS) + len(PLANES))


def remote(source, target, send_sem, recv_sem, where):
    return pltpu.make_async_remote_copy(
        src_ref=source,
        dst_ref=target,
        send_sem=send_sem,
        recv_sem=recv_sem,
        device_id=device(*where),
        device_id_type=MESH,
    )


NCOL = len(COLUMNS)


class Sum:
    def __init__(self, part, total, recv_a, half, recv_b, recv_c, sems, spot):
        self.part, self.total, self.recv_a, self.half = part, total, recv_a, half
        self.recv_b, self.recv_c = recv_b, recv_c
        self.sems = sems
        self.x, self.y, self.z, self.core = spot
        self.q = self.x * NY + self.y
        self.mate = (self.x, self.y, self.z, 1 - self.core)

    def column(self, i):
        dx, dy = COLUMNS[i] if i < NCOL else (0, 0)
        x, y = around(self.x, dx, NX), around(self.y, dy, NY)
        return (x, y, self.z, self.core), x * NY + y

    def column_before(self, i):
        dx, dy = COLUMNS[i] if i < NCOL else (0, 0)
        return around(self.x, NX - dx, NX) * NY + around(self.y, NY - dy, NY)

    def a_copy(self, i):
        at = self.column(i)[1]
        sem = self.sems[0]
        return remote(
            self.part.at[1 - self.core, at], self.recv_a.at[i], sem.at[0, i], sem.at[1, i], self.mate
        )

    def start_a(self):
        for i in range(NQ):
            self.a_copy(i).start()

    def b_copy(self, i):
        sem = self.sems[1]
        return remote(
            self.half.at[i], self.recv_b.at[i], sem.at[0, i], sem.at[1, i], self.column(i)[0]
        )

    def a_to_b(self):
        for i in range(NQ):
            at = self.column(i)[1]
            self.a_copy(i).wait_recv()
            self.half[i] = self.part[self.core, at] + self.recv_a[i]
            if i < NCOL:
                self.b_copy(i).start()

    def c_copy(self, i, slot):
        sem = self.sems[2]
        there = around(self.z, PLANES[i], NZ)
        return remote(
            self.recv_c.at[self.z],
            self.recv_c.at[slot],
            sem.at[0, i],
            sem.at[1, i],
            (self.x, self.y, there, self.core),
        )

    def b_to_c(self):
        chunk = self.half[NCOL]
        for i in reversed(range(NCOL)):
            self.b_copy(i).wait_recv()
            chunk = chunk + self.recv_b[i]
        self.recv_c[self.z] = chunk
        for i in range(len(PLANES)):
            self.c_copy(i, self.z).start()

    def e_copy(self, i, slot):
        sem = self.sems[3]
        return remote(
            self.total.at[self.core, self.q],
            self.total.at[self.core, slot],
            sem.at[0, i],
            sem.at[1, i],
            self.column(i)[0],
        )

    def f_copy(self, i, side):
        at = self.column_before(i)
        sem = self.sems[4]
        return remote(
            self.total.at[self.core, at],
            self.total.at[side, at],
            sem.at[0, i],
            sem.at[1, i],
            self.mate,
        )

    def c_to_e(self):
        for i in range(len(PLANES)):
            self.c_copy(i, around(self.z, NZ - PLANES[i], NZ)).wait_recv()
        chunk = self.recv_c[0]
        for i in range(1, NZ):
            chunk = chunk + self.recv_c[i]
        self.total[self.core, self.q] = chunk
        for i in range(NCOL):
            self.e_copy(i, self.q).start()
        self.f_copy(NCOL, self.core).start()

    def e_to_f(self):
        for i in reversed(range(NCOL)):
            self.e_copy(i, self.column_before(i)).wait_recv()
            self.f_copy(i, self.core).start()

    def finish(self):
        for i in reversed(range(NQ)):
            self.f_copy(i, 1 - self.core).wait_recv()
        for i in range(NQ):
            self.a_copy(i).wait_send()
            self.f_copy(i, self.core).wait_send()
        for i in range(NCOL):
            self.b_copy(i).wait_send()
            self.e_copy(i, self.q).wait_send()
        for i in range(len(PLANES)):
            self.c_copy(i, self.z).wait_send()


def sum_scratch(rows, lanes, dtype):
    return [
        pltpu.VMEM((NQ, rows, lanes), dtype),
        pltpu.VMEM((NQ, rows, lanes), dtype),
        pltpu.VMEM((NCOL, rows, lanes), dtype),
        pltpu.VMEM((NZ, rows, lanes), dtype),
        pltpu.SemaphoreType.DMA((2, NQ)),
        pltpu.SemaphoreType.DMA((2, NCOL)),
        pltpu.SemaphoreType.DMA((2, len(PLANES))),
        pltpu.SemaphoreType.DMA((2, NCOL)),
        pltpu.SemaphoreType.DMA((2, NQ)),
    ]


def fetch_kernel(owner_ref, tiles_ref, feat_hbm, out_ref, feat_ref, feat_sem, part, *scratch):
    load = pltpu.make_async_copy(feat_hbm, feat_ref, feat_sem)
    load.start()
    spot = place()
    core = spot[3]
    greet(spot)
    load.wait()
    me = lax.axis_index("rows") * lax.axis_size("sub") + lax.axis_index("sub")
    rows = part.shape[2]
    per_tile = TILE // rows
    run = Sum(part, out_ref, *scratch[:4], scratch[4:], spot)

    def build(s):
        mine = jnp.full((rows, WIDTH), (owner_ref[s] == me).astype(F32)).astype(BF16)
        for t in range(BLOCK // TILE):
            tile = feat_ref[tiles_ref[s, t]]
            for i in range(per_tile):
                part[s, t * per_tile + i] = tile[i * rows : (i + 1) * rows] * mine

    build(1 - core)
    run.start_a()
    build(core)
    run.a_to_b()
    run.b_to_c()
    run.c_to_e()
    run.e_to_f()
    run.finish()


def fetch_blocks(block_owner, block_tiles, features):
    rows = BLOCK // NQ
    shape = (STEPS, NQ, rows, WIDTH)
    tiled = features.reshape(-1, TILE, WIDTH)
    out = pl.pallas_call(
        fetch_kernel,
        out_shape=jax.ShapeDtypeStruct(shape, BF16),
        in_specs=[smem(), smem(), pl.BlockSpec(memory_space=pl.ANY)],
        out_specs=vmem(),
        scratch_shapes=[
            pltpu.VMEM(tiled.shape, BF16),
            pltpu.SemaphoreType.DMA,
            pltpu.VMEM(shape, BF16),
            *sum_scratch(rows, WIDTH, BF16),
        ],
        compiler_params=pltpu.CompilerParams(
            collective_id=0, has_side_effects=True, vmem_limit_bytes=16 << 20
        ),
        name="fetch_blocks",
    )(block_owner, block_tiles, tiled)
    return out.reshape(STEPS * BLOCK, WIDTH)


LOG2E_SCALED = math.log2(math.e) / WIDTH


def column_norms(rows):
    wide = rows.astype(F32)
    return jnp.sum(wide * wide, axis=1, keepdims=True)


def slab_kernel(block_ref, feat_ref, res_ref, coef_ref, slab_ref, part_ref, norm_ref):
    @pl.when(pl.program_id(0) == 0)
    def _():
        norm = column_norms(block_ref[...]) * LOG2E_SCALED
        norm_ref[...] = jnp.broadcast_to(norm, norm_ref.shape)
        part_ref[...] = jnp.zeros_like(part_ref)

    feat = feat_ref[...]
    norms = column_norms(feat) * LOG2E_SCALED
    along = jnp.transpose(jnp.broadcast_to(norms, (CHUNK, 128)))[0:1, :]
    weighted = (res_ref[...] - RIDGE * coef_ref[...]).astype(BF16)
    slabs = []
    for s in range(STEPS):
        at = pl.ds(s * BLOCK, BLOCK)
        cross = dot_nt(block_ref[at, :], feat)
        power = (2.0 * LOG2E_SCALED) * cross - along - norm_ref[at, 0:1]
        slab = jnp.exp2(power).astype(BF16)
        slab_ref[at, :] = slab
        slabs.append(slab)
        part_ref[:, s * TARGETS : (s + 1) * TARGETS] += dot(slab, weighted)
    part_ref[:, STEPS * TARGETS :] += dot_nt(slabs[1], slabs[0])


def slab_parts(blocks, features, residual, coefficients):
    rows = features.shape[0]
    return pl.pallas_call(
        slab_kernel,
        grid=(rows // CHUNK,),
        out_shape=(
            jax.ShapeDtypeStruct((STEPS * BLOCK, rows), BF16),
            jax.ShapeDtypeStruct((BLOCK, STEPS * TARGETS + BLOCK), F32),
        ),
        in_specs=[
            pl.BlockSpec((STEPS * BLOCK, WIDTH), lambda i: (0, 0)),
            pl.BlockSpec((CHUNK, WIDTH), lambda i: (i, 0)),
            pl.BlockSpec((CHUNK, TARGETS), lambda i: (i, 0)),
            pl.BlockSpec((CHUNK, TARGETS), lambda i: (i, 0)),
        ],
        out_specs=(
            pl.BlockSpec((STEPS * BLOCK, CHUNK), lambda i: (0, i)),
            pl.BlockSpec((BLOCK, STEPS * TARGETS + BLOCK), lambda i: (0, 0)),
        ),
        scratch_shapes=[pltpu.VMEM((STEPS * BLOCK, 128), F32)],
        compiler_params=pltpu.CompilerParams(vmem_limit_bytes=28 << 20),
        name="slab_parts",
    )(blocks, features, residual, coefficients)


PANEL = 4
HALF_TILE = TILE // 2


def eliminate(a, begin, end):
    n = TILE
    row = lax.broadcasted_iota(jnp.int32, (n, n), 0)
    lane = lax.broadcasted_iota(jnp.int32, (n, n), 1)
    for first in range(begin, end, PANEL):
        columns = [
            jnp.broadcast_to(a[:, first + j : first + j + 1], (n, n)) for j in range(PANEL)
        ]
        for j in range(PANEL):
            k = first + j
            column = columns[j]
            inverse = 1.0 / column[k : k + 1, :]
            column = jnp.where(row == k, column - 1.0, column)
            a = jnp.where(lane == k, jnp.where(row == k, 1.0, 0.0), a)
            a = a - column * (a[k : k + 1, :] * inverse)
            for jj in range(j + 1, PANEL):
                other = columns[jj]
                columns[jj] = other - column * (other[k : k + 1, :] * inverse)
    return a


def split3(wide):
    high = wide.astype(BF16)
    rest = wide - high.astype(F32)
    middle = rest.astype(BF16)
    low = (rest - middle.astype(F32)).astype(BF16)
    return high, middle, low


def product(left, right):
    lh, lm, ll = left
    rh, rm, rl = right
    small = dot(lh, rl) + dot(lm, rm) + dot(ll, rh)
    return dot(lh, rh) + (dot(lh, rm) + dot(lm, rh) + small)


def solve_kernel(
    step_size,
    block_ref,
    part_ref,
    update_ref,
    low_ref,
    total,
    inv,
    thirds,
    between,
    swap_sem,
    *scratch,
):
    spot = place()
    core = spot[3]
    greet(spot)
    run = Sum(part_ref, total, *scratch[:4], scratch[4:], spot)
    run.start_a()

    def block(s):
        return block_ref[pl.ds(pl.multiple_of(s * BLOCK, BLOCK), BLOCK), :]

    def kernel(left, right):
        a = column_norms(left) * LOG2E_SCALED
        b = column_norms(right) * LOG2E_SCALED
        along = jnp.transpose(jnp.broadcast_to(b, (BLOCK, TILE)))[0:1, :]
        return jnp.exp2((2.0 * LOG2E_SCALED) * dot_nt(left, right) - along - a)

    own = block(core)
    row = lax.broadcasted_iota(jnp.int32, (BLOCK, BLOCK), 0)
    lane = lax.broadcasted_iota(jnp.int32, (BLOCK, BLOCK), 1)
    inv[core] = kernel(own, own) + jnp.where(row == lane, RIDGE, 0.0)
    between[...] = kernel(block(1), block(0)).astype(BF16)

    stages = {0: run.a_to_b, 3: run.b_to_c, 5: run.c_to_e, 7: run.e_to_f}

    def hook(k, half):
        for at, stage in stages.items():
            if at % 2 == half:
                pl.when(k == at // 2)(stage)

    def step(k, carry):
        at = pl.ds(pl.multiple_of(k * TILE, TILE), TILE)
        inv[core, at, at] = eliminate(inv[core, at, at], 0, HALF_TILE)
        hook(k, 0)
        tile = eliminate(inv[core, at, at], HALF_TILE, TILE)
        inside = lax.div(lax.broadcasted_iota(jnp.int32, (TILE, BLOCK), 1), TILE) == k
        lead = dot(tile, inv[core, at, :], HI)
        lead = jnp.where(inside, jnp.concatenate([tile] * (BLOCK // TILE), axis=1), lead)
        column = inv[core, :, at]
        inv[core, :, at] = jnp.zeros_like(column)
        inv[core] -= dot(column, lead, HI)
        inv[core, at, :] = lead
        hook(k, 1)
        return carry

    lax.fori_loop(0, BLOCK // TILE, step, 0)

    def swap(side):
        return remote(inv.at[core], inv.at[side], swap_sem.at[0], swap_sem.at[1], run.mate)

    swap(core).start()
    swap(1 - core).wait_recv()
    for s in range(STEPS):
        for i, third in enumerate(split3(inv[s])):
            thirds[s, i] = third
    run.finish()

    sums = total[...].reshape(BLOCK, total.shape[3])
    both = [(thirds[s, 0], thirds[s, 1], thirds[s, 2]) for s in range(STEPS)]
    first = product(both[0], split3(sums[:, :TARGETS])) * step_size
    first_low = first.astype(BF16)
    shift = sum(dot(third, first_low) for third in split3(sums[:, STEPS * TARGETS :]))
    past = sum(dot(between[...], third) for third in split3(first))
    gradient = sums[:, TARGETS : STEPS * TARGETS] - shift - RIDGE * past
    second = product(both[1], split3(gradient)) * step_size
    update_ref[0:BLOCK] = first
    update_ref[BLOCK:] = second
    low_ref[:, 0:BLOCK] = jnp.transpose(first).astype(BF16)
    low_ref[:, BLOCK:] = jnp.transpose(second).astype(BF16)
    swap(core).wait_send()


def solve(step_size, blocks, parts):
    height, lanes = parts.shape
    rows = height // (2 * NQ)
    shape = (2, NQ, rows, lanes)
    return pl.pallas_call(
        functools.partial(solve_kernel, step_size),
        out_shape=(
            jax.ShapeDtypeStruct((STEPS * BLOCK, TARGETS), F32),
            jax.ShapeDtypeStruct((TARGETS, STEPS * BLOCK), BF16),
        ),
        in_specs=[vmem(), vmem()],
        out_specs=(vmem(), vmem()),
        scratch_shapes=[
            pltpu.VMEM(shape, F32),
            pltpu.VMEM((STEPS, BLOCK, BLOCK), F32),
            pltpu.VMEM((STEPS, 3, BLOCK, BLOCK), BF16),
            pltpu.VMEM((BLOCK, BLOCK), BF16),
            pltpu.SemaphoreType.DMA((2,)),
            *sum_scratch(rows, lanes, F32),
        ],
        compiler_params=pltpu.CompilerParams(
            collective_id=1, has_side_effects=True, vmem_limit_bytes=28 << 20
        ),
        name="solve",
    )(blocks, parts.reshape(shape))


ROWS_STEP = 1024


def final_kernel(
    owner_ref, tiles_ref, update_ref, low_ref, slab_ref, res_ref, coef_ref, res_out, coef_out
):
    step = pl.program_id(0)
    res_out[...] = res_ref[...] - jnp.transpose(dot(low_ref[...], slab_ref[...]))
    coef_out[...] = coef_ref[...]
    me = lax.axis_index("rows") * lax.axis_size("sub") + lax.axis_index("sub")
    tiles_here = ROWS_STEP // TILE
    for s in range(STEPS):
        for t in range(BLOCK // TILE):
            tile = tiles_ref[s, t]

            @pl.when((owner_ref[s] == me) & (lax.div(tile, tiles_here) == step))
            def _():
                at = pl.ds(pl.multiple_of(lax.rem(tile, tiles_here) * TILE, TILE), TILE)
                coef_out[at, :] += update_ref[pl.ds(s * BLOCK + t * TILE, TILE), :]


def final(owner, tiles, updates, low, slabs, residual, coefficients):
    rows = residual.shape[0]
    whole = lambda i: (0, 0)
    chunk = pl.BlockSpec((ROWS_STEP, TARGETS), lambda i: (i, 0))
    return pl.pallas_call(
        final_kernel,
        grid=(rows // ROWS_STEP,),
        out_shape=(
            jax.ShapeDtypeStruct(residual.shape, F32),
            jax.ShapeDtypeStruct(coefficients.shape, F32),
        ),
        in_specs=[
            smem(),
            smem(),
            pl.BlockSpec(updates.shape, whole),
            pl.BlockSpec(low.shape, whole),
            pl.BlockSpec((STEPS * BLOCK, ROWS_STEP), lambda i: (0, i)),
            chunk,
            chunk,
        ],
        out_specs=(chunk, chunk),
        compiler_params=pltpu.CompilerParams(vmem_limit_bytes=16 << 20),
        name="final",
    )(owner, tiles, updates, low, slabs, residual, coefficients)


def local(features, residual, coefficients, block_owner, block_tiles):
    devices = lax.axis_size("rows") * lax.axis_size("sub")
    step_size = 1.0 / math.sqrt(features.shape[0] * devices)
    blocks = fetch_blocks(block_owner, block_tiles, features)
    slabs, parts = slab_parts(blocks, features, residual, coefficients)
    updates, low = solve(step_size, blocks, parts)
    return final(block_owner, block_tiles, updates, low, slabs, residual, coefficients)


def solution(mesh):
    in_specs = (
        P(("rows", "sub"), None),
        P(("rows", "sub"), None),
        P(("rows", "sub"), None),
        P(),
        P(),
    )
    out_specs = (P(("rows", "sub"), None), P(("rows", "sub"), None))
    return jax.shard_map(local, mesh=mesh, in_specs=in_specs, out_specs=out_specs, check_vma=False)
```

```python
import functools
import math

import jax
import jax.numpy as jnp
from jax import lax
from jax.experimental import pallas as pl
from jax.experimental.pallas import tpu as pltpu
from jax.sharding import PartitionSpec as P

MESH = pl.DeviceIdType.MESH
HI = lax.Precision.HIGHEST
F32 = jnp.float32
BF16 = jnp.bfloat16

BLOCK = 512
TILE = 128
STEPS = 2
RIDGE = 0.5
WIDTH = 512
TARGETS = 128
NX, NY, NZ = 4, 4, 8
NQ = NX * NY
CHUNK = 1024
ROWS_DEV = 4096
VMEM_BYTES = 64 << 20


def vmem():
    return pl.BlockSpec(memory_space=pltpu.VMEM)


def smem():
    return pl.BlockSpec(memory_space=pltpu.SMEM)


def dot(a, b, precision=None):
    return jnp.dot(a, b, precision=precision, preferred_element_type=F32)


def dot_nt(a, b, precision=None):
    return lax.dot_general(
        a, b, (((1,), (1,)), ((), ())), precision=precision, preferred_element_type=F32
    )


def place():
    across, within = lax.axis_index("rows"), lax.axis_index("sub")
    core = lax.rem(across, 2)
    y = lax.rem(lax.div(across, 2), NY)
    z = lax.div(across, 2 * NY) * 2 + lax.rem(within, 2)
    x = lax.div(within, 2)
    return (x, y, z), core


def device(chip, core):
    x, y, z = chip
    return (lax.div(z, 2) * (2 * NY) + y * 2 + core, x * 2 + lax.rem(z, 2))


SIZES = (NX, NY, NZ)


def moved(chip, step):
    return tuple(
        lax.rem(c + (s + size) % size, size) if s % size else c
        for c, s, size in zip(chip, step, SIZES)
    )


def back(step):
    return tuple(-s for s in step)


def hops(step):
    return sum(min(s, size - s) for s, size in zip(step, SIZES))


class Columns:
    size = NX * NY
    steps = sorted(
        [(i, j, 0) for i in range(NX) for j in range(NY) if i or j], key=lambda s: -hops(s)
    )

    @staticmethod
    def number(chip):
        return chip[0] * NY + chip[1]


class Planes:
    size = NZ
    steps = sorted([(0, 0, k) for k in range(1, NZ)], key=lambda s: -hops(s))

    @staticmethod
    def number(chip):
        return chip[2]


def greet(chip, core):
    barrier = pltpu.get_barrier_semaphore()
    others = [(moved(chip, step), core) for step in Columns.steps + Planes.steps]
    others.append((chip, 1 - core))
    for there, side in others:
        pl.semaphore_signal(barrier, inc=1, device_id=device(there, side), device_id_type=MESH)


def await_greetings():
    pl.semaphore_wait(pltpu.get_barrier_semaphore(), len(Columns.steps) + len(Planes.steps) + 1)


def remote(source, target, sems, i, where):
    return pltpu.make_async_remote_copy(
        src_ref=source,
        dst_ref=target,
        send_sem=sems.at[0, i],
        recv_sem=sems.at[1, i],
        device_id=device(*where),
        device_id_type=MESH,
    )


class Flow:
    def __init__(self, chip, core, first, second, part_at, total_at, scratch):
        self.chip, self.core, self.first, self.second = chip, core, first, second
        self.part_at, self.total_at = part_at, total_at
        self.recv_a, self.half, self.recv_b, self.recv_c = scratch[:4]
        self.sem_a, self.sem_b, self.sem_c, self.sem_e, self.sem_f = scratch[4:]
        self.steps = first.steps + [(0, 0, 0)]
        self.last = len(first.steps)
        self.mate = (chip, 1 - core)
        self.chunk = first.number(chip)
        self.slot = second.number(chip)

    def ahead(self, i):
        there = moved(self.chip, self.steps[i])
        return (there, self.core), self.first.number(there)

    def behind(self, i):
        return self.first.number(moved(self.chip, back(self.steps[i])))

    def a_copy(self, i):
        part = self.part_at(1 - self.core, self.ahead(i)[1])
        return remote(part, self.recv_a.at[i], self.sem_a, i, self.mate)

    def b_copy(self, i):
        return remote(self.half.at[i], self.recv_b.at[i], self.sem_b, i, self.ahead(i)[0])

    def c_copy(self, i, slot):
        there = moved(self.chip, self.second.steps[i])
        mine, target = self.recv_c.at[self.slot], self.recv_c.at[slot]
        return remote(mine, target, self.sem_c, i, (there, self.core))

    def e_copy(self, i, chunk):
        mine, target = self.total_at(self.core, self.chunk), self.total_at(self.core, chunk)
        return remote(mine, target, self.sem_e, i, self.ahead(i)[0])

    def f_copy(self, i, side):
        chunk = self.behind(i)
        mine, target = self.total_at(self.core, chunk), self.total_at(side, chunk)
        return remote(mine, target, self.sem_f, i, self.mate)

    def start_a(self, i):
        self.a_copy(i).start()

    def a_to_b(self, i):
        self.a_copy(i).wait_recv()
        self.half[i] = self.part_at(self.core, self.ahead(i)[1])[...] + self.recv_a[i]
        if i < self.last:
            self.b_copy(i).start()

    def b_to_c(self):
        chunk = self.half[self.last]
        for i in reversed(range(self.last)):
            self.b_copy(i).wait_recv()
            chunk = chunk + self.recv_b[i]
        self.recv_c[self.slot] = chunk
        for i in range(len(self.second.steps)):
            self.c_copy(i, self.slot).start()

    def c_to_e(self):
        for i in range(len(self.second.steps)):
            source = moved(self.chip, back(self.second.steps[i]))
            self.c_copy(i, self.second.number(source)).wait_recv()
        chunk = self.recv_c[0]
        for i in range(1, self.second.size):
            chunk = chunk + self.recv_c[i]
        self.total_at(self.core, self.chunk)[...] = chunk
        for i in range(self.last):
            self.e_copy(i, self.chunk).start()
        self.f_copy(self.last, self.core).start()

    def e_to_f(self, i):
        self.e_copy(i, self.behind(i)).wait_recv()
        self.f_copy(i, self.core).start()

    def finish(self):
        for i in reversed(range(self.first.size)):
            self.f_copy(i, 1 - self.core).wait_recv()

    def drain(self):
        for i in range(self.first.size):
            self.a_copy(i).wait_send()
            self.f_copy(i, self.core).wait_send()
        for i in range(self.last):
            self.b_copy(i).wait_send()
            self.e_copy(i, self.chunk).wait_send()
        for i in range(len(self.second.steps)):
            self.c_copy(i, self.slot).wait_send()


def flow_scratch(first, second, shape, dtype):
    def pair(n):
        return pltpu.SemaphoreType.DMA((2, n))

    n1, n2 = len(first.steps), len(second.steps)
    return [
        pltpu.VMEM((first.size, *shape), dtype),
        pltpu.VMEM((first.size, *shape), dtype),
        pltpu.VMEM((n1, *shape), dtype),
        pltpu.VMEM((second.size, *shape), dtype),
        pair(first.size),
        pair(n1),
        pair(n2),
        pair(n1),
        pair(first.size),
    ]


FLOW_SCRATCH = 9


class Flows:
    def __init__(self, *flows):
        self.flows = flows

    def in_turn(self, count, call):
        most = max(count(flow) for flow in self.flows)
        for i in range(most):
            for flow in self.flows:
                if i < count(flow):
                    call(flow, i)

    def start_a(self):
        self.in_turn(lambda f: f.first.size, lambda f, i: f.start_a(i))

    def a_to_b(self):
        self.in_turn(lambda f: f.first.size, lambda f, i: f.a_to_b(i))

    def b_to_c(self):
        for flow in reversed(self.flows):
            flow.b_to_c()

    def c_to_e(self):
        for flow in self.flows:
            flow.c_to_e()

    def e_to_f(self):
        self.in_turn(lambda f: f.last, lambda f, i: f.e_to_f(f.last - 1 - i))

    def finish(self):
        for flow in self.flows:
            flow.finish()

    def drain(self):
        for flow in self.flows:
            flow.drain()


PANEL = 4
HALF_TILE = TILE // 2


def eliminate(a, begin, end):
    n = TILE
    row = lax.broadcasted_iota(jnp.int32, (n, n), 0)
    lane = lax.broadcasted_iota(jnp.int32, (n, n), 1)
    for first in range(begin, end, PANEL):
        columns = [
            jnp.broadcast_to(a[:, first + j : first + j + 1], (n, n)) for j in range(PANEL)
        ]
        for j in range(PANEL):
            k = first + j
            column = columns[j]
            inverse = 1.0 / column[k : k + 1, :]
            column = jnp.where(row == k, column - 1.0, column)
            a = jnp.where(lane == k, jnp.where(row == k, 1.0, 0.0), a)
            a = a - column * (a[k : k + 1, :] * inverse)
            for jj in range(j + 1, PANEL):
                other = columns[jj]
                columns[jj] = other - column * (other[k : k + 1, :] * inverse)
    return a


def split3(wide):
    high = wide.astype(BF16)
    rest = wide - high.astype(F32)
    middle = rest.astype(BF16)
    low = (rest - middle.astype(F32)).astype(BF16)
    return high, middle, low


def product(left, right):
    lh, lm, ll = left
    rh, rm, rl = right
    small = dot(lh, rl) + dot(lm, rm) + dot(ll, rh)
    return dot(lh, rh) + (dot(lh, rm) + dot(lm, rh) + small)


LOG2E_SCALED = math.log2(math.e) / WIDTH


def column_norms(rows):
    wide = rows.astype(F32)
    return jnp.sum(wide * wide, axis=1, keepdims=True) * LOG2E_SCALED


def along_lanes(column):
    return jnp.transpose(jnp.broadcast_to(column, (column.shape[0], 128)))[0:1, :]


def kernel_of(cross, column, lane_row):
    return jnp.exp2((2.0 * LOG2E_SCALED) * cross - lane_row - column)


FETCH_ROWS = BLOCK // NQ
FETCH_CUT = 384
FETCH_FLOWS = ((Columns, Planes, (FETCH_ROWS, FETCH_CUT)), (Planes, Columns, (2, FETCH_ROWS, WIDTH - FETCH_CUT)))
HALF = BLOCK // 2
SUM_FLOWS = ((Columns, Planes, (HALF // NQ, BLOCK)), (Planes, Columns, (HALF // NZ, STEPS * TARGETS)))
CHUNKS = ROWS_DEV // CHUNK
CHUNK_TILES = CHUNK // TILE


def update_kernel(
    step_size,
    owner_ref,
    tiles_ref,
    feat_hbm,
    res_hbm,
    coef_hbm,
    update_ref,
    low_ref,
    slab_hbm,
    feat_ref,
    res_ref,
    coef_ref,
    weighted_ref,
    along_ref,
    slab_ref,
    load_sem,
    slab_sem,
    masked,
    blocks,
    norm_ref,
    product_part,
    product_sum,
    grad_part,
    grad_sum,
    inv,
    thirds,
    between,
    swap_sem,
    *scratch,
):
    loads = [
        pltpu.make_async_copy(source, target, load_sem.at[i])
        for i, (source, target) in enumerate(
            [(feat_hbm, feat_ref), (res_hbm, res_ref), (coef_hbm, coef_ref)]
        )
    ]
    loads[0].start()
    chip, core = place()
    greet(chip, core)
    for load in loads[1:]:
        load.start()

    me = lax.axis_index("rows") * lax.axis_size("sub") + lax.axis_index("sub")
    loads[0].wait()
    per_tile = TILE // FETCH_ROWS

    def build(s):
        mine = jnp.full((FETCH_ROWS, WIDTH), (owner_ref[s] == me).astype(F32)).astype(BF16)
        for t in range(BLOCK // TILE):
            tile = feat_ref[tiles_ref[s, t]]
            for i in range(per_tile):
                at = slice(i * FETCH_ROWS, (i + 1) * FETCH_ROWS)
                masked[s, t * per_tile + i] = tile[at] * mine

    left, right = pl.ds(0, FETCH_CUT), pl.ds(FETCH_CUT, WIDTH - FETCH_CUT)

    def pair_of(ref):
        return (
            lambda side, chunk: ref.at[side, chunk, :, left],
            lambda side, chunk: ref.at[side, pl.ds(2 * chunk, 2), :, right],
        )

    def flows_of(kinds, parts, totals, scratch):
        flows = []
        for i, (first, second, _) in enumerate(kinds):
            mine = scratch[i * FLOW_SCRATCH : (i + 1) * FLOW_SCRATCH]
            flows.append(Flow(chip, core, first, second, parts[i], totals[i], mine))
        return Flows(*flows)

    fetch = flows_of(FETCH_FLOWS, pair_of(masked), pair_of(blocks), scratch)
    build(1 - core)
    await_greetings()
    fetch.start_a()
    build(core)
    fetch.a_to_b()

    def norms_of(i, carry):
        rows = feat_ref[pl.ds(i * CHUNK_TILES, CHUNK_TILES)].reshape(CHUNK, WIDTH)
        along_ref[i] = jnp.broadcast_to(along_lanes(column_norms(rows)), (8, CHUNK))
        return carry

    lax.fori_loop(0, CHUNKS, norms_of, 0)
    fetch.b_to_c()
    for load in loads[1:]:
        load.wait()
    weighted_ref[...] = (res_ref[...] - RIDGE * coef_ref[...]).astype(BF16)
    product_part[...] = jnp.zeros_like(product_part)
    grad_part[...] = jnp.zeros_like(grad_part)
    fetch.c_to_e()
    fetch.e_to_f()
    fetch.finish()

    for s in range(STEPS):
        norm = column_norms(blocks[s].reshape(BLOCK, WIDTH))
        norm_ref[s] = jnp.broadcast_to(norm, (BLOCK, 128))

    def slab_copy(i):
        return pltpu.make_async_copy(slab_ref.at[i], slab_hbm.at[i], slab_sem.at[i])

    def slab_step(i, carry):
        feat = feat_ref[pl.ds(i * CHUNK_TILES, CHUNK_TILES)].reshape(CHUNK, WIDTH)
        weighted = weighted_ref[pl.ds(pl.multiple_of(i * CHUNK, CHUNK), CHUNK), :]
        along = along_ref[i][0:1, :]
        slabs = []
        for s in range(STEPS):
            cross = dot_nt(blocks[s].reshape(BLOCK, WIDTH), feat)
            slab = kernel_of(cross, norm_ref[s][:, 0:1], along).astype(BF16)
            slab_ref[i, pl.ds(s * BLOCK, BLOCK), :] = slab
            slabs.append(slab)
            term = dot(slab, weighted).reshape(2, NZ, HALF // NZ, TARGETS)
            grad_part[:, :, :, pl.ds(s * TARGETS, TARGETS)] += term
        term = dot_nt(slabs[1], slabs[0])
        product_part[...] += term.reshape(product_part.shape)
        slab_copy(i).start()
        return carry

    lax.fori_loop(0, CHUNKS, slab_step, 0)

    sums = flows_of(
        SUM_FLOWS,
        (
            lambda side, chunk: product_part.at[side, chunk],
            lambda side, chunk: grad_part.at[side, chunk],
        ),
        (
            lambda side, chunk: product_sum.at[side, chunk],
            lambda side, chunk: grad_sum.at[side, chunk],
        ),
        scratch[2 * FLOW_SCRATCH :],
    )
    sums.start_a()

    def block_kernel(a, b):
        cross = dot_nt(blocks[a].reshape(BLOCK, WIDTH), blocks[b].reshape(BLOCK, WIDTH))
        return kernel_of(cross, norm_ref[a][:, 0:1], along_lanes(norm_ref[b][:, 0:1]))

    row = lax.broadcasted_iota(jnp.int32, (BLOCK, BLOCK), 0)
    lane = lax.broadcasted_iota(jnp.int32, (BLOCK, BLOCK), 1)
    inv[core] = block_kernel(core, core) + jnp.where(row == lane, RIDGE, 0.0)
    sums.a_to_b()
    between[...] = block_kernel(1, 0).astype(BF16)

    stages = {2: sums.b_to_c, 4: sums.c_to_e, 6: sums.e_to_f}

    def hook(k, half):
        for at, stage in stages.items():
            if at % 2 == half:
                pl.when(k == at // 2)(stage)

    def step(k, carry):
        at = pl.ds(pl.multiple_of(k * TILE, TILE), TILE)
        inv[core, at, at] = eliminate(inv[core, at, at], 0, HALF_TILE)
        hook(k, 0)
        tile = eliminate(inv[core, at, at], HALF_TILE, TILE)
        inside = lax.div(lax.broadcasted_iota(jnp.int32, (TILE, BLOCK), 1), TILE) == k
        lead = dot(tile, inv[core, at, :], HI)
        lead = jnp.where(inside, jnp.concatenate([tile] * (BLOCK // TILE), axis=1), lead)
        column = inv[core, :, at]
        inv[core, :, at] = jnp.zeros_like(column)
        inv[core] -= dot(column, lead, HI)
        inv[core, at, :] = lead
        hook(k, 1)
        return carry

    lax.fori_loop(0, BLOCK // TILE, step, 0)

    def swap(side):
        return remote(inv.at[core], inv.at[side], swap_sem, 0, (chip, 1 - core))

    swap(core).start()
    swap(1 - core).wait_recv()
    for s in range(STEPS):
        for i, third in enumerate(split3(inv[s])):
            thirds[s, i] = third
    sums.finish()

    both = [(thirds[s, 0], thirds[s, 1], thirds[s, 2]) for s in range(STEPS)]
    grads = grad_sum[...].reshape(BLOCK, STEPS * TARGETS)
    first = product(both[0], split3(grads[:, :TARGETS])) * step_size
    first_low = first.astype(BF16)
    slab_product = product_sum[...].reshape(BLOCK, BLOCK)
    shift = sum(dot(third, first_low) for third in split3(slab_product))
    past = sum(dot(between[...], third) for third in split3(first))
    gradient = grads[:, TARGETS:] - shift - RIDGE * past
    second = product(both[1], split3(gradient)) * step_size
    update_ref[0:BLOCK] = first
    update_ref[BLOCK:] = second
    low_ref[:, 0:BLOCK] = jnp.transpose(first).astype(BF16)
    low_ref[:, BLOCK:] = jnp.transpose(second).astype(BF16)

    swap(core).wait_send()
    fetch.drain()
    sums.drain()
    for i in range(CHUNKS):
        slab_copy(i).wait()


def updates_of(step_size, block_owner, block_tiles, features, residual, coefficients):
    anywhere = pl.BlockSpec(memory_space=pl.ANY)
    tiled = features.reshape(-1, TILE, WIDTH)
    slab_shape = (CHUNKS, STEPS * BLOCK, CHUNK)
    fetch_shape = (STEPS, NQ, FETCH_ROWS, WIDTH)
    product_shape = (2, NQ, HALF // NQ, BLOCK)
    grad_shape = (2, NZ, HALF // NZ, STEPS * TARGETS)
    flows = []
    for first, second, shape in FETCH_FLOWS:
        flows += flow_scratch(first, second, shape, BF16)
    for first, second, shape in SUM_FLOWS:
        flows += flow_scratch(first, second, shape, F32)
    return pl.pallas_call(
        functools.partial(update_kernel, step_size),
        out_shape=(
            jax.ShapeDtypeStruct((STEPS * BLOCK, TARGETS), F32),
            jax.ShapeDtypeStruct((TARGETS, STEPS * BLOCK), BF16),
            jax.ShapeDtypeStruct(slab_shape, BF16),
        ),
        in_specs=[smem(), smem(), anywhere, anywhere, anywhere],
        out_specs=(vmem(), vmem(), anywhere),
        scratch_shapes=[
            pltpu.VMEM(tiled.shape, BF16),
            pltpu.VMEM(residual.shape, F32),
            pltpu.VMEM(coefficients.shape, F32),
            pltpu.VMEM(residual.shape, BF16),
            pltpu.VMEM((CHUNKS, 8, CHUNK), F32),
            pltpu.VMEM(slab_shape, BF16),
            pltpu.SemaphoreType.DMA((3,)),
            pltpu.SemaphoreType.DMA((CHUNKS,)),
            pltpu.VMEM(fetch_shape, BF16),
            pltpu.VMEM(fetch_shape, BF16),
            pltpu.VMEM((STEPS, BLOCK, 128), F32),
            pltpu.VMEM(product_shape, F32),
            pltpu.VMEM(product_shape, F32),
            pltpu.VMEM(grad_shape, F32),
            pltpu.VMEM(grad_shape, F32),
            pltpu.VMEM((STEPS, BLOCK, BLOCK), F32),
            pltpu.VMEM((STEPS, 3, BLOCK, BLOCK), BF16),
            pltpu.VMEM((BLOCK, BLOCK), BF16),
            pltpu.SemaphoreType.DMA((2, 1)),
            *flows,
        ],
        compiler_params=pltpu.CompilerParams(
            collective_id=0, has_side_effects=True, vmem_limit_bytes=VMEM_BYTES
        ),
        name="updates",
    )(block_owner, block_tiles, tiled, residual, coefficients)


ROWS_STEP = CHUNK


def final_kernel(
    owner_ref, tiles_ref, update_ref, low_ref, slab_ref, res_ref, coef_ref, res_out, coef_out
):
    step = pl.program_id(0)
    res_out[...] = res_ref[...] - jnp.transpose(dot(low_ref[...], slab_ref[0]))
    coef_out[...] = coef_ref[...]
    me = lax.axis_index("rows") * lax.axis_size("sub") + lax.axis_index("sub")
    tiles_here = ROWS_STEP // TILE
    for s in range(STEPS):
        for t in range(BLOCK // TILE):
            tile = tiles_ref[s, t]

            @pl.when((owner_ref[s] == me) & (lax.div(tile, tiles_here) == step))
            def _():
                at = pl.ds(pl.multiple_of(lax.rem(tile, tiles_here) * TILE, TILE), TILE)
                coef_out[at, :] += update_ref[pl.ds(s * BLOCK + t * TILE, TILE), :]


def final(owner, tiles, updates, low, slabs, residual, coefficients):
    rows = residual.shape[0]
    whole = lambda i: (0, 0)
    chunk = pl.BlockSpec((ROWS_STEP, TARGETS), lambda i: (i, 0))
    return pl.pallas_call(
        final_kernel,
        grid=(rows // ROWS_STEP,),
        out_shape=(
            jax.ShapeDtypeStruct(residual.shape, F32),
            jax.ShapeDtypeStruct(coefficients.shape, F32),
        ),
        in_specs=[
            smem(),
            smem(),
            pl.BlockSpec(updates.shape, whole),
            pl.BlockSpec(low.shape, whole),
            pl.BlockSpec((1, STEPS * BLOCK, ROWS_STEP), lambda i: (i, 0, 0)),
            chunk,
            chunk,
        ],
        out_specs=(chunk, chunk),
        compiler_params=pltpu.CompilerParams(vmem_limit_bytes=VMEM_BYTES),
        name="final",
    )(owner, tiles, updates, low, slabs, residual, coefficients)


def local(features, residual, coefficients, block_owner, block_tiles):
    devices = lax.axis_size("rows") * lax.axis_size("sub")
    step_size = 1.0 / math.sqrt(features.shape[0] * devices)
    updates, low, slabs = updates_of(
        step_size, block_owner, block_tiles, features, residual, coefficients
    )
    return final(block_owner, block_tiles, updates, low, slabs, residual, coefficients)


def solution(mesh):
    in_specs = (
        P(("rows", "sub"), None),
        P(("rows", "sub"), None),
        P(("rows", "sub"), None),
        P(),
        P(),
    )
    out_specs = (P(("rows", "sub"), None), P(("rows", "sub"), None))
    return jax.shard_map(local, mesh=mesh, in_specs=in_specs, out_specs=out_specs, check_vma=False)
```

```python
import functools
import math

import jax
import jax.numpy as jnp
from jax import lax
from jax.experimental import pallas as pl
from jax.experimental.pallas import tpu as pltpu
from jax.sharding import PartitionSpec as P

MESH = pl.DeviceIdType.MESH
HI = lax.Precision.HIGHEST
F32 = jnp.float32
BF16 = jnp.bfloat16

BLOCK = 512
TILE = 128
STEPS = 2
RIDGE = 0.5
WIDTH = 512
TARGETS = 128
NX, NY, NZ = 4, 4, 8
NQ = NX * NY
CHUNK = 1024
ROWS_DEV = 4096
VMEM_BYTES = 64 << 20


def vmem():
    return pl.BlockSpec(memory_space=pltpu.VMEM)


def smem():
    return pl.BlockSpec(memory_space=pltpu.SMEM)


def dot(a, b, precision=None):
    return jnp.dot(a, b, precision=precision, preferred_element_type=F32)


def dot_nt(a, b, precision=None):
    return lax.dot_general(
        a, b, (((1,), (1,)), ((), ())), precision=precision, preferred_element_type=F32
    )


def place():
    across, within = lax.axis_index("rows"), lax.axis_index("sub")
    core = lax.rem(across, 2)
    y = lax.rem(lax.div(across, 2), NY)
    z = lax.div(across, 2 * NY) * 2 + lax.rem(within, 2)
    x = lax.div(within, 2)
    return (x, y, z), core


def device(chip, core):
    x, y, z = chip
    return (lax.div(z, 2) * (2 * NY) + y * 2 + core, x * 2 + lax.rem(z, 2))


SIZES = (NX, NY, NZ)


def moved(chip, step):
    return tuple(
        lax.rem(c + (s + size) % size, size) if s % size else c
        for c, s, size in zip(chip, step, SIZES)
    )


def back(step):
    return tuple(-s for s in step)


def hops(step):
    return sum(min(s, size - s) for s, size in zip(step, SIZES))


class Columns:
    size = NX * NY
    steps = sorted(
        [(i, j, 0) for i in range(NX) for j in range(NY) if i or j], key=lambda s: -hops(s)
    )

    @staticmethod
    def number(chip):
        return chip[0] * NY + chip[1]


class Planes:
    size = NZ
    steps = sorted([(0, 0, k) for k in range(1, NZ)], key=lambda s: -hops(s))

    @staticmethod
    def number(chip):
        return chip[2]


def greet(chip, core):
    barrier = pltpu.get_barrier_semaphore()
    others = [(moved(chip, step), core) for step in Columns.steps + Planes.steps]
    others.append((chip, 1 - core))
    for there, side in others:
        pl.semaphore_signal(barrier, inc=1, device_id=device(there, side), device_id_type=MESH)


def await_greetings():
    pl.semaphore_wait(pltpu.get_barrier_semaphore(), len(Columns.steps) + len(Planes.steps) + 1)


def remote(source, target, sems, i, where):
    return pltpu.make_async_remote_copy(
        src_ref=source,
        dst_ref=target,
        send_sem=sems.at[0, i],
        recv_sem=sems.at[1, i],
        device_id=device(*where),
        device_id_type=MESH,
    )


class Flow:
    def __init__(self, chip, core, first, second, part_at, total_at, scratch):
        self.chip, self.core, self.first, self.second = chip, core, first, second
        self.part_at, self.total_at = part_at, total_at
        self.recv_a, self.half, self.recv_b, self.recv_c = scratch[:4]
        self.sem_a, self.sem_b, self.sem_c, self.sem_e, self.sem_f = scratch[4:]
        self.steps = first.steps + [(0, 0, 0)]
        self.last = len(first.steps)
        self.mate = (chip, 1 - core)
        self.chunk = first.number(chip)
        self.slot = second.number(chip)

    def ahead(self, i):
        there = moved(self.chip, self.steps[i])
        return (there, self.core), self.first.number(there)

    def behind(self, i):
        return self.first.number(moved(self.chip, back(self.steps[i])))

    def a_copy(self, i):
        part = self.part_at(1 - self.core, self.ahead(i)[1])
        return remote(part, self.recv_a.at[i], self.sem_a, i, self.mate)

    def b_copy(self, i):
        return remote(self.half.at[i], self.recv_b.at[i], self.sem_b, i, self.ahead(i)[0])

    def c_copy(self, i, slot):
        there = moved(self.chip, self.second.steps[i])
        mine, target = self.recv_c.at[self.slot], self.recv_c.at[slot]
        return remote(mine, target, self.sem_c, i, (there, self.core))

    def e_copy(self, i, chunk):
        mine, target = self.total_at(self.core, self.chunk), self.total_at(self.core, chunk)
        return remote(mine, target, self.sem_e, i, self.ahead(i)[0])

    def f_copy(self, i, side):
        chunk = self.behind(i)
        mine, target = self.total_at(self.core, chunk), self.total_at(side, chunk)
        return remote(mine, target, self.sem_f, i, self.mate)

    def start_a(self, i):
        self.a_copy(i).start()

    def a_to_b(self, i):
        self.a_copy(i).wait_recv()
        self.half[i] = self.part_at(self.core, self.ahead(i)[1])[...] + self.recv_a[i]
        if i < self.last:
            self.b_copy(i).start()

    def b_to_c(self):
        chunk = self.half[self.last]
        for i in reversed(range(self.last)):
            self.b_copy(i).wait_recv()
            chunk = chunk + self.recv_b[i]
        self.recv_c[self.slot] = chunk
        for i in range(len(self.second.steps)):
            self.c_copy(i, self.slot).start()

    def c_to_e(self):
        for i in range(len(self.second.steps)):
            source = moved(self.chip, back(self.second.steps[i]))
            self.c_copy(i, self.second.number(source)).wait_recv()
        chunk = self.recv_c[0]
        for i in range(1, self.second.size):
            chunk = chunk + self.recv_c[i]
        self.total_at(self.core, self.chunk)[...] = chunk
        for i in range(self.last):
            self.e_copy(i, self.chunk).start()
        self.f_copy(self.last, self.core).start()

    def e_to_f(self, i):
        self.e_copy(i, self.behind(i)).wait_recv()
        self.f_copy(i, self.core).start()

    def finish(self):
        for i in reversed(range(self.first.size)):
            self.f_copy(i, 1 - self.core).wait_recv()

    def drain(self):
        for i in range(self.first.size):
            self.a_copy(i).wait_send()
            self.f_copy(i, self.core).wait_send()
        for i in range(self.last):
            self.b_copy(i).wait_send()
            self.e_copy(i, self.chunk).wait_send()
        for i in range(len(self.second.steps)):
            self.c_copy(i, self.slot).wait_send()


def flow_scratch(first, second, shape, dtype):
    def pair(n):
        return pltpu.SemaphoreType.DMA((2, n))

    n1, n2 = len(first.steps), len(second.steps)
    return [
        pltpu.VMEM((first.size, *shape), dtype),
        pltpu.VMEM((first.size, *shape), dtype),
        pltpu.VMEM((n1, *shape), dtype),
        pltpu.VMEM((second.size, *shape), dtype),
        pair(first.size),
        pair(n1),
        pair(n2),
        pair(n1),
        pair(first.size),
    ]


FLOW_SCRATCH = 9


class Flows:
    def __init__(self, *flows):
        self.flows = flows

    def in_turn(self, count, call):
        most = max(count(flow) for flow in self.flows)
        for i in range(most):
            for flow in self.flows:
                if i < count(flow):
                    call(flow, i)

    def start_a(self):
        self.in_turn(lambda f: f.first.size, lambda f, i: f.start_a(i))

    def a_to_b(self):
        self.in_turn(lambda f: f.first.size, lambda f, i: f.a_to_b(i))

    def b_to_c(self):
        for flow in reversed(self.flows):
            flow.b_to_c()

    def c_to_e(self):
        for flow in self.flows:
            flow.c_to_e()

    def e_to_f(self):
        self.in_turn(lambda f: f.last, lambda f, i: f.e_to_f(f.last - 1 - i))

    def finish(self):
        for flow in self.flows:
            flow.finish()

    def drain(self):
        for flow in self.flows:
            flow.drain()


PANEL = 16
PANELS = TILE // PANEL


def eliminate(a, panel):
    n, first = TILE, panel * PANEL
    mine = slice(first, first + PANEL)
    row = lax.broadcasted_iota(jnp.int32, (PANEL, n), 0)
    lane = lax.broadcasted_iota(jnp.int32, (PANEL, n), 1)
    lane_all = lax.broadcasted_iota(jnp.int32, (n, n), 1)
    columns = [jnp.broadcast_to(a[:, first + j : first + j + 1], (n, n)) for j in range(PANEL)]
    square = [column[mine] for column in columns]
    rows = jnp.where(
        (lane >= first) & (lane < first + PANEL),
        jnp.where(lane - first == row, 1.0, 0.0),
        a[mine],
    )
    for k in range(PANEL):
        inverse = 1.0 / square[k][k : k + 1]
        column = jnp.where(row == k, square[k] - 1.0, square[k])
        for j in range(k + 1, PANEL):
            square[j] = square[j] - column * (square[j][k : k + 1] * inverse)
        rows = rows - column * (rows[k : k + 1] * inverse)
    change = columns[0] * rows[0:1]
    for j in range(1, PANEL):
        change = change + columns[j] * rows[j : j + 1]
    a = jnp.where((lane_all >= first) & (lane_all < first + PANEL), 0.0, a) - change
    pieces = [a[:first], rows, a[first + PANEL :]]
    return jnp.concatenate([piece for piece in pieces if piece.shape[0]], axis=0)


def split3(wide):
    high = wide.astype(BF16)
    rest = wide - high.astype(F32)
    middle = rest.astype(BF16)
    low = (rest - middle.astype(F32)).astype(BF16)
    return high, middle, low


def product(left, right):
    lh, lm, ll = left
    rh, rm, rl = right
    small = dot(lh, rl) + dot(lm, rm) + dot(ll, rh)
    return dot(lh, rh) + (dot(lh, rm) + dot(lm, rh) + small)


LOG2E_SCALED = math.log2(math.e) / WIDTH


def column_norms(rows):
    wide = rows.astype(F32)
    return jnp.sum(wide * wide, axis=1, keepdims=True) * LOG2E_SCALED


def along_lanes(column):
    return jnp.transpose(jnp.broadcast_to(column, (column.shape[0], 128)))[0:1, :]


def kernel_of(cross, column, lane_row):
    return jnp.exp2((2.0 * LOG2E_SCALED) * cross - lane_row - column)


FETCH_ROWS = BLOCK // NQ
FETCH_CUT = 384
FETCH_FLOWS = ((Columns, Planes, (FETCH_ROWS, FETCH_CUT)), (Planes, Columns, (2, FETCH_ROWS, WIDTH - FETCH_CUT)))
HALF = BLOCK // 2
SUM_FLOWS = ((Columns, Planes, (HALF // NQ, BLOCK)), (Planes, Columns, (HALF // NZ, STEPS * TARGETS)))
CHUNKS = ROWS_DEV // CHUNK
CHUNK_TILES = CHUNK // TILE


def update_kernel(
    step_size,
    owner_ref,
    tiles_ref,
    feat_hbm,
    res_hbm,
    coef_hbm,
    update_ref,
    low_ref,
    slab_hbm,
    feat_ref,
    res_ref,
    coef_ref,
    weighted_ref,
    along_ref,
    slab_ref,
    load_sem,
    slab_sem,
    masked,
    blocks,
    norm_ref,
    product_part,
    product_sum,
    grad_part,
    grad_sum,
    inv,
    thirds,
    between,
    first_tile,
    swap_sem,
    *scratch,
):
    loads = [
        pltpu.make_async_copy(source, target, load_sem.at[i])
        for i, (source, target) in enumerate(
            [(feat_hbm, feat_ref), (res_hbm, res_ref), (coef_hbm, coef_ref)]
        )
    ]
    loads[0].start()
    chip, core = place()
    greet(chip, core)
    for load in loads[1:]:
        load.start()

    me = lax.axis_index("rows") * lax.axis_size("sub") + lax.axis_index("sub")
    loads[0].wait()
    per_tile = TILE // FETCH_ROWS

    def build(s):
        mine = jnp.full((FETCH_ROWS, WIDTH), (owner_ref[s] == me).astype(F32)).astype(BF16)
        for t in range(BLOCK // TILE):
            tile = feat_ref[tiles_ref[s, t]]
            for i in range(per_tile):
                at = slice(i * FETCH_ROWS, (i + 1) * FETCH_ROWS)
                masked[s, t * per_tile + i] = tile[at] * mine

    left, right = pl.ds(0, FETCH_CUT), pl.ds(FETCH_CUT, WIDTH - FETCH_CUT)

    def pair_of(ref):
        return (
            lambda side, chunk: ref.at[side, chunk, :, left],
            lambda side, chunk: ref.at[side, pl.ds(2 * chunk, 2), :, right],
        )

    def flows_of(kinds, parts, totals, scratch):
        flows = []
        for i, (first, second, _) in enumerate(kinds):
            mine = scratch[i * FLOW_SCRATCH : (i + 1) * FLOW_SCRATCH]
            flows.append(Flow(chip, core, first, second, parts[i], totals[i], mine))
        return Flows(*flows)

    fetch = flows_of(FETCH_FLOWS, pair_of(masked), pair_of(blocks), scratch)
    build(1 - core)
    await_greetings()
    fetch.start_a()
    build(core)
    fetch.a_to_b()

    def norms_of(i, carry):
        rows = feat_ref[pl.ds(i * CHUNK_TILES, CHUNK_TILES)].reshape(CHUNK, WIDTH)
        along_ref[i] = jnp.broadcast_to(along_lanes(column_norms(rows)), (8, CHUNK))
        return carry

    lax.fori_loop(0, CHUNKS, norms_of, 0)
    fetch.b_to_c()
    for load in loads[1:]:
        load.wait()
    weighted_ref[...] = (res_ref[...] - RIDGE * coef_ref[...]).astype(BF16)
    fetch.c_to_e()
    fetch.e_to_f()
    fetch.finish()

    for s in range(STEPS):
        norm = column_norms(blocks[s].reshape(BLOCK, WIDTH))
        norm_ref[s] = jnp.broadcast_to(norm, (BLOCK, 128))

    def slab_copy(i):
        at = pl.ds(i * CHUNK, CHUNK)
        return pltpu.make_async_copy(slab_ref.at[:, at], slab_hbm.at[:, at], slab_sem.at[i])

    def block_rows(s):
        return blocks[s].reshape(BLOCK, WIDTH)

    def cross_of(unit):
        i, s = unit // STEPS, unit % STEPS
        feat = feat_ref[i * CHUNK_TILES : (i + 1) * CHUNK_TILES].reshape(CHUNK, WIDTH)
        return dot_nt(block_rows(s), feat)

    row = lax.broadcasted_iota(jnp.int32, (BLOCK, BLOCK), 0)
    lane = lax.broadcasted_iota(jnp.int32, (BLOCK, BLOCK), 1)
    ridge = jnp.where(row == lane, RIDGE, 0.0)
    corner = blocks[core, 0 : TILE // FETCH_ROWS].reshape(TILE, WIDTH)
    corner_norm = norm_ref[core, 0:TILE, 0:1]
    tile = kernel_of(dot_nt(corner, corner), corner_norm, along_lanes(corner_norm))
    tile = tile + ridge[:TILE, :TILE]
    units = CHUNKS * STEPS
    cross = cross_of(0)
    for unit in range(units):
        i, s = unit // STEPS, unit % STEPS
        later = cross_of(unit + 1) if unit + 1 < units else None
        slab = kernel_of(cross, norm_ref[s][:, 0:1], along_ref[i][0:1, :]).astype(BF16)
        slab_ref[s * BLOCK : (s + 1) * BLOCK, i * CHUNK : (i + 1) * CHUNK] = slab
        if unit < PANELS:
            tile = eliminate(tile, unit)
        if s == STEPS - 1:
            slab_copy(i).start()
        cross = later
    first_tile[...] = tile

    def share(half):
        at = [pl.ds(pl.multiple_of(s * BLOCK + half * HALF, HALF), HALF) for s in range(STEPS)]
        for s in range(STEPS):
            term = dot(slab_ref[at[s], :], weighted_ref[...]).reshape(NZ, HALF // NZ, TARGETS)
            grad_part[half, :, :, s * TARGETS : (s + 1) * TARGETS] = term
        term = dot_nt(slab_ref[at[1], :], slab_ref[0:BLOCK, :])
        product_part[half] = term.reshape(product_part.shape[1:])

    sums = flows_of(
        SUM_FLOWS,
        (
            lambda side, chunk: product_part.at[side, chunk],
            lambda side, chunk: grad_part.at[side, chunk],
        ),
        (
            lambda side, chunk: product_sum.at[side, chunk],
            lambda side, chunk: grad_sum.at[side, chunk],
        ),
        scratch[2 * FLOW_SCRATCH :],
    )
    share(1 - core)
    sums.start_a()
    share(core)
    sums.a_to_b()

    def block_kernel(a, b):
        cross = dot_nt(block_rows(a), block_rows(b))
        return kernel_of(cross, norm_ref[a][:, 0:1], along_lanes(norm_ref[b][:, 0:1]))

    inv[core] = block_kernel(core, core) + ridge
    between[...] = block_kernel(1, 0).astype(BF16)

    def spread(k, tile):
        at = pl.ds(pl.multiple_of(k * TILE, TILE), TILE)
        inside = lax.div(lax.broadcasted_iota(jnp.int32, (TILE, BLOCK), 1), TILE) == k
        lead = dot(tile, inv[core, at, :], HI)
        lead = jnp.where(inside, jnp.concatenate([tile] * (BLOCK // TILE), axis=1), lead)
        column = inv[core, :, at]
        inv[core, :, at] = jnp.zeros_like(column)
        inv[core] -= dot(column, lead, HI)
        inv[core, at, :] = lead

    stages = {(1, 2): sums.b_to_c, (2, 2): sums.c_to_e, (3, 2): sums.e_to_f}

    def step(k, carry):
        at = pl.ds(pl.multiple_of(k * TILE, TILE), TILE)
        for part in range(4):
            tile = inv[core, at, at]
            for panel in range(part * PANELS // 4, (part + 1) * PANELS // 4):
                tile = eliminate(tile, panel)
            inv[core, at, at] = tile
            for (at_k, at_part), stage in stages.items():
                if at_part == part:
                    pl.when(k == at_k)(stage)
        spread(k, inv[core, at, at])
        return carry

    spread(0, first_tile[...])
    lax.fori_loop(1, BLOCK // TILE, step, 0)

    def swap(side):
        return remote(inv.at[core], inv.at[side], swap_sem, 0, (chip, 1 - core))

    swap(core).start()
    swap(1 - core).wait_recv()
    for s in range(STEPS):
        for i, third in enumerate(split3(inv[s])):
            thirds[s, i] = third
    sums.finish()

    both = [(thirds[s, 0], thirds[s, 1], thirds[s, 2]) for s in range(STEPS)]
    grads = grad_sum[...].reshape(BLOCK, STEPS * TARGETS)
    first = product(both[0], split3(grads[:, :TARGETS])) * step_size
    first_low = first.astype(BF16)
    slab_product = product_sum[...].reshape(BLOCK, BLOCK)
    shift = sum(dot(third, first_low) for third in split3(slab_product))
    past = sum(dot(between[...], third) for third in split3(first))
    gradient = grads[:, TARGETS:] - shift - RIDGE * past
    second = product(both[1], split3(gradient)) * step_size
    update_ref[0:BLOCK] = first
    update_ref[BLOCK:] = second
    low_ref[:, 0:BLOCK] = jnp.transpose(first).astype(BF16)
    low_ref[:, BLOCK:] = jnp.transpose(second).astype(BF16)

    swap(core).wait_send()
    fetch.drain()
    sums.drain()
    for i in range(CHUNKS):
        slab_copy(i).wait()


def updates_of(step_size, block_owner, block_tiles, features, residual, coefficients):
    anywhere = pl.BlockSpec(memory_space=pl.ANY)
    hbm = pl.BlockSpec(memory_space=pltpu.HBM)
    tiled = features.reshape(-1, TILE, WIDTH)
    slab_shape = (STEPS * BLOCK, ROWS_DEV)
    fetch_shape = (STEPS, NQ, FETCH_ROWS, WIDTH)
    product_shape = (2, NQ, HALF // NQ, BLOCK)
    grad_shape = (2, NZ, HALF // NZ, STEPS * TARGETS)
    flows = []
    for first, second, shape in FETCH_FLOWS:
        flows += flow_scratch(first, second, shape, BF16)
    for first, second, shape in SUM_FLOWS:
        flows += flow_scratch(first, second, shape, F32)
    return pl.pallas_call(
        functools.partial(update_kernel, step_size),
        out_shape=(
            jax.ShapeDtypeStruct((STEPS * BLOCK, TARGETS), F32),
            jax.ShapeDtypeStruct((TARGETS, STEPS * BLOCK), BF16),
            pltpu.VMEM(slab_shape, BF16),
        ),
        in_specs=[smem(), smem(), hbm, hbm, hbm],
        out_specs=(vmem(), vmem(), anywhere),
        scratch_shapes=[
            pltpu.VMEM(tiled.shape, BF16),
            pltpu.VMEM(residual.shape, F32),
            pltpu.VMEM(coefficients.shape, F32),
            pltpu.VMEM(residual.shape, BF16),
            pltpu.VMEM((CHUNKS, 8, CHUNK), F32),
            pltpu.VMEM(slab_shape, BF16),
            pltpu.SemaphoreType.DMA((3,)),
            pltpu.SemaphoreType.DMA((CHUNKS,)),
            pltpu.VMEM(fetch_shape, BF16),
            pltpu.VMEM(fetch_shape, BF16),
            pltpu.VMEM((STEPS, BLOCK, 128), F32),
            pltpu.VMEM(product_shape, F32),
            pltpu.VMEM(product_shape, F32),
            pltpu.VMEM(grad_shape, F32),
            pltpu.VMEM(grad_shape, F32),
            pltpu.VMEM((STEPS, BLOCK, BLOCK), F32),
            pltpu.VMEM((STEPS, 3, BLOCK, BLOCK), BF16),
            pltpu.VMEM((BLOCK, BLOCK), BF16),
            pltpu.VMEM((TILE, TILE), F32),
            pltpu.SemaphoreType.DMA((2, 1)),
            *flows,
        ],
        compiler_params=pltpu.CompilerParams(
            collective_id=0, has_side_effects=True, vmem_limit_bytes=44 << 20
        ),
        name="updates",
    )(block_owner, block_tiles, tiled, residual, coefficients)


ROWS_STEP = CHUNK


def final_kernel(
    owner_ref, tiles_ref, update_ref, low_ref, slab_ref, res_ref, coef_ref, res_out, coef_out
):
    step = pl.program_id(0)
    res_out[...] = res_ref[...] - jnp.transpose(dot(low_ref[...], slab_ref[...]))
    coef_out[...] = coef_ref[...]
    me = lax.axis_index("rows") * lax.axis_size("sub") + lax.axis_index("sub")
    tiles_here = ROWS_STEP // TILE
    for s in range(STEPS):
        for t in range(BLOCK // TILE):
            tile = tiles_ref[s, t]

            @pl.when((owner_ref[s] == me) & (lax.div(tile, tiles_here) == step))
            def _():
                at = pl.ds(pl.multiple_of(lax.rem(tile, tiles_here) * TILE, TILE), TILE)
                coef_out[at, :] += update_ref[pl.ds(s * BLOCK + t * TILE, TILE), :]


def final(owner, tiles, updates, low, slabs, residual, coefficients):
    rows = residual.shape[0]
    whole = lambda i: (0, 0)
    chunk = pl.BlockSpec((ROWS_STEP, TARGETS), lambda i: (i, 0))
    return pl.pallas_call(
        final_kernel,
        grid=(rows // ROWS_STEP,),
        out_shape=(
            jax.ShapeDtypeStruct(residual.shape, F32),
            jax.ShapeDtypeStruct(coefficients.shape, F32),
        ),
        in_specs=[
            smem(),
            smem(),
            pl.BlockSpec(updates.shape, whole),
            pl.BlockSpec(low.shape, whole),
            pl.BlockSpec((STEPS * BLOCK, ROWS_STEP), lambda i: (0, i)),
            chunk,
            chunk,
        ],
        out_specs=(chunk, chunk),
        compiler_params=pltpu.CompilerParams(vmem_limit_bytes=24 << 20),
        name="final",
    )(owner, tiles, updates, low, slabs, residual, coefficients)


def local(features, residual, coefficients, block_owner, block_tiles):
    devices = lax.axis_size("rows") * lax.axis_size("sub")
    step_size = 1.0 / math.sqrt(features.shape[0] * devices)
    updates, low, slabs = updates_of(
        step_size, block_owner, block_tiles, features, residual, coefficients
    )
    return final(block_owner, block_tiles, updates, low, slabs, residual, coefficients)


def solution(mesh):
    in_specs = (
        P(("rows", "sub"), None),
        P(("rows", "sub"), None),
        P(("rows", "sub"), None),
        P(),
        P(),
    )
    out_specs = (P(("rows", "sub"), None), P(("rows", "sub"), None))
    return jax.shard_map(local, mesh=mesh, in_specs=in_specs, out_specs=out_specs, check_vma=False)
```

```python
import functools
import math

import jax
import jax.numpy as jnp
from jax import lax
from jax.experimental import pallas as pl
from jax.experimental.pallas import tpu as pltpu
from jax.sharding import PartitionSpec as P

MESH = pl.DeviceIdType.MESH
HI = lax.Precision.HIGHEST
F32 = jnp.float32
BF16 = jnp.bfloat16

BLOCK = 512
TILE = 128
STEPS = 2
RIDGE = 0.5
WIDTH = 512
TARGETS = 128
NX, NY, NZ = 4, 4, 8
NQ = NX * NY
CHUNK = 1024
ROWS_DEV = 4096
VMEM_BYTES = 64 << 20


def vmem():
    return pl.BlockSpec(memory_space=pltpu.VMEM)


def smem():
    return pl.BlockSpec(memory_space=pltpu.SMEM)


def dot(a, b, precision=None):
    return jnp.dot(a, b, precision=precision, preferred_element_type=F32)


def dot_nt(a, b, precision=None):
    return lax.dot_general(
        a, b, (((1,), (1,)), ((), ())), precision=precision, preferred_element_type=F32
    )


def place():
    across, within = lax.axis_index("rows"), lax.axis_index("sub")
    core = lax.rem(across, 2)
    y = lax.rem(lax.div(across, 2), NY)
    z = lax.div(across, 2 * NY) * 2 + lax.rem(within, 2)
    x = lax.div(within, 2)
    return (x, y, z), core


def device(chip, core):
    x, y, z = chip
    return (lax.div(z, 2) * (2 * NY) + y * 2 + core, x * 2 + lax.rem(z, 2))


SIZES = (NX, NY, NZ)


def moved(chip, step):
    return tuple(
        lax.rem(c + (s + size) % size, size) if s % size else c
        for c, s, size in zip(chip, step, SIZES)
    )


def back(step):
    return tuple(-s for s in step)


def hops(step):
    return sum(min(s, size - s) for s, size in zip(step, SIZES))


class Columns:
    size = NX * NY
    steps = sorted(
        [(i, j, 0) for i in range(NX) for j in range(NY) if i or j], key=lambda s: -hops(s)
    )

    @staticmethod
    def number(chip):
        return chip[0] * NY + chip[1]


class Planes:
    size = NZ
    steps = sorted([(0, 0, k) for k in range(1, NZ)], key=lambda s: -hops(s))

    @staticmethod
    def number(chip):
        return chip[2]


def greet(chip, core):
    barrier = pltpu.get_barrier_semaphore()
    others = [(moved(chip, step), core) for step in Columns.steps + Planes.steps]
    others.append((chip, 1 - core))
    for there, side in others:
        pl.semaphore_signal(barrier, inc=1, device_id=device(there, side), device_id_type=MESH)


def await_greetings():
    pl.semaphore_wait(pltpu.get_barrier_semaphore(), len(Columns.steps) + len(Planes.steps) + 1)


def remote(source, target, sems, i, where):
    return pltpu.make_async_remote_copy(
        src_ref=source,
        dst_ref=target,
        send_sem=sems.at[0, i],
        recv_sem=sems.at[1, i],
        device_id=device(*where),
        device_id_type=MESH,
    )


class Flow:
    def __init__(self, chip, core, first, second, part_at, total_at, scratch):
        self.chip, self.core, self.first, self.second = chip, core, first, second
        self.part_at, self.total_at = part_at, total_at
        self.recv_a, self.half, self.recv_b, self.recv_c = scratch[:4]
        self.sem_a, self.sem_b, self.sem_c, self.sem_e, self.sem_f = scratch[4:]
        self.steps = first.steps + [(0, 0, 0)]
        self.last = len(first.steps)
        self.mate = (chip, 1 - core)
        self.chunk = first.number(chip)
        self.slot = second.number(chip)

    def ahead(self, i):
        there = moved(self.chip, self.steps[i])
        return (there, self.core), self.first.number(there)

    def behind(self, i):
        return self.first.number(moved(self.chip, back(self.steps[i])))

    def a_copy(self, i):
        part = self.part_at(1 - self.core, self.ahead(i)[1])
        return remote(part, self.recv_a.at[i], self.sem_a, i, self.mate)

    def b_copy(self, i):
        return remote(self.half.at[i], self.recv_b.at[i], self.sem_b, i, self.ahead(i)[0])

    def c_copy(self, i, slot):
        there = moved(self.chip, self.second.steps[i])
        mine, target = self.recv_c.at[self.slot], self.recv_c.at[slot]
        return remote(mine, target, self.sem_c, i, (there, self.core))

    def e_copy(self, i, chunk):
        mine, target = self.total_at(self.core, self.chunk), self.total_at(self.core, chunk)
        return remote(mine, target, self.sem_e, i, self.ahead(i)[0])

    def f_copy(self, i, side):
        chunk = self.behind(i)
        mine, target = self.total_at(self.core, chunk), self.total_at(side, chunk)
        return remote(mine, target, self.sem_f, i, self.mate)

    def start_a(self, i):
        self.a_copy(i).start()

    def a_to_b(self, i):
        self.a_copy(i).wait_recv()
        self.half[i] = self.part_at(self.core, self.ahead(i)[1])[...] + self.recv_a[i]
        if i < self.last:
            self.b_copy(i).start()

    def b_to_c(self):
        chunk = self.half[self.last]
        for i in reversed(range(self.last)):
            self.b_copy(i).wait_recv()
            chunk = chunk + self.recv_b[i]
        self.recv_c[self.slot] = chunk
        for i in range(len(self.second.steps)):
            self.c_copy(i, self.slot).start()

    def c_to_e(self):
        for i in range(len(self.second.steps)):
            source = moved(self.chip, back(self.second.steps[i]))
            self.c_copy(i, self.second.number(source)).wait_recv()
        chunk = self.recv_c[0]
        for i in range(1, self.second.size):
            chunk = chunk + self.recv_c[i]
        self.total_at(self.core, self.chunk)[...] = chunk
        for i in range(self.last):
            self.e_copy(i, self.chunk).start()
        self.f_copy(self.last, self.core).start()

    def e_to_f(self, i):
        self.e_copy(i, self.behind(i)).wait_recv()
        self.f_copy(i, self.core).start()

    def finish(self):
        for i in reversed(range(self.first.size)):
            self.f_copy(i, 1 - self.core).wait_recv()

    def drain(self):
        for i in range(self.first.size):
            self.a_copy(i).wait_send()
            self.f_copy(i, self.core).wait_send()
        for i in range(self.last):
            self.b_copy(i).wait_send()
            self.e_copy(i, self.chunk).wait_send()
        for i in range(len(self.second.steps)):
            self.c_copy(i, self.slot).wait_send()


def flow_scratch(first, second, shape, dtype):
    def pair(n):
        return pltpu.SemaphoreType.DMA((2, n))

    n1, n2 = len(first.steps), len(second.steps)
    return [
        pltpu.VMEM((first.size, *shape), dtype),
        pltpu.VMEM((first.size, *shape), dtype),
        pltpu.VMEM((n1, *shape), dtype),
        pltpu.VMEM((second.size, *shape), dtype),
        pair(first.size),
        pair(n1),
        pair(n2),
        pair(n1),
        pair(first.size),
    ]


FLOW_SCRATCH = 9


class Flows:
    def __init__(self, *flows):
        self.flows = flows

    def in_turn(self, count, call):
        most = max(count(flow) for flow in self.flows)
        for i in range(most):
            for flow in self.flows:
                if i < count(flow):
                    call(flow, i)

    def start_a(self):
        self.in_turn(lambda f: f.first.size, lambda f, i: f.start_a(i))

    def a_to_b(self):
        self.in_turn(lambda f: f.first.size, lambda f, i: f.a_to_b(i))

    def b_to_c(self):
        for flow in reversed(self.flows):
            flow.b_to_c()

    def c_to_e(self):
        for flow in self.flows:
            flow.c_to_e()

    def e_to_f(self):
        self.in_turn(lambda f: f.last, lambda f, i: f.e_to_f(f.last - 1 - i))

    def finish(self):
        for flow in self.flows:
            flow.finish()

    def drain(self):
        for flow in self.flows:
            flow.drain()


PANEL = 16
PANELS = TILE // PANEL


def eliminate(a, panel):
    n, first = TILE, panel * PANEL
    mine = slice(first, first + PANEL)
    row = lax.broadcasted_iota(jnp.int32, (PANEL, n), 0)
    lane = lax.broadcasted_iota(jnp.int32, (PANEL, n), 1)
    lane_all = lax.broadcasted_iota(jnp.int32, (n, n), 1)
    columns = [jnp.broadcast_to(a[:, first + j : first + j + 1], (n, n)) for j in range(PANEL)]
    square = [column[mine] for column in columns]
    rows = jnp.where(
        (lane >= first) & (lane < first + PANEL),
        jnp.where(lane - first == row, 1.0, 0.0),
        a[mine],
    )
    for k in range(PANEL):
        inverse = 1.0 / square[k][k : k + 1]
        column = jnp.where(row == k, square[k] - 1.0, square[k])
        for j in range(k + 1, PANEL):
            square[j] = square[j] - column * (square[j][k : k + 1] * inverse)
        rows = rows - column * (rows[k : k + 1] * inverse)
    change = columns[0] * rows[0:1]
    for j in range(1, PANEL):
        change = change + columns[j] * rows[j : j + 1]
    a = jnp.where((lane_all >= first) & (lane_all < first + PANEL), 0.0, a) - change
    pieces = [a[:first], rows, a[first + PANEL :]]
    return jnp.concatenate([piece for piece in pieces if piece.shape[0]], axis=0)


def split3(wide):
    high = wide.astype(BF16)
    rest = wide - high.astype(F32)
    middle = rest.astype(BF16)
    low = (rest - middle.astype(F32)).astype(BF16)
    return high, middle, low


def stacked_dot(thirds, right):
    rows = thirds[0].shape[0]
    whole = dot(jnp.concatenate(thirds, axis=0), right)
    return [whole[i * rows : (i + 1) * rows] for i in range(len(thirds))]


def product(left, right):
    high = stacked_dot(left, right[0])
    middle = stacked_dot(left[:2], right[1])
    low = dot(left[0], right[2])
    return high[0] + ((high[1] + middle[0]) + (high[2] + middle[1] + low))


LOG2E_SCALED = math.log2(math.e) / WIDTH


def column_norms(rows):
    wide = rows.astype(F32)
    return jnp.sum(wide * wide, axis=1, keepdims=True) * LOG2E_SCALED


def along_lanes(column):
    return jnp.transpose(jnp.broadcast_to(column, (column.shape[0], 128)))[0:1, :]


def kernel_of(cross, column, lane_row):
    return jnp.exp2((2.0 * LOG2E_SCALED) * cross - lane_row - column)


FETCH_ROWS = BLOCK // NQ
FETCH_CUT = 384
FETCH_FLOWS = ((Columns, Planes, (FETCH_ROWS, FETCH_CUT)), (Planes, Columns, (2, FETCH_ROWS, WIDTH - FETCH_CUT)))
HALF = BLOCK // 2
SUM_FLOWS = ((Columns, Planes, (HALF // NQ, BLOCK)), (Planes, Columns, (HALF // NZ, STEPS * TARGETS)))
CHUNKS = ROWS_DEV // CHUNK
CHUNK_TILES = CHUNK // TILE


def update_kernel(
    step_size,
    owner_ref,
    tiles_ref,
    feat_hbm,
    res_hbm,
    coef_hbm,
    update_ref,
    low_ref,
    slab_ref,
    feat_ref,
    res_ref,
    coef_ref,
    weighted_ref,
    along_ref,
    load_sem,
    masked,
    blocks,
    norm_ref,
    product_part,
    product_sum,
    grad_part,
    grad_sum,
    inv,
    thirds,
    between,
    first_tile,
    swap_sem,
    *scratch,
):
    loads = [
        pltpu.make_async_copy(source, target, load_sem.at[i])
        for i, (source, target) in enumerate(
            [(feat_hbm, feat_ref), (res_hbm, res_ref), (coef_hbm, coef_ref)]
        )
    ]
    loads[0].start()
    chip, core = place()
    greet(chip, core)
    for load in loads[1:]:
        load.start()

    me = lax.axis_index("rows") * lax.axis_size("sub") + lax.axis_index("sub")
    loads[0].wait()
    per_tile = TILE // FETCH_ROWS

    def build(s):
        mine = jnp.full((FETCH_ROWS, WIDTH), (owner_ref[s] == me).astype(F32)).astype(BF16)
        for t in range(BLOCK // TILE):
            tile = feat_ref[tiles_ref[s, t]]
            for i in range(per_tile):
                at = slice(i * FETCH_ROWS, (i + 1) * FETCH_ROWS)
                masked[s, t * per_tile + i] = tile[at] * mine

    left, right = pl.ds(0, FETCH_CUT), pl.ds(FETCH_CUT, WIDTH - FETCH_CUT)

    def pair_of(ref):
        return (
            lambda side, chunk: ref.at[side, chunk, :, left],
            lambda side, chunk: ref.at[side, pl.ds(2 * chunk, 2), :, right],
        )

    def flows_of(kinds, parts, totals, scratch):
        flows = []
        for i, (first, second, _) in enumerate(kinds):
            mine = scratch[i * FLOW_SCRATCH : (i + 1) * FLOW_SCRATCH]
            flows.append(Flow(chip, core, first, second, parts[i], totals[i], mine))
        return Flows(*flows)

    fetch = flows_of(FETCH_FLOWS, pair_of(masked), pair_of(blocks), scratch)
    build(1 - core)
    await_greetings()
    fetch.start_a()
    build(core)
    fetch.a_to_b()

    def norms_of(i, carry):
        rows = feat_ref[pl.ds(i * CHUNK_TILES, CHUNK_TILES)].reshape(CHUNK, WIDTH)
        along_ref[i] = jnp.broadcast_to(along_lanes(column_norms(rows)), (8, CHUNK))
        return carry

    lax.fori_loop(0, CHUNKS, norms_of, 0)
    fetch.b_to_c()
    for load in loads[1:]:
        load.wait()
    weighted_ref[...] = (res_ref[...] - RIDGE * coef_ref[...]).astype(BF16)
    fetch.c_to_e()
    fetch.e_to_f()

    def block_rows(s):
        return blocks[s].reshape(BLOCK, WIDTH)

    def set_norm(s):
        norm_ref[s] = jnp.broadcast_to(column_norms(block_rows(s)), (BLOCK, 128))

    sides = [core] * CHUNKS + [1 - core] * CHUNKS
    units = len(sides)

    def cross_of(unit):
        i = unit % CHUNKS
        feat = feat_ref[i * CHUNK_TILES : (i + 1) * CHUNK_TILES].reshape(CHUNK, WIDTH)
        return dot_nt(block_rows(sides[unit]), feat)

    set_norm(core)
    row = lax.broadcasted_iota(jnp.int32, (BLOCK, BLOCK), 0)
    lane = lax.broadcasted_iota(jnp.int32, (BLOCK, BLOCK), 1)
    ridge = jnp.where(row == lane, RIDGE, 0.0)
    corner = blocks[core, 0 : TILE // FETCH_ROWS].reshape(TILE, WIDTH)
    corner_norm = norm_ref[core, 0:TILE, 0:1]
    tile = kernel_of(dot_nt(corner, corner), corner_norm, along_lanes(corner_norm))
    tile = tile + ridge[:TILE, :TILE]
    cross = cross_of(0)
    for unit in range(units):
        i = unit % CHUNKS
        if unit == CHUNKS - 1:
            fetch.finish()
            set_norm(1 - core)
        later = cross_of(unit + 1) if unit + 1 < units else None
        slab = kernel_of(cross, norm_ref[sides[unit]][:, 0:1], along_ref[i][0:1, :]).astype(BF16)
        at = pl.ds(pl.multiple_of(sides[unit] * BLOCK, BLOCK), BLOCK)
        slab_ref[at, i * CHUNK : (i + 1) * CHUNK] = slab
        if unit < PANELS:
            tile = eliminate(tile, unit)
        cross = later
    first_tile[...] = tile

    def share(half):
        at = [pl.ds(pl.multiple_of(s * BLOCK + half * HALF, HALF), HALF) for s in range(STEPS)]
        for s in range(STEPS):
            term = dot(slab_ref[at[s], :], weighted_ref[...]).reshape(NZ, HALF // NZ, TARGETS)
            grad_part[half, :, :, s * TARGETS : (s + 1) * TARGETS] = term
        term = dot_nt(slab_ref[at[0], :], slab_ref[BLOCK:, :])
        product_part[half] = term.reshape(product_part.shape[1:])

    sums = flows_of(
        SUM_FLOWS,
        (
            lambda side, chunk: product_part.at[side, chunk],
            lambda side, chunk: grad_part.at[side, chunk],
        ),
        (
            lambda side, chunk: product_sum.at[side, chunk],
            lambda side, chunk: grad_sum.at[side, chunk],
        ),
        scratch[2 * FLOW_SCRATCH :],
    )
    share(1 - core)
    sums.start_a()
    share(core)
    sums.a_to_b()

    def block_kernel(a, b):
        cross = dot_nt(block_rows(a), block_rows(b))
        return kernel_of(cross, norm_ref[a][:, 0:1], along_lanes(norm_ref[b][:, 0:1]))

    inv[core] = block_kernel(core, core) + ridge
    between[...] = block_kernel(0, 1).astype(BF16)

    def spread(k, tile):
        at = pl.ds(pl.multiple_of(k * TILE, TILE), TILE)
        inside = lax.div(lax.broadcasted_iota(jnp.int32, (TILE, BLOCK), 1), TILE) == k
        lead = dot(tile, inv[core, at, :], HI)
        lead = jnp.where(inside, jnp.concatenate([tile] * (BLOCK // TILE), axis=1), lead)
        column = inv[core, :, at]
        inv[core, :, at] = jnp.zeros_like(column)
        inv[core] -= dot(column, lead, HI)
        inv[core, at, :] = lead

    stages = {(1, 3): sums.b_to_c, (3, 0): sums.c_to_e}

    def step(k, carry):
        at = pl.ds(pl.multiple_of(k * TILE, TILE), TILE)
        for part in range(4):
            tile = inv[core, at, at]
            for panel in range(part * PANELS // 4, (part + 1) * PANELS // 4):
                tile = eliminate(tile, panel)
            inv[core, at, at] = tile
            for (at_k, at_part), stage in stages.items():
                if at_part == part:
                    pl.when(k == at_k)(stage)
        spread(k, inv[core, at, at])
        return carry

    spread(0, first_tile[...])
    lax.fori_loop(1, BLOCK // TILE, step, 0)

    def swap(side):
        return remote(inv.at[core], inv.at[side], swap_sem, 0, (chip, 1 - core))

    def split(s):
        for i, third in enumerate(split3(inv[s])):
            thirds[s, i] = third

    swap(core).start()
    split(core)
    swap(1 - core).wait_recv()
    split(1 - core)
    sums.e_to_f()
    sums.finish()

    both = [[thirds[s, i] for i in range(3)] for s in range(STEPS)]
    grads = jnp.transpose(grad_sum[...].reshape(BLOCK, STEPS * TARGETS))
    first = product(split3(grads[:TARGETS]), both[0]) * step_size
    first_low = first.astype(BF16)
    slab_product = product_sum[...].reshape(BLOCK, BLOCK)
    shift = sum(dot(first_low, third) for third in split3(slab_product))
    past = sum(stacked_dot(split3(first), between[...]))
    gradient = grads[TARGETS:] - shift - RIDGE * past
    second = product(split3(gradient), both[1]) * step_size
    for s, update in enumerate((first, second)):
        update_ref[s] = update
        low_ref[:, s * BLOCK : (s + 1) * BLOCK] = update.astype(BF16)

    swap(core).wait_send()
    fetch.drain()
    sums.drain()


def updates_of(step_size, block_owner, block_tiles, features, residual, coefficients):
    hbm = pl.BlockSpec(memory_space=pltpu.HBM)
    tiled = features.reshape(-1, TILE, WIDTH)
    slab_shape = (STEPS * BLOCK, ROWS_DEV)
    fetch_shape = (STEPS, NQ, FETCH_ROWS, WIDTH)
    product_shape = (2, NQ, HALF // NQ, BLOCK)
    grad_shape = (2, NZ, HALF // NZ, STEPS * TARGETS)
    flows = []
    for first, second, shape in FETCH_FLOWS:
        flows += flow_scratch(first, second, shape, BF16)
    for first, second, shape in SUM_FLOWS:
        flows += flow_scratch(first, second, shape, F32)
    return pl.pallas_call(
        functools.partial(update_kernel, step_size),
        out_shape=(
            pltpu.VMEM((STEPS, TARGETS, BLOCK), F32),
            pltpu.VMEM((TARGETS, STEPS * BLOCK), BF16),
            pltpu.VMEM(slab_shape, BF16),
        ),
        in_specs=[smem(), smem(), hbm, hbm, hbm],
        out_specs=(vmem(), vmem(), vmem()),
        scratch_shapes=[
            pltpu.VMEM(tiled.shape, BF16),
            pltpu.VMEM(residual.shape, F32),
            pltpu.VMEM(coefficients.shape, F32),
            pltpu.VMEM(residual.shape, BF16),
            pltpu.VMEM((CHUNKS, 8, CHUNK), F32),
            pltpu.SemaphoreType.DMA((3,)),
            pltpu.VMEM(fetch_shape, BF16),
            pltpu.VMEM(fetch_shape, BF16),
            pltpu.VMEM((STEPS, BLOCK, 128), F32),
            pltpu.VMEM(product_shape, F32),
            pltpu.VMEM(product_shape, F32),
            pltpu.VMEM(grad_shape, F32),
            pltpu.VMEM(grad_shape, F32),
            pltpu.VMEM((STEPS, BLOCK, BLOCK), F32),
            pltpu.VMEM((STEPS, 3, BLOCK, BLOCK), BF16),
            pltpu.VMEM((BLOCK, BLOCK), BF16),
            pltpu.VMEM((TILE, TILE), F32),
            pltpu.SemaphoreType.DMA((2, 1)),
            *flows,
        ],
        compiler_params=pltpu.CompilerParams(
            collective_id=0, has_side_effects=True, vmem_limit_bytes=48 << 20
        ),
        name="updates",
    )(block_owner, block_tiles, tiled, residual, coefficients)


ROWS_STEP = CHUNK


def final_kernel(
    owner_ref, tiles_ref, update_ref, low_ref, slab_ref, res_ref, coef_ref, res_out, coef_out
):
    step = pl.program_id(0)
    here = pl.ds(pl.multiple_of(step * ROWS_STEP, ROWS_STEP), ROWS_STEP)
    res_out[...] = res_ref[here, :] - jnp.transpose(dot(low_ref[...], slab_ref[:, here]))
    coef_out[...] = coef_ref[here, :]
    me = lax.axis_index("rows") * lax.axis_size("sub") + lax.axis_index("sub")
    tiles_here = ROWS_STEP // TILE
    for s in range(STEPS):
        for t in range(BLOCK // TILE):
            tile = tiles_ref[s, t]

            @pl.when((owner_ref[s] == me) & (lax.div(tile, tiles_here) == step))
            def _():
                at = pl.ds(pl.multiple_of(lax.rem(tile, tiles_here) * TILE, TILE), TILE)
                coef_out[at, :] += jnp.transpose(update_ref[s, :, t * TILE : (t + 1) * TILE])


def final(owner, tiles, updates, low, slabs, residual, coefficients):
    rows = residual.shape[0]
    chunk = pl.BlockSpec((ROWS_STEP, TARGETS), lambda i: (i, 0))
    return pl.pallas_call(
        final_kernel,
        grid=(rows // ROWS_STEP,),
        out_shape=(
            jax.ShapeDtypeStruct(residual.shape, F32),
            jax.ShapeDtypeStruct(coefficients.shape, F32),
        ),
        in_specs=[smem(), smem(), vmem(), vmem(), vmem(), vmem(), vmem()],
        out_specs=(chunk, chunk),
        compiler_params=pltpu.CompilerParams(vmem_limit_bytes=24 << 20),
        name="final",
    )(owner, tiles, updates, low, slabs, residual, coefficients)


def local(features, residual, coefficients, block_owner, block_tiles):
    devices = lax.axis_size("rows") * lax.axis_size("sub")
    step_size = 1.0 / math.sqrt(features.shape[0] * devices)
    updates, low, slabs = updates_of(
        step_size, block_owner, block_tiles, features, residual, coefficients
    )
    return final(block_owner, block_tiles, updates, low, slabs, residual, coefficients)


def solution(mesh):
    in_specs = (
        P(("rows", "sub"), None),
        P(("rows", "sub"), None),
        P(("rows", "sub"), None),
        P(),
        P(),
    )
    out_specs = (P(("rows", "sub"), None), P(("rows", "sub"), None))
    return jax.shard_map(local, mesh=mesh, in_specs=in_specs, out_specs=out_specs, check_vma=False)
```

```python
import functools
import math

import jax
import jax.numpy as jnp
from jax import lax
from jax.experimental import pallas as pl
from jax.experimental.pallas import tpu as pltpu
from jax.sharding import PartitionSpec as P

MESH = pl.DeviceIdType.MESH
HI = lax.Precision.HIGHEST
F32 = jnp.float32
BF16 = jnp.bfloat16

BLOCK = 512
TILE = 128
STEPS = 2
RIDGE = 0.5
WIDTH = 512
TARGETS = 128
NX, NY, NZ = 4, 4, 8
NQ = NX * NY
CHUNK = 1024
ROWS_DEV = 4096
VMEM_BYTES = 64 << 20


def vmem():
    return pl.BlockSpec(memory_space=pltpu.VMEM)


def smem():
    return pl.BlockSpec(memory_space=pltpu.SMEM)


def dot(a, b, precision=None):
    return jnp.dot(a, b, precision=precision, preferred_element_type=F32)


def dot_nt(a, b, precision=None):
    return lax.dot_general(
        a, b, (((1,), (1,)), ((), ())), precision=precision, preferred_element_type=F32
    )


def place():
    across, within = lax.axis_index("rows"), lax.axis_index("sub")
    core = lax.rem(across, 2)
    y = lax.rem(lax.div(across, 2), NY)
    z = lax.div(across, 2 * NY) * 2 + lax.rem(within, 2)
    x = lax.div(within, 2)
    return (x, y, z), core


def device(chip, core):
    x, y, z = chip
    return (lax.div(z, 2) * (2 * NY) + y * 2 + core, x * 2 + lax.rem(z, 2))


SIZES = (NX, NY, NZ)


def moved(chip, step):
    return tuple(
        lax.rem(c + (s + size) % size, size) if s % size else c
        for c, s, size in zip(chip, step, SIZES)
    )


def back(step):
    return tuple(-s for s in step)


def hops(step):
    return sum(min(s, size - s) for s, size in zip(step, SIZES))


class Columns:
    size = NX * NY
    steps = sorted(
        [(i, j, 0) for i in range(NX) for j in range(NY) if i or j], key=lambda s: -hops(s)
    )

    @staticmethod
    def number(chip):
        return chip[0] * NY + chip[1]


class Planes:
    size = NZ
    steps = sorted([(0, 0, k) for k in range(1, NZ)], key=lambda s: -hops(s))

    @staticmethod
    def number(chip):
        return chip[2]


def greet(chip, core):
    barrier = pltpu.get_barrier_semaphore()
    others = [(moved(chip, step), core) for step in Columns.steps + Planes.steps]
    others.append((chip, 1 - core))
    for there, side in others:
        pl.semaphore_signal(barrier, inc=1, device_id=device(there, side), device_id_type=MESH)


def await_greetings():
    pl.semaphore_wait(pltpu.get_barrier_semaphore(), len(Columns.steps) + len(Planes.steps) + 1)


def remote(source, target, sems, i, where):
    return pltpu.make_async_remote_copy(
        src_ref=source,
        dst_ref=target,
        send_sem=sems.at[0, i],
        recv_sem=sems.at[1, i],
        device_id=device(*where),
        device_id_type=MESH,
    )


class Flow:
    def __init__(self, chip, core, first, second, part_at, total_at, scratch):
        self.chip, self.core, self.first, self.second = chip, core, first, second
        self.part_at, self.total_at = part_at, total_at
        self.recv_a, self.half, self.recv_b, self.recv_c = scratch[:4]
        self.sem_a, self.sem_b, self.sem_c, self.sem_e, self.sem_f = scratch[4:]
        self.steps = first.steps + [(0, 0, 0)]
        self.last = len(first.steps)
        self.mate = (chip, 1 - core)
        self.chunk = first.number(chip)
        self.slot = second.number(chip)

    def ahead(self, i):
        there = moved(self.chip, self.steps[i])
        return (there, self.core), self.first.number(there)

    def behind(self, i):
        return self.first.number(moved(self.chip, back(self.steps[i])))

    def a_copy(self, i):
        part = self.part_at(1 - self.core, self.ahead(i)[1])
        return remote(part, self.recv_a.at[i], self.sem_a, i, self.mate)

    def b_copy(self, i):
        return remote(self.half.at[i], self.recv_b.at[i], self.sem_b, i, self.ahead(i)[0])

    def c_copy(self, i, slot):
        there = moved(self.chip, self.second.steps[i])
        mine, target = self.recv_c.at[self.slot], self.recv_c.at[slot]
        return remote(mine, target, self.sem_c, i, (there, self.core))

    def e_copy(self, i, chunk):
        mine, target = self.total_at(self.core, self.chunk), self.total_at(self.core, chunk)
        return remote(mine, target, self.sem_e, i, self.ahead(i)[0])

    def f_copy(self, i, side):
        chunk = self.behind(i)
        mine, target = self.total_at(self.core, chunk), self.total_at(side, chunk)
        return remote(mine, target, self.sem_f, i, self.mate)

    def start_a(self, i):
        self.a_copy(i).start()

    def a_to_b(self, i):
        self.a_copy(i).wait_recv()
        self.half[i] = self.part_at(self.core, self.ahead(i)[1])[...] + self.recv_a[i]
        if i < self.last:
            self.b_copy(i).start()

    def b_to_c(self):
        chunk = self.half[self.last]
        for i in reversed(range(self.last)):
            self.b_copy(i).wait_recv()
            chunk = chunk + self.recv_b[i]
        self.recv_c[self.slot] = chunk
        for i in range(len(self.second.steps)):
            self.c_copy(i, self.slot).start()

    def c_to_e(self):
        for i in range(len(self.second.steps)):
            source = moved(self.chip, back(self.second.steps[i]))
            self.c_copy(i, self.second.number(source)).wait_recv()
        chunk = self.recv_c[0]
        for i in range(1, self.second.size):
            chunk = chunk + self.recv_c[i]
        self.total_at(self.core, self.chunk)[...] = chunk
        for i in range(self.last):
            self.e_copy(i, self.chunk).start()
        self.f_copy(self.last, self.core).start()

    def e_to_f(self, i):
        self.e_copy(i, self.behind(i)).wait_recv()
        self.f_copy(i, self.core).start()

    def finish(self):
        for i in reversed(range(self.first.size)):
            self.f_copy(i, 1 - self.core).wait_recv()

    def drain_scatter(self):
        for i in range(self.first.size):
            self.a_copy(i).wait_send()
        for i in range(self.last):
            self.b_copy(i).wait_send()
        for i in range(len(self.second.steps)):
            self.c_copy(i, self.slot).wait_send()

    def drain_gather(self):
        for i in range(self.last):
            self.e_copy(i, self.chunk).wait_send()
        for i in range(self.first.size):
            self.f_copy(i, self.core).wait_send()


def flow_scratch(first, second, shape, dtype):
    def pair(n):
        return pltpu.SemaphoreType.DMA((2, n))

    n1, n2 = len(first.steps), len(second.steps)
    return [
        pltpu.VMEM((first.size, *shape), dtype),
        pltpu.VMEM((first.size, *shape), dtype),
        pltpu.VMEM((n1, *shape), dtype),
        pltpu.VMEM((second.size, *shape), dtype),
        pair(first.size),
        pair(n1),
        pair(n2),
        pair(n1),
        pair(first.size),
    ]


FLOW_SCRATCH = 9


class Flows:
    def __init__(self, *flows):
        self.flows = flows

    def in_turn(self, count, call):
        most = max(count(flow) for flow in self.flows)
        for i in range(most):
            for flow in self.flows:
                if i < count(flow):
                    call(flow, i)

    def start_a(self):
        self.in_turn(lambda f: f.first.size, lambda f, i: f.start_a(i))

    def a_to_b(self):
        self.in_turn(lambda f: f.first.size, lambda f, i: f.a_to_b(i))

    def b_to_c(self):
        for flow in reversed(self.flows):
            flow.b_to_c()

    def c_to_e(self):
        for flow in self.flows:
            flow.c_to_e()

    def e_to_f(self):
        self.in_turn(lambda f: f.last, lambda f, i: f.e_to_f(f.last - 1 - i))

    def finish(self):
        for flow in self.flows:
            flow.finish()

    def drain_scatter(self):
        for flow in self.flows:
            flow.drain_scatter()

    def drain_gather(self):
        for flow in self.flows:
            flow.drain_gather()


PANEL = 16
PANELS = TILE // PANEL


def eliminate(a, panel):
    n, first = TILE, panel * PANEL
    mine = slice(first, first + PANEL)
    row = lax.broadcasted_iota(jnp.int32, (PANEL, n), 0)
    lane = lax.broadcasted_iota(jnp.int32, (PANEL, n), 1)
    lane_all = lax.broadcasted_iota(jnp.int32, (n, n), 1)
    columns = [jnp.broadcast_to(a[:, first + j : first + j + 1], (n, n)) for j in range(PANEL)]
    square = [column[mine] for column in columns]
    rows = jnp.where(
        (lane >= first) & (lane < first + PANEL),
        jnp.where(lane - first == row, 1.0, 0.0),
        a[mine],
    )
    for k in range(PANEL):
        inverse = 1.0 / square[k][k : k + 1]
        column = jnp.where(row == k, square[k] - 1.0, square[k])
        for j in range(k + 1, PANEL):
            square[j] = square[j] - column * (square[j][k : k + 1] * inverse)
        rows = rows - column * (rows[k : k + 1] * inverse)
    change = columns[0] * rows[0:1]
    for j in range(1, PANEL):
        change = change + columns[j] * rows[j : j + 1]
    a = jnp.where((lane_all >= first) & (lane_all < first + PANEL), 0.0, a) - change
    pieces = [a[:first], rows, a[first + PANEL :]]
    return jnp.concatenate([piece for piece in pieces if piece.shape[0]], axis=0)


def split3(wide):
    high = wide.astype(BF16)
    rest = wide - high.astype(F32)
    middle = rest.astype(BF16)
    low = (rest - middle.astype(F32)).astype(BF16)
    return high, middle, low


def stacked_dot(thirds, right):
    rows = thirds[0].shape[0]
    whole = dot(jnp.concatenate(thirds, axis=0), right)
    return [whole[i * rows : (i + 1) * rows] for i in range(len(thirds))]


def product(left, right):
    high = stacked_dot(left, right[0])
    middle = stacked_dot(left[:2], right[1])
    low = dot(left[0], right[2])
    return high[0] + ((high[1] + middle[0]) + (high[2] + middle[1] + low))


LOG2E_SCALED = math.log2(math.e) / WIDTH


def column_norms(rows):
    wide = rows.astype(F32)
    return jnp.sum(wide * wide, axis=1, keepdims=True) * LOG2E_SCALED


def along_lanes(column):
    return jnp.transpose(jnp.broadcast_to(column, (column.shape[0], 128)))[0:1, :]


def kernel_of(cross, column, lane_row):
    return jnp.exp2((2.0 * LOG2E_SCALED) * cross - lane_row - column)


FETCH_ROWS = BLOCK // NQ
FETCH_CUT = 384
FETCH_FLOWS = ((Columns, Planes, (FETCH_ROWS, FETCH_CUT)), (Planes, Columns, (2, FETCH_ROWS, WIDTH - FETCH_CUT)))
HALF = BLOCK // 2
SUM_FLOWS = ((Columns, Planes, (HALF // NQ, BLOCK)), (Planes, Columns, (HALF // NZ, STEPS * TARGETS)))
CHUNKS = ROWS_DEV // CHUNK
CHUNK_TILES = CHUNK // TILE


def update_kernel(
    step_size,
    owner_ref,
    tiles_ref,
    feat_hbm,
    res_hbm,
    coef_hbm,
    update_ref,
    low_ref,
    slab_ref,
    res_ref,
    coef_ref,
    feat_ref,
    weighted_ref,
    along_ref,
    feat_sem,
    load_sem,
    masked,
    blocks,
    norm_ref,
    product_part,
    product_sum,
    grad_part,
    grad_sum,
    inv,
    thirds,
    between,
    first_tile,
    swap_sem,
    *scratch,
):
    def load_feat(i):
        at = pl.ds(i * CHUNK_TILES, CHUNK_TILES)
        return pltpu.make_async_copy(feat_hbm.at[at], feat_ref.at[at], feat_sem.at[i])

    for i in range(CHUNKS):
        load_feat(i).start()
    loads = [
        pltpu.make_async_copy(source, target, load_sem.at[i])
        for i, (source, target) in enumerate([(res_hbm, res_ref), (coef_hbm, coef_ref)])
    ]
    chip, core = place()
    greet(chip, core)
    for load in loads:
        load.start()

    me = lax.axis_index("rows") * lax.axis_size("sub") + lax.axis_index("sub")
    for i in range(CHUNKS):
        load_feat(i).wait()
    per_tile = TILE // FETCH_ROWS

    def build(s):
        mine = jnp.full((FETCH_ROWS, WIDTH), (owner_ref[s] == me).astype(F32)).astype(BF16)
        for t in range(BLOCK // TILE):
            tile = feat_ref[tiles_ref[s, t]]
            for i in range(per_tile):
                at = slice(i * FETCH_ROWS, (i + 1) * FETCH_ROWS)
                masked[s, t * per_tile + i] = tile[at] * mine

    left, right = pl.ds(0, FETCH_CUT), pl.ds(FETCH_CUT, WIDTH - FETCH_CUT)

    def pair_of(ref):
        return (
            lambda side, chunk: ref.at[side, chunk, :, left],
            lambda side, chunk: ref.at[side, pl.ds(2 * chunk, 2), :, right],
        )

    def flows_of(kinds, parts, totals, scratch):
        flows = []
        for i, (first, second, _) in enumerate(kinds):
            mine = scratch[i * FLOW_SCRATCH : (i + 1) * FLOW_SCRATCH]
            flows.append(Flow(chip, core, first, second, parts[i], totals[i], mine))
        return Flows(*flows)

    fetch = flows_of(FETCH_FLOWS, pair_of(masked), pair_of(blocks), scratch)
    build(1 - core)
    await_greetings()
    fetch.start_a()
    build(core)
    fetch.a_to_b()

    def norms_of(i, carry):
        rows = feat_ref[pl.ds(i * CHUNK_TILES, CHUNK_TILES)].reshape(CHUNK, WIDTH)
        along_ref[i] = jnp.broadcast_to(along_lanes(column_norms(rows)), (8, CHUNK))
        return carry

    lax.fori_loop(0, CHUNKS, norms_of, 0)
    fetch.b_to_c()
    for load in loads:
        load.wait()
    weighted_ref[...] = (res_ref[...] - RIDGE * coef_ref[...]).astype(BF16)
    fetch.c_to_e()
    fetch.e_to_f()

    def block_rows(s):
        return blocks[s].reshape(BLOCK, WIDTH)

    def set_norm(s):
        norm_ref[s] = jnp.broadcast_to(column_norms(block_rows(s)), (BLOCK, 128))

    sides = [core] * CHUNKS + [1 - core] * CHUNKS
    units = len(sides)

    def cross_of(unit):
        i = unit % CHUNKS
        feat = feat_ref[i * CHUNK_TILES : (i + 1) * CHUNK_TILES].reshape(CHUNK, WIDTH)
        return dot_nt(block_rows(sides[unit]), feat)

    set_norm(core)
    row = lax.broadcasted_iota(jnp.int32, (BLOCK, BLOCK), 0)
    lane = lax.broadcasted_iota(jnp.int32, (BLOCK, BLOCK), 1)
    ridge = jnp.where(row == lane, RIDGE, 0.0)
    corner = blocks[core, 0 : TILE // FETCH_ROWS].reshape(TILE, WIDTH)
    corner_norm = norm_ref[core, 0:TILE, 0:1]
    tile = kernel_of(dot_nt(corner, corner), corner_norm, along_lanes(corner_norm))
    tile = tile + ridge[:TILE, :TILE]
    cross = cross_of(0)
    for unit in range(units):
        i = unit % CHUNKS
        if unit == CHUNKS - 1:
            fetch.finish()
            set_norm(1 - core)
        later = cross_of(unit + 1) if unit + 1 < units else None
        slab = kernel_of(cross, norm_ref[sides[unit]][:, 0:1], along_ref[i][0:1, :]).astype(BF16)
        at = pl.ds(pl.multiple_of(sides[unit] * BLOCK, BLOCK), BLOCK)
        slab_ref[at, i * CHUNK : (i + 1) * CHUNK] = slab
        if unit < PANELS:
            tile = eliminate(tile, unit)
        cross = later
    first_tile[...] = tile

    def share(half):
        at = [pl.ds(pl.multiple_of(s * BLOCK + half * HALF, HALF), HALF) for s in range(STEPS)]
        for s in range(STEPS):
            term = dot(slab_ref[at[s], :], weighted_ref[...]).reshape(NZ, HALF // NZ, TARGETS)
            grad_part[half, :, :, s * TARGETS : (s + 1) * TARGETS] = term
        term = dot_nt(slab_ref[at[0], :], slab_ref[BLOCK:, :])
        product_part[half] = term.reshape(product_part.shape[1:])

    sums = flows_of(
        SUM_FLOWS,
        (
            lambda side, chunk: product_part.at[side, chunk],
            lambda side, chunk: grad_part.at[side, chunk],
        ),
        (
            lambda side, chunk: product_sum.at[side, chunk],
            lambda side, chunk: grad_sum.at[side, chunk],
        ),
        scratch[2 * FLOW_SCRATCH :],
    )
    share(1 - core)
    sums.start_a()
    share(core)
    sums.a_to_b()

    def block_kernel(a, b):
        cross = dot_nt(block_rows(a), block_rows(b))
        return kernel_of(cross, norm_ref[a][:, 0:1], along_lanes(norm_ref[b][:, 0:1]))

    inv[core] = block_kernel(core, core) + ridge
    between[...] = block_kernel(0, 1).astype(BF16)
    fetch.drain_scatter()
    fetch.drain_gather()

    def spread(k, tile):
        at = pl.ds(pl.multiple_of(k * TILE, TILE), TILE)
        inside = lax.div(lax.broadcasted_iota(jnp.int32, (TILE, BLOCK), 1), TILE) == k
        lead = dot(tile, inv[core, at, :], HI)
        lead = jnp.where(inside, jnp.concatenate([tile] * (BLOCK // TILE), axis=1), lead)
        column = inv[core, :, at]
        inv[core, :, at] = jnp.zeros_like(column)
        inv[core] -= dot(column, lead, HI)
        inv[core, at, :] = lead

    stages = {(1, 3): sums.b_to_c, (3, 0): sums.c_to_e}

    def step(k, carry):
        at = pl.ds(pl.multiple_of(k * TILE, TILE), TILE)
        for part in range(4):
            tile = inv[core, at, at]
            for panel in range(part * PANELS // 4, (part + 1) * PANELS // 4):
                tile = eliminate(tile, panel)
            inv[core, at, at] = tile
            for (at_k, at_part), stage in stages.items():
                if at_part == part:
                    pl.when(k == at_k)(stage)
        spread(k, inv[core, at, at])
        return carry

    spread(0, first_tile[...])
    lax.fori_loop(1, BLOCK // TILE, step, 0)

    def swap(side):
        return remote(inv.at[core], inv.at[side], swap_sem, 0, (chip, 1 - core))

    def split(s):
        for i, third in enumerate(split3(inv[s])):
            thirds[s, i] = third

    swap(core).start()
    split(core)
    swap(1 - core).wait_recv()
    split(1 - core)
    sums.drain_scatter()
    sums.e_to_f()
    sums.flows[1].finish()

    both = [[thirds[s, i] for i in range(3)] for s in range(STEPS)]
    grads = jnp.transpose(grad_sum[...].reshape(BLOCK, STEPS * TARGETS))
    first = product(split3(grads[:TARGETS]), both[0]) * step_size
    first_low = first.astype(BF16)
    past = sum(stacked_dot(split3(first), between[...]))
    sums.flows[0].finish()
    slab_product = product_sum[...].reshape(BLOCK, BLOCK)
    shift = sum(dot(first_low, third) for third in split3(slab_product))
    gradient = grads[TARGETS:] - shift - RIDGE * past
    second = product(split3(gradient), both[1]) * step_size
    for s, update in enumerate((first, second)):
        update_ref[s] = update
        low_ref[:, s * BLOCK : (s + 1) * BLOCK] = update.astype(BF16)

    swap(core).wait_send()
    sums.drain_gather()


def updates_of(step_size, block_owner, block_tiles, features, residual, coefficients):
    hbm = pl.BlockSpec(memory_space=pltpu.HBM)
    tiled = features.reshape(-1, TILE, WIDTH)
    slab_shape = (STEPS * BLOCK, ROWS_DEV)
    fetch_shape = (STEPS, NQ, FETCH_ROWS, WIDTH)
    product_shape = (2, NQ, HALF // NQ, BLOCK)
    grad_shape = (2, NZ, HALF // NZ, STEPS * TARGETS)
    flows = []
    for first, second, shape in FETCH_FLOWS:
        flows += flow_scratch(first, second, shape, BF16)
    for first, second, shape in SUM_FLOWS:
        flows += flow_scratch(first, second, shape, F32)
    return pl.pallas_call(
        functools.partial(update_kernel, step_size),
        out_shape=(
            pltpu.VMEM((STEPS, TARGETS, BLOCK), F32),
            pltpu.VMEM((TARGETS, STEPS * BLOCK), BF16),
            pltpu.VMEM(slab_shape, BF16),
            pltpu.VMEM(residual.shape, F32),
            pltpu.VMEM(coefficients.shape, F32),
        ),
        in_specs=[smem(), smem(), hbm, hbm, hbm],
        out_specs=(vmem(),) * 5,
        scratch_shapes=[
            pltpu.VMEM(tiled.shape, BF16),
            pltpu.VMEM(residual.shape, BF16),
            pltpu.VMEM((CHUNKS, 8, CHUNK), F32),
            pltpu.SemaphoreType.DMA((CHUNKS,)),
            pltpu.SemaphoreType.DMA((2,)),
            pltpu.VMEM(fetch_shape, BF16),
            pltpu.VMEM(fetch_shape, BF16),
            pltpu.VMEM((STEPS, BLOCK, 128), F32),
            pltpu.VMEM(product_shape, F32),
            pltpu.VMEM(product_shape, F32),
            pltpu.VMEM(grad_shape, F32),
            pltpu.VMEM(grad_shape, F32),
            pltpu.VMEM((STEPS, BLOCK, BLOCK), F32),
            pltpu.VMEM((STEPS, 3, BLOCK, BLOCK), BF16),
            pltpu.VMEM((BLOCK, BLOCK), BF16),
            pltpu.VMEM((TILE, TILE), F32),
            pltpu.SemaphoreType.DMA((2, 1)),
            *flows,
        ],
        compiler_params=pltpu.CompilerParams(
            collective_id=0, has_side_effects=True, vmem_limit_bytes=48 << 20
        ),
        name="updates",
    )(block_owner, block_tiles, tiled, residual, coefficients)


ROWS_STEP = 512


def final_kernel(
    owner_ref,
    tiles_ref,
    update_ref,
    low_ref,
    slab_ref,
    res_ref,
    coef_ref,
    res_hbm,
    coef_hbm,
    res_new,
    coef_new,
    res_sem,
    coef_sem,
):
    me = lax.axis_index("rows") * lax.axis_size("sub") + lax.axis_index("sub")
    coef_new[...] = coef_ref[...]
    for s in range(STEPS):

        @pl.when(owner_ref[s] == me)
        def _():
            for t in range(BLOCK // TILE):
                at = pl.ds(pl.multiple_of(tiles_ref[s, t] * TILE, TILE), TILE)
                coef_new[at, :] += jnp.transpose(update_ref[s, :, t * TILE : (t + 1) * TILE])

    coef_copy = pltpu.make_async_copy(coef_new, coef_hbm, coef_sem)
    coef_copy.start()
    copies = []
    for i in range(res_ref.shape[0] // ROWS_STEP):
        here = pl.ds(i * ROWS_STEP, ROWS_STEP)
        res_new[here, :] = res_ref[here, :] - jnp.transpose(dot(low_ref[...], slab_ref[:, here]))
        copies.append(
            pltpu.make_async_copy(res_new.at[here, :], res_hbm.at[here, :], res_sem.at[i])
        )
        copies[-1].start()
    for copy in copies + [coef_copy]:
        copy.wait()


def final(owner, tiles, updates, low, slabs, residual, coefficients):
    rows = residual.shape[0]
    anywhere = pl.BlockSpec(memory_space=pl.ANY)
    return pl.pallas_call(
        final_kernel,
        out_shape=(
            jax.ShapeDtypeStruct(residual.shape, F32),
            jax.ShapeDtypeStruct(coefficients.shape, F32),
        ),
        in_specs=[smem(), smem(), vmem(), vmem(), vmem(), vmem(), vmem()],
        out_specs=(anywhere, anywhere),
        scratch_shapes=[
            pltpu.VMEM(residual.shape, F32),
            pltpu.VMEM(coefficients.shape, F32),
            pltpu.SemaphoreType.DMA((rows // ROWS_STEP,)),
            pltpu.SemaphoreType.DMA,
        ],
        compiler_params=pltpu.CompilerParams(vmem_limit_bytes=24 << 20),
        name="final",
    )(owner, tiles, updates, low, slabs, residual, coefficients)


def local(features, residual, coefficients, block_owner, block_tiles):
    devices = lax.axis_size("rows") * lax.axis_size("sub")
    step_size = 1.0 / math.sqrt(features.shape[0] * devices)
    results = updates_of(
        step_size, block_owner, block_tiles, features, residual, coefficients
    )
    return final(block_owner, block_tiles, *results)


def solution(mesh):
    in_specs = (
        P(("rows", "sub"), None),
        P(("rows", "sub"), None),
        P(("rows", "sub"), None),
        P(),
        P(),
    )
    out_specs = (P(("rows", "sub"), None), P(("rows", "sub"), None))
    return jax.shard_map(local, mesh=mesh, in_specs=in_specs, out_specs=out_specs, check_vma=False)
```

```python
import functools
import math

import jax
import jax.numpy as jnp
from jax import lax
from jax.experimental import pallas as pl
from jax.experimental.pallas import tpu as pltpu
from jax.sharding import PartitionSpec as P

MESH = pl.DeviceIdType.MESH
F32 = jnp.float32
BF16 = jnp.bfloat16

BLOCK = 512
TILE = 128
STEPS = 2
RIDGE = 0.5
WIDTH = 512
TARGETS = 128
NX, NY, NZ = 4, 4, 8
NQ = NX * NY
CHUNK = 1024
ROWS_DEV = 4096
VMEM_BYTES = 64 << 20


def vmem():
    return pl.BlockSpec(memory_space=pltpu.VMEM)


def smem():
    return pl.BlockSpec(memory_space=pltpu.SMEM)


def dot(a, b, precision=None):
    return jnp.dot(a, b, precision=precision, preferred_element_type=F32)


def dot_nt(a, b, precision=None):
    return lax.dot_general(
        a, b, (((1,), (1,)), ((), ())), precision=precision, preferred_element_type=F32
    )


def place():
    across, within = lax.axis_index("rows"), lax.axis_index("sub")
    core = lax.rem(across, 2)
    y = lax.rem(lax.div(across, 2), NY)
    z = lax.div(across, 2 * NY) * 2 + lax.rem(within, 2)
    x = lax.div(within, 2)
    return (x, y, z), core


def device(chip, core):
    x, y, z = chip
    return (lax.div(z, 2) * (2 * NY) + y * 2 + core, x * 2 + lax.rem(z, 2))


SIZES = (NX, NY, NZ)


def moved(chip, step):
    return tuple(
        lax.rem(c + (s + size) % size, size) if s % size else c
        for c, s, size in zip(chip, step, SIZES)
    )


def back(step):
    return tuple(-s for s in step)


def hops(step):
    return sum(min(s, size - s) for s, size in zip(step, SIZES))


class Columns:
    size = NX * NY
    steps = sorted(
        [(i, j, 0) for i in range(NX) for j in range(NY) if i or j], key=lambda s: -hops(s)
    )

    @staticmethod
    def number(chip):
        return chip[0] * NY + chip[1]


class Planes:
    size = NZ
    steps = sorted([(0, 0, k) for k in range(1, NZ)], key=lambda s: -hops(s))

    @staticmethod
    def number(chip):
        return chip[2]


def greet(chip, core):
    barrier = pltpu.get_barrier_semaphore()
    others = [(moved(chip, step), core) for step in Columns.steps + Planes.steps]
    others.append((chip, 1 - core))
    for there, side in others:
        pl.semaphore_signal(barrier, inc=1, device_id=device(there, side), device_id_type=MESH)


def await_greetings():
    pl.semaphore_wait(pltpu.get_barrier_semaphore(), len(Columns.steps) + len(Planes.steps) + 1)


def remote(source, target, sems, i, where):
    return pltpu.make_async_remote_copy(
        src_ref=source,
        dst_ref=target,
        send_sem=sems.at[0, i],
        recv_sem=sems.at[1, i],
        device_id=device(*where),
        device_id_type=MESH,
    )


class Flow:
    def __init__(self, chip, core, first, second, part_at, total_at, scratch):
        self.chip, self.core, self.first, self.second = chip, core, first, second
        self.part_at, self.total_at = part_at, total_at
        self.recv_a, self.half, self.recv_b, self.recv_c = scratch[:4]
        self.sem_a, self.sem_b, self.sem_c, self.sem_e, self.sem_f = scratch[4:]
        self.steps = first.steps + [(0, 0, 0)]
        self.last = len(first.steps)
        self.mate = (chip, 1 - core)
        self.chunk = first.number(chip)
        self.slot = second.number(chip)

    def ahead(self, i):
        there = moved(self.chip, self.steps[i])
        return (there, self.core), self.first.number(there)

    def behind(self, i):
        return self.first.number(moved(self.chip, back(self.steps[i])))

    def a_copy(self, i):
        part = self.part_at(1 - self.core, self.ahead(i)[1])
        return remote(part, self.recv_a.at[i], self.sem_a, i, self.mate)

    def b_copy(self, i):
        return remote(self.half.at[i], self.recv_b.at[i], self.sem_b, i, self.ahead(i)[0])

    def c_copy(self, i, slot):
        there = moved(self.chip, self.second.steps[i])
        mine, target = self.recv_c.at[self.slot], self.recv_c.at[slot]
        return remote(mine, target, self.sem_c, i, (there, self.core))

    def e_copy(self, i, chunk):
        mine, target = self.total_at(self.core, self.chunk), self.total_at(self.core, chunk)
        return remote(mine, target, self.sem_e, i, self.ahead(i)[0])

    def f_copy(self, i, side):
        chunk = self.behind(i)
        mine, target = self.total_at(self.core, chunk), self.total_at(side, chunk)
        return remote(mine, target, self.sem_f, i, self.mate)

    def start_a(self, i):
        self.a_copy(i).start()

    def a_to_b(self, i):
        self.a_copy(i).wait_recv()
        self.half[i] = self.part_at(self.core, self.ahead(i)[1])[...] + self.recv_a[i]
        if i < self.last:
            self.b_copy(i).start()

    def b_to_c(self):
        chunk = self.half[self.last]
        for i in reversed(range(self.last)):
            self.b_copy(i).wait_recv()
            chunk = chunk + self.recv_b[i]
        self.recv_c[self.slot] = chunk
        for i in range(len(self.second.steps)):
            self.c_copy(i, self.slot).start()

    def c_to_e(self):
        for i in range(len(self.second.steps)):
            source = moved(self.chip, back(self.second.steps[i]))
            self.c_copy(i, self.second.number(source)).wait_recv()
        chunk = self.recv_c[0]
        for i in range(1, self.second.size):
            chunk = chunk + self.recv_c[i]
        self.total_at(self.core, self.chunk)[...] = chunk
        for i in range(self.last):
            self.e_copy(i, self.chunk).start()
        self.f_copy(self.last, self.core).start()

    def e_to_f(self, i):
        self.e_copy(i, self.behind(i)).wait_recv()
        self.f_copy(i, self.core).start()

    def finish(self):
        for i in reversed(range(self.first.size)):
            self.f_copy(i, 1 - self.core).wait_recv()

    def drain_scatter(self):
        for i in range(self.first.size):
            self.a_copy(i).wait_send()
        for i in range(self.last):
            self.b_copy(i).wait_send()
        for i in range(len(self.second.steps)):
            self.c_copy(i, self.slot).wait_send()

    def drain_gather(self):
        for i in range(self.last):
            self.e_copy(i, self.chunk).wait_send()
        for i in range(self.first.size):
            self.f_copy(i, self.core).wait_send()


def flow_scratch(first, second, shape, dtype):
    def pair(n):
        return pltpu.SemaphoreType.DMA((2, n))

    n1, n2 = len(first.steps), len(second.steps)
    return [
        pltpu.VMEM((first.size, *shape), dtype),
        pltpu.VMEM((first.size, *shape), dtype),
        pltpu.VMEM((n1, *shape), dtype),
        pltpu.VMEM((second.size, *shape), dtype),
        pair(first.size),
        pair(n1),
        pair(n2),
        pair(n1),
        pair(first.size),
    ]


FLOW_SCRATCH = 9


class Flows:
    def __init__(self, *flows):
        self.flows = flows

    def in_turn(self, count, call):
        most = max(count(flow) for flow in self.flows)
        for i in range(most):
            for flow in self.flows:
                if i < count(flow):
                    call(flow, i)

    def start_a(self):
        self.in_turn(lambda f: f.first.size, lambda f, i: f.start_a(i))

    def a_to_b(self):
        self.in_turn(lambda f: f.first.size, lambda f, i: f.a_to_b(i))

    def b_to_c(self):
        for flow in reversed(self.flows):
            flow.b_to_c()

    def c_to_e(self):
        for flow in self.flows:
            flow.c_to_e()

    def e_to_f(self):
        self.in_turn(lambda f: f.last, lambda f, i: f.e_to_f(f.last - 1 - i))

    def finish(self):
        for flow in self.flows:
            flow.finish()

    def drain_scatter(self):
        for flow in self.flows:
            flow.drain_scatter()

    def drain_gather(self):
        for flow in self.flows:
            flow.drain_gather()


PANEL = 16
PANELS = TILE // PANEL


def split3(wide):
    high = wide.astype(BF16)
    rest = wide - high.astype(F32)
    middle = rest.astype(BF16)
    low = (rest - middle.astype(F32)).astype(BF16)
    return high, middle, low


LEFT_THIRDS = (0, 0, 1, 0, 2, 1)
RIGHT_THIRDS = (0, 1, 0, 2, 0, 1)


def wide_dot(left, right):
    left, right = split3(left), split3(right)
    return dot(
        jnp.concatenate([left[i] for i in LEFT_THIRDS], axis=1),
        jnp.concatenate([right[i] for i in RIGHT_THIRDS], axis=0),
    )


def eliminate(a, panel):
    n, first = TILE, panel * PANEL
    mine = slice(first, first + PANEL)
    row = lax.broadcasted_iota(jnp.int32, (PANEL, n), 0)
    lane = lax.broadcasted_iota(jnp.int32, (PANEL, n), 1)
    square = [
        jnp.broadcast_to(a[mine, first + j : first + j + 1], (PANEL, n)) for j in range(PANEL)
    ]
    rows = jnp.where(
        (lane >= first) & (lane < first + PANEL),
        jnp.where(lane - first == row, 1.0, 0.0),
        a[mine],
    )
    for k in range(PANEL):
        inverse = 1.0 / square[k][k : k + 1]
        column = jnp.where(row == k, square[k] - 1.0, square[k])
        for j in range(k + 1, PANEL):
            square[j] = square[j] - column * (square[j][k : k + 1] * inverse)
        rows = rows - column * (rows[k : k + 1] * inverse)
    lane_all = lax.broadcasted_iota(jnp.int32, (n, n), 1)
    inside = (lane_all >= first) & (lane_all < first + PANEL)
    columns = jnp.where(inside, a, 0.0)
    if first:
        columns = pltpu.roll(columns, n - first, 1)
    left = [third.astype(F32) for third in split3(columns)]
    right = split3(rows)
    packed = left[0]
    for i, t in enumerate(LEFT_THIRDS[1:]):
        packed = packed + pltpu.roll(left[t], PANEL * (i + 1), 1)
    below = [right[t] for t in RIGHT_THIRDS]
    below.append(jnp.zeros((n - PANEL * len(below), n), BF16))
    change = dot(packed.astype(BF16), jnp.concatenate(below, axis=0))
    a = jnp.where(inside, 0.0, a) - change
    pieces = [a[:first], rows, a[first + PANEL :]]
    return jnp.concatenate([piece for piece in pieces if piece.shape[0]], axis=0)


def stacked_dot(thirds, right):
    rows = thirds[0].shape[0]
    whole = dot(jnp.concatenate(thirds, axis=0), right)
    return [whole[i * rows : (i + 1) * rows] for i in range(len(thirds))]


def product(left, right):
    high = stacked_dot(left, right[0])
    middle = stacked_dot(left[:2], right[1])
    low = dot(left[0], right[2])
    return high[0] + ((high[1] + middle[0]) + (high[2] + middle[1] + low))


LOG2E_SCALED = math.log2(math.e) / WIDTH


def column_norms(rows):
    wide = rows.astype(F32)
    return jnp.sum(wide * wide, axis=1, keepdims=True) * LOG2E_SCALED


def along_lanes(column):
    return jnp.transpose(jnp.broadcast_to(column, (column.shape[0], 128)))[0:1, :]


def kernel_of(cross, column, lane_row):
    return jnp.exp2((2.0 * LOG2E_SCALED) * cross - lane_row - column)


FETCH_ROWS = BLOCK // NQ
FETCH_CUT = 384
FETCH_FLOWS = ((Columns, Planes, (FETCH_ROWS, FETCH_CUT)), (Planes, Columns, (2, FETCH_ROWS, WIDTH - FETCH_CUT)))
HALF = BLOCK // 2
SUM_FLOWS = ((Columns, Planes, (HALF // NQ, BLOCK)), (Planes, Columns, (HALF // NZ, STEPS * TARGETS)))
CHUNKS = ROWS_DEV // CHUNK
CHUNK_TILES = CHUNK // TILE


def update_kernel(
    step_size,
    owner_ref,
    tiles_ref,
    feat_hbm,
    res_hbm,
    coef_hbm,
    update_ref,
    low_ref,
    slab_ref,
    res_ref,
    coef_ref,
    feat_ref,
    weighted_ref,
    along_ref,
    feat_sem,
    load_sem,
    masked,
    blocks,
    norm_ref,
    product_part,
    product_sum,
    grad_part,
    grad_sum,
    inv,
    thirds,
    between,
    swap_sem,
    *scratch,
):
    def load_feat(i):
        at = pl.ds(i * CHUNK_TILES, CHUNK_TILES)
        return pltpu.make_async_copy(feat_hbm.at[at], feat_ref.at[at], feat_sem.at[i])

    for i in range(CHUNKS):
        load_feat(i).start()
    loads = [
        pltpu.make_async_copy(source, target, load_sem.at[i])
        for i, (source, target) in enumerate([(res_hbm, res_ref), (coef_hbm, coef_ref)])
    ]
    chip, core = place()
    greet(chip, core)
    for load in loads:
        load.start()

    me = lax.axis_index("rows") * lax.axis_size("sub") + lax.axis_index("sub")
    for i in range(CHUNKS):
        load_feat(i).wait()
    per_tile = TILE // FETCH_ROWS

    def build(s):
        mine = jnp.full((FETCH_ROWS, WIDTH), (owner_ref[s] == me).astype(F32)).astype(BF16)
        for t in range(BLOCK // TILE):
            tile = feat_ref[tiles_ref[s, t]]
            for i in range(per_tile):
                at = slice(i * FETCH_ROWS, (i + 1) * FETCH_ROWS)
                masked[s, t * per_tile + i] = tile[at] * mine

    left, right = pl.ds(0, FETCH_CUT), pl.ds(FETCH_CUT, WIDTH - FETCH_CUT)

    def pair_of(ref):
        return (
            lambda side, chunk: ref.at[side, chunk, :, left],
            lambda side, chunk: ref.at[side, pl.ds(2 * chunk, 2), :, right],
        )

    def flows_of(kinds, parts, totals, scratch):
        flows = []
        for i, (first, second, _) in enumerate(kinds):
            mine = scratch[i * FLOW_SCRATCH : (i + 1) * FLOW_SCRATCH]
            flows.append(Flow(chip, core, first, second, parts[i], totals[i], mine))
        return Flows(*flows)

    fetch = flows_of(FETCH_FLOWS, pair_of(masked), pair_of(blocks), scratch)
    build(1 - core)
    await_greetings()
    fetch.start_a()
    build(core)
    fetch.a_to_b()

    def norms_of(i, carry):
        rows = feat_ref[pl.ds(i * CHUNK_TILES, CHUNK_TILES)].reshape(CHUNK, WIDTH)
        along_ref[i] = jnp.broadcast_to(along_lanes(column_norms(rows)), (8, CHUNK))
        return carry

    lax.fori_loop(0, CHUNKS, norms_of, 0)
    fetch.b_to_c()
    for load in loads:
        load.wait()
    weighted_ref[...] = (res_ref[...] - RIDGE * coef_ref[...]).astype(BF16)
    fetch.c_to_e()
    fetch.e_to_f()

    def block_rows(s):
        return blocks[s].reshape(BLOCK, WIDTH)

    def set_norm(s):
        norm_ref[s] = jnp.broadcast_to(column_norms(block_rows(s)), (BLOCK, 128))

    sides = [core] * CHUNKS + [1 - core] * CHUNKS
    units = len(sides)

    def cross_of(unit):
        i = unit % CHUNKS
        feat = feat_ref[i * CHUNK_TILES : (i + 1) * CHUNK_TILES].reshape(CHUNK, WIDTH)
        return dot_nt(block_rows(sides[unit]), feat)

    set_norm(core)
    cross = cross_of(0)
    for unit in range(units):
        i = unit % CHUNKS
        if unit == CHUNKS - 1:
            fetch.finish()
            set_norm(1 - core)
        later = cross_of(unit + 1) if unit + 1 < units else None
        slab = kernel_of(cross, norm_ref[sides[unit]][:, 0:1], along_ref[i][0:1, :]).astype(BF16)
        at = pl.ds(pl.multiple_of(sides[unit] * BLOCK, BLOCK), BLOCK)
        slab_ref[at, i * CHUNK : (i + 1) * CHUNK] = slab
        cross = later

    def share(half):
        at = [pl.ds(pl.multiple_of(s * BLOCK + half * HALF, HALF), HALF) for s in range(STEPS)]
        for s in range(STEPS):
            term = dot(slab_ref[at[s], :], weighted_ref[...]).reshape(NZ, HALF // NZ, TARGETS)
            grad_part[half, :, :, s * TARGETS : (s + 1) * TARGETS] = term
        term = dot_nt(slab_ref[at[0], :], slab_ref[BLOCK:, :])
        product_part[half] = term.reshape(product_part.shape[1:])

    sums = flows_of(
        SUM_FLOWS,
        (
            lambda side, chunk: product_part.at[side, chunk],
            lambda side, chunk: grad_part.at[side, chunk],
        ),
        (
            lambda side, chunk: product_sum.at[side, chunk],
            lambda side, chunk: grad_sum.at[side, chunk],
        ),
        scratch[2 * FLOW_SCRATCH :],
    )
    share(1 - core)
    sums.start_a()
    share(core)
    sums.a_to_b()

    def block_kernel(a, b):
        cross = dot_nt(block_rows(a), block_rows(b))
        return kernel_of(cross, norm_ref[a][:, 0:1], along_lanes(norm_ref[b][:, 0:1]))

    row = lax.broadcasted_iota(jnp.int32, (BLOCK, BLOCK), 0)
    lane = lax.broadcasted_iota(jnp.int32, (BLOCK, BLOCK), 1)
    inv[core] = block_kernel(core, core) + jnp.where(row == lane, RIDGE, 0.0)
    between[...] = block_kernel(0, 1).astype(BF16)
    fetch.drain_scatter()
    fetch.drain_gather()

    def spread(k, tile):
        at = pl.ds(pl.multiple_of(k * TILE, TILE), TILE)
        inside = lax.div(lax.broadcasted_iota(jnp.int32, (TILE, BLOCK), 1), TILE) == k
        lead = wide_dot(tile, inv[core, at, :])
        lead = jnp.where(inside, jnp.concatenate([tile] * (BLOCK // TILE), axis=1), lead)
        column = inv[core, :, at]
        inv[core, :, at] = jnp.zeros_like(column)
        inv[core] -= wide_dot(column, lead)
        inv[core, at, :] = lead

    stages = {(1, 0): sums.b_to_c, (2, 4): sums.c_to_e}

    def look(k, part):
        for (at_k, at_part), stage in stages.items():
            if at_part == part:
                pl.when(k == at_k)(stage)

    def step(k, carry):
        at = pl.ds(pl.multiple_of(k * TILE, TILE), TILE)
        for part in range(4):
            tile = inv[core, at, at]
            for panel in range(part * PANELS // 4, (part + 1) * PANELS // 4):
                tile = eliminate(tile, panel)
            inv[core, at, at] = tile
            look(k, part)
        spread(k, inv[core, at, at])
        look(k, 4)
        return carry

    lax.fori_loop(0, BLOCK // TILE, step, 0)

    def swap(side):
        return remote(inv.at[core], inv.at[side], swap_sem, 0, (chip, 1 - core))

    def split(s):
        for i, third in enumerate(split3(inv[s])):
            thirds[s, i] = third

    swap(core).start()
    split(core)
    swap(1 - core).wait_recv()
    split(1 - core)
    sums.drain_scatter()
    sums.e_to_f()
    sums.flows[1].finish()

    both = [[thirds[s, i] for i in range(3)] for s in range(STEPS)]
    grads = jnp.transpose(grad_sum[...].reshape(BLOCK, STEPS * TARGETS))
    first = product(split3(grads[:TARGETS]), both[0]) * step_size
    first_low = first.astype(BF16)
    past = sum(stacked_dot(split3(first), between[...]))
    sums.flows[0].finish()
    slab_product = product_sum[...].reshape(BLOCK, BLOCK)
    shift = sum(dot(first_low, third) for third in split3(slab_product))
    gradient = grads[TARGETS:] - shift - RIDGE * past
    second = product(split3(gradient), both[1]) * step_size
    for s, update in enumerate((first, second)):
        update_ref[s] = update
        low_ref[:, s * BLOCK : (s + 1) * BLOCK] = update.astype(BF16)

    swap(core).wait_send()
    sums.drain_gather()


def updates_of(step_size, block_owner, block_tiles, features, residual, coefficients):
    hbm = pl.BlockSpec(memory_space=pltpu.HBM)
    tiled = features.reshape(-1, TILE, WIDTH)
    slab_shape = (STEPS * BLOCK, ROWS_DEV)
    fetch_shape = (STEPS, NQ, FETCH_ROWS, WIDTH)
    product_shape = (2, NQ, HALF // NQ, BLOCK)
    grad_shape = (2, NZ, HALF // NZ, STEPS * TARGETS)
    flows = []
    for first, second, shape in FETCH_FLOWS:
        flows += flow_scratch(first, second, shape, BF16)
    for first, second, shape in SUM_FLOWS:
        flows += flow_scratch(first, second, shape, F32)
    return pl.pallas_call(
        functools.partial(update_kernel, step_size),
        out_shape=(
            pltpu.VMEM((STEPS, TARGETS, BLOCK), F32),
            pltpu.VMEM((TARGETS, STEPS * BLOCK), BF16),
            pltpu.VMEM(slab_shape, BF16),
            pltpu.VMEM(residual.shape, F32),
            pltpu.VMEM(coefficients.shape, F32),
        ),
        in_specs=[smem(), smem(), hbm, hbm, hbm],
        out_specs=(vmem(),) * 5,
        scratch_shapes=[
            pltpu.VMEM(tiled.shape, BF16),
            pltpu.VMEM(residual.shape, BF16),
            pltpu.VMEM((CHUNKS, 8, CHUNK), F32),
            pltpu.SemaphoreType.DMA((CHUNKS,)),
            pltpu.SemaphoreType.DMA((2,)),
            pltpu.VMEM(fetch_shape, BF16),
            pltpu.VMEM(fetch_shape, BF16),
            pltpu.VMEM((STEPS, BLOCK, 128), F32),
            pltpu.VMEM(product_shape, F32),
            pltpu.VMEM(product_shape, F32),
            pltpu.VMEM(grad_shape, F32),
            pltpu.VMEM(grad_shape, F32),
            pltpu.VMEM((STEPS, BLOCK, BLOCK), F32),
            pltpu.VMEM((STEPS, 3, BLOCK, BLOCK), BF16),
            pltpu.VMEM((BLOCK, BLOCK), BF16),
            pltpu.SemaphoreType.DMA((2, 1)),
            *flows,
        ],
        compiler_params=pltpu.CompilerParams(
            collective_id=0, has_side_effects=True, vmem_limit_bytes=48 << 20
        ),
        name="updates",
    )(block_owner, block_tiles, tiled, residual, coefficients)


ROWS_STEP = 512


def final_kernel(
    owner_ref,
    tiles_ref,
    update_ref,
    low_ref,
    slab_ref,
    res_ref,
    coef_ref,
    res_hbm,
    coef_hbm,
    res_new,
    coef_new,
    res_sem,
    coef_sem,
):
    me = lax.axis_index("rows") * lax.axis_size("sub") + lax.axis_index("sub")
    coef_new[...] = coef_ref[...]
    for s in range(STEPS):

        @pl.when(owner_ref[s] == me)
        def _():
            for t in range(BLOCK // TILE):
                at = pl.ds(pl.multiple_of(tiles_ref[s, t] * TILE, TILE), TILE)
                coef_new[at, :] += jnp.transpose(update_ref[s, :, t * TILE : (t + 1) * TILE])

    coef_copy = pltpu.make_async_copy(coef_new, coef_hbm, coef_sem)
    coef_copy.start()
    copies = []
    for i in range(res_ref.shape[0] // ROWS_STEP):
        here = pl.ds(i * ROWS_STEP, ROWS_STEP)
        res_new[here, :] = res_ref[here, :] - jnp.transpose(dot(low_ref[...], slab_ref[:, here]))
        copies.append(
            pltpu.make_async_copy(res_new.at[here, :], res_hbm.at[here, :], res_sem.at[i])
        )
        copies[-1].start()
    for copy in copies + [coef_copy]:
        copy.wait()


def final(owner, tiles, updates, low, slabs, residual, coefficients):
    rows = residual.shape[0]
    anywhere = pl.BlockSpec(memory_space=pl.ANY)
    return pl.pallas_call(
        final_kernel,
        out_shape=(
            jax.ShapeDtypeStruct(residual.shape, F32),
            jax.ShapeDtypeStruct(coefficients.shape, F32),
        ),
        in_specs=[smem(), smem(), vmem(), vmem(), vmem(), vmem(), vmem()],
        out_specs=(anywhere, anywhere),
        scratch_shapes=[
            pltpu.VMEM(residual.shape, F32),
            pltpu.VMEM(coefficients.shape, F32),
            pltpu.SemaphoreType.DMA((rows // ROWS_STEP,)),
            pltpu.SemaphoreType.DMA,
        ],
        compiler_params=pltpu.CompilerParams(vmem_limit_bytes=24 << 20),
        name="final",
    )(owner, tiles, updates, low, slabs, residual, coefficients)


def local(features, residual, coefficients, block_owner, block_tiles):
    devices = lax.axis_size("rows") * lax.axis_size("sub")
    step_size = 1.0 / math.sqrt(features.shape[0] * devices)
    results = updates_of(
        step_size, block_owner, block_tiles, features, residual, coefficients
    )
    return final(block_owner, block_tiles, *results)


def solution(mesh):
    in_specs = (
        P(("rows", "sub"), None),
        P(("rows", "sub"), None),
        P(("rows", "sub"), None),
        P(),
        P(),
    )
    out_specs = (P(("rows", "sub"), None), P(("rows", "sub"), None))
    return jax.shard_map(local, mesh=mesh, in_specs=in_specs, out_specs=out_specs, check_vma=False)
```

```python
import functools
import math

import jax
import jax.numpy as jnp
from jax import lax
from jax.experimental import pallas as pl
from jax.experimental.pallas import tpu as pltpu
from jax.sharding import PartitionSpec as P

MESH = pl.DeviceIdType.MESH
F32 = jnp.float32
BF16 = jnp.bfloat16

BLOCK = 512
TILE = 128
STEPS = 2
RIDGE = 0.5
WIDTH = 512
TARGETS = 128
NX, NY, NZ = 4, 4, 8
NQ = NX * NY
CHUNK = 1024
ROWS_DEV = 4096
VMEM_BYTES = 64 << 20


def vmem():
    return pl.BlockSpec(memory_space=pltpu.VMEM)


def smem():
    return pl.BlockSpec(memory_space=pltpu.SMEM)


def dot(a, b, precision=None):
    return jnp.dot(a, b, precision=precision, preferred_element_type=F32)


def dot_nt(a, b, precision=None):
    return lax.dot_general(
        a, b, (((1,), (1,)), ((), ())), precision=precision, preferred_element_type=F32
    )


def place():
    across, within = lax.axis_index("rows"), lax.axis_index("sub")
    core = lax.rem(across, 2)
    y = lax.rem(lax.div(across, 2), NY)
    z = lax.div(across, 2 * NY) * 2 + lax.rem(within, 2)
    x = lax.div(within, 2)
    return (x, y, z), core


def device(chip, core):
    x, y, z = chip
    return (lax.div(z, 2) * (2 * NY) + y * 2 + core, x * 2 + lax.rem(z, 2))


SIZES = (NX, NY, NZ)


def moved(chip, step):
    return tuple(
        lax.rem(c + (s + size) % size, size) if s % size else c
        for c, s, size in zip(chip, step, SIZES)
    )


def back(step):
    return tuple(-s for s in step)


def hops(step):
    return sum(min(s, size - s) for s, size in zip(step, SIZES))


COLUMN_STEPS = sorted(
    [(i, j, 0) for i in range(NX) for j in range(NY) if i or j], key=lambda s: -hops(s)
)
GROUP_STEPS = (2, 1, 3, 0)


class Columns:
    size = NX * NY
    steps = COLUMN_STEPS
    groups = [[i for i, s in enumerate(COLUMN_STEPS) if s[0] == dx] for dx in GROUP_STEPS]
    members = NY

    @staticmethod
    def number(chip):
        return chip[0] * NY + chip[1]

    @staticmethod
    def group_start(chip, j):
        return moved(chip, (-GROUP_STEPS[j], 0, 0))[0] * NY


class Planes:
    size = NZ
    steps = sorted([(0, 0, k) for k in range(1, NZ)], key=lambda s: -hops(s))

    groups = [list(range(NZ - 1))]
    members = NZ

    @staticmethod
    def number(chip):
        return chip[2]

    @staticmethod
    def group_start(chip, j):
        return 0


def greet(chip, core):
    barrier = pltpu.get_barrier_semaphore()
    others = [(moved(chip, step), core) for step in Columns.steps + Planes.steps]
    others.append((chip, 1 - core))
    for there, side in others:
        pl.semaphore_signal(barrier, inc=1, device_id=device(there, side), device_id_type=MESH)


def await_greetings():
    pl.semaphore_wait(pltpu.get_barrier_semaphore(), len(Columns.steps) + len(Planes.steps) + 1)


def remote(source, target, sems, i, where):
    return pltpu.make_async_remote_copy(
        src_ref=source,
        dst_ref=target,
        send_sem=sems.at[0, i],
        recv_sem=sems.at[1, i],
        device_id=device(*where),
        device_id_type=MESH,
    )


class Chunks:
    def __init__(self, ref, per=1, lanes=None):
        self.ref, self.per, self.lanes = ref, per, lanes

    def some(self, side, index):
        if self.lanes is None:
            return self.ref.at[side, index]
        return self.ref.at[side, index, :, self.lanes]

    def one(self, side, chunk):
        return self.some(side, chunk if self.per == 1 else pl.ds(self.per * chunk, self.per))

    def run(self, side, start, count):
        return self.some(side, pl.ds(self.per * start, self.per * count))


class Flow:
    def __init__(self, chip, core, first, second, part, total, scratch):
        self.chip, self.core, self.first, self.second = chip, core, first, second
        self.part, self.total = part, total
        self.recv_a, self.half, self.recv_b, self.recv_c = scratch[:4]
        self.sem_a, self.sem_b, self.sem_c, self.sem_e, self.sem_f = scratch[4:]
        self.steps = first.steps + [(0, 0, 0)]
        self.last = len(first.steps)
        self.mate = (chip, 1 - core)
        self.chunk = first.number(chip)
        self.slot = second.number(chip)

    def ahead(self, i):
        there = moved(self.chip, self.steps[i])
        return (there, self.core), self.first.number(there)

    def behind(self, i):
        return self.first.number(moved(self.chip, back(self.steps[i])))

    def a_copy(self):
        part = self.part.run(1 - self.core, 0, self.first.size)
        return remote(part, self.recv_a.at[0], self.sem_a, 0, self.mate)

    def b_copy(self, i):
        return remote(self.half.at[i], self.recv_b.at[i], self.sem_b, i, self.ahead(i)[0])

    def c_copy(self, i, slot):
        there = moved(self.chip, self.second.steps[i])
        mine, target = self.recv_c.at[self.slot], self.recv_c.at[slot]
        return remote(mine, target, self.sem_c, i, (there, self.core))

    def e_copy(self, i, chunk):
        mine, target = self.total.one(self.core, self.chunk), self.total.one(self.core, chunk)
        return remote(mine, target, self.sem_e, i, self.ahead(i)[0])

    def f_copy(self, j, side):
        start, count = self.first.group_start(self.chip, j), self.first.members
        mine, target = self.total.run(self.core, start, count), self.total.run(side, start, count)
        return remote(mine, target, self.sem_f, j, self.mate)

    def a_to_b(self, i):
        if i == 0:
            self.a_copy().wait_recv()
        chunk = self.ahead(i)[1]
        other = Chunks(self.recv_a, self.part.per).one(0, chunk)
        self.half[i] = self.part.one(self.core, chunk)[...] + other[...]
        if i < self.last:
            self.b_copy(i).start()

    def b_to_c(self):
        chunk = self.half[self.last]
        for i in reversed(range(self.last)):
            self.b_copy(i).wait_recv()
            chunk = chunk + self.recv_b[i]
        self.recv_c[self.slot] = chunk
        for i in range(len(self.second.steps)):
            self.c_copy(i, self.slot).start()

    def c_to_e(self):
        for i in range(len(self.second.steps)):
            source = moved(self.chip, back(self.second.steps[i]))
            self.c_copy(i, self.second.number(source)).wait_recv()
        chunk = self.recv_c[0]
        for i in range(1, self.second.size):
            chunk = chunk + self.recv_c[i]
        self.total.one(self.core, self.chunk)[...] = chunk
        for i in range(self.last):
            self.e_copy(i, self.chunk).start()

    def e_to_f(self, j):
        for i in self.first.groups[j]:
            self.e_copy(i, self.behind(i)).wait_recv()
        self.f_copy(j, self.core).start()

    def finish(self):
        for j in range(len(self.first.groups)):
            self.f_copy(j, 1 - self.core).wait_recv()

    def drain_scatter(self):
        self.a_copy().wait_send()
        for i in range(self.last):
            self.b_copy(i).wait_send()
        for i in range(len(self.second.steps)):
            self.c_copy(i, self.slot).wait_send()

    def drain_gather(self):
        for i in range(self.last):
            self.e_copy(i, self.chunk).wait_send()
        for j in range(len(self.first.groups)):
            self.f_copy(j, self.core).wait_send()


def flow_scratch(first, second, half, shape, dtype):
    def pair(n):
        return pltpu.SemaphoreType.DMA((2, n))

    n1, n2 = len(first.steps), len(second.steps)
    return [
        pltpu.VMEM((1, *half), dtype),
        pltpu.VMEM((first.size, *shape), dtype),
        pltpu.VMEM((n1, *shape), dtype),
        pltpu.VMEM((second.size, *shape), dtype),
        pair(1),
        pair(n1),
        pair(n2),
        pair(n1),
        pair(len(first.groups)),
    ]


FLOW_SCRATCH = 9


class Flows:
    def __init__(self, *flows):
        self.flows = flows

    def in_turn(self, count, call):
        most = max(count(flow) for flow in self.flows)
        for i in range(most):
            for flow in self.flows:
                if i < count(flow):
                    call(flow, i)

    def start_a(self):
        for flow in self.flows:
            flow.a_copy().start()

    def a_to_b(self):
        self.in_turn(lambda f: f.first.size, lambda f, i: f.a_to_b(i))

    def b_to_c(self):
        for flow in reversed(self.flows):
            flow.b_to_c()

    def c_to_e(self):
        for flow in self.flows:
            flow.c_to_e()

    def e_to_f(self):
        self.in_turn(lambda f: len(f.first.groups), lambda f, j: f.e_to_f(j))

    def finish(self):
        for flow in self.flows:
            flow.finish()

    def drain_scatter(self):
        for flow in self.flows:
            flow.drain_scatter()

    def drain_gather(self):
        for flow in self.flows:
            flow.drain_gather()


PANEL = 16
PANELS = TILE // PANEL


def split3(wide):
    high = wide.astype(BF16)
    rest = wide - high.astype(F32)
    middle = rest.astype(BF16)
    low = (rest - middle.astype(F32)).astype(BF16)
    return high, middle, low


LEFT_THIRDS = (0, 0, 1, 0, 2, 1)
RIGHT_THIRDS = (0, 1, 0, 2, 0, 1)


def wide_dot(left, right):
    left, right = split3(left), split3(right)
    return dot(
        jnp.concatenate([left[i] for i in LEFT_THIRDS], axis=1),
        jnp.concatenate([right[i] for i in RIGHT_THIRDS], axis=0),
    )


def eliminate(a, panel):
    n, first = TILE, panel * PANEL
    mine = slice(first, first + PANEL)
    row = lax.broadcasted_iota(jnp.int32, (PANEL, n), 0)
    lane = lax.broadcasted_iota(jnp.int32, (PANEL, n), 1)
    square = [
        jnp.broadcast_to(a[mine, first + j : first + j + 1], (PANEL, n)) for j in range(PANEL)
    ]
    rows = jnp.where(
        (lane >= first) & (lane < first + PANEL),
        jnp.where(lane - first == row, 1.0, 0.0),
        a[mine],
    )
    for k in range(PANEL):
        inverse = 1.0 / square[k][k : k + 1]
        column = jnp.where(row == k, square[k] - 1.0, square[k])
        for j in range(k + 1, PANEL):
            square[j] = square[j] - column * (square[j][k : k + 1] * inverse)
        rows = rows - column * (rows[k : k + 1] * inverse)
    lane_all = lax.broadcasted_iota(jnp.int32, (n, n), 1)
    inside = (lane_all >= first) & (lane_all < first + PANEL)
    columns = jnp.where(inside, a, 0.0)
    if first:
        columns = pltpu.roll(columns, n - first, 1)
    left = [third.astype(F32) for third in split3(columns)]
    right = split3(rows)
    packed = left[0]
    for i, t in enumerate(LEFT_THIRDS[1:]):
        packed = packed + pltpu.roll(left[t], PANEL * (i + 1), 1)
    below = [right[t] for t in RIGHT_THIRDS]
    below.append(jnp.zeros((n - PANEL * len(below), n), BF16))
    change = dot(packed.astype(BF16), jnp.concatenate(below, axis=0))
    a = jnp.where(inside, 0.0, a) - change
    pieces = [a[:first], rows, a[first + PANEL :]]
    return jnp.concatenate([piece for piece in pieces if piece.shape[0]], axis=0)


def stacked_dot(thirds, right):
    rows = thirds[0].shape[0]
    whole = dot(jnp.concatenate(thirds, axis=0), right)
    return [whole[i * rows : (i + 1) * rows] for i in range(len(thirds))]


def product(left, right):
    high = stacked_dot(left, right[0])
    middle = stacked_dot(left[:2], right[1])
    low = dot(left[0], right[2])
    return high[0] + ((high[1] + middle[0]) + (high[2] + middle[1] + low))


LOG2E_SCALED = math.log2(math.e) / WIDTH


def column_norms(rows):
    wide = rows.astype(F32)
    return jnp.sum(wide * wide, axis=1, keepdims=True) * LOG2E_SCALED


def along_lanes(column):
    return jnp.transpose(jnp.broadcast_to(column, (column.shape[0], 128)))[0:1, :]


def kernel_of(cross, column, lane_row):
    return jnp.exp2((2.0 * LOG2E_SCALED) * cross - lane_row - column)


FETCH_ROWS = BLOCK // NQ
FETCH_CUT = 384
FETCH_REST = WIDTH - FETCH_CUT
HALF = BLOCK // 2
FETCH_FLOWS = (
    (Columns, Planes, (NQ, FETCH_ROWS, FETCH_CUT), (FETCH_ROWS, FETCH_CUT)),
    (Planes, Columns, (NQ, FETCH_ROWS, FETCH_REST), (NQ // NZ, FETCH_ROWS, FETCH_REST)),
)
SUM_FLOWS = (
    (Columns, Planes, (NQ, HALF // NQ, BLOCK), (HALF // NQ, BLOCK)),
    (Planes, Columns, (NZ, HALF // NZ, STEPS * TARGETS), (HALF // NZ, STEPS * TARGETS)),
)
CHUNKS = ROWS_DEV // CHUNK
CHUNK_TILES = CHUNK // TILE


def update_kernel(
    step_size,
    owner_ref,
    tiles_ref,
    feat_hbm,
    res_hbm,
    coef_hbm,
    update_ref,
    low_ref,
    slab_ref,
    res_ref,
    coef_ref,
    feat_ref,
    weighted_ref,
    along_ref,
    feat_sem,
    load_sem,
    masked,
    blocks,
    norm_ref,
    product_part,
    product_sum,
    grad_part,
    grad_sum,
    inv,
    thirds,
    between,
    swap_sem,
    *scratch,
):
    def load_feat(i):
        at = pl.ds(i * CHUNK_TILES, CHUNK_TILES)
        return pltpu.make_async_copy(feat_hbm.at[at], feat_ref.at[at], feat_sem.at[i])

    for i in range(CHUNKS):
        load_feat(i).start()
    loads = [
        pltpu.make_async_copy(source, target, load_sem.at[i])
        for i, (source, target) in enumerate([(res_hbm, res_ref), (coef_hbm, coef_ref)])
    ]
    chip, core = place()
    greet(chip, core)
    for load in loads:
        load.start()

    me = lax.axis_index("rows") * lax.axis_size("sub") + lax.axis_index("sub")
    for i in range(CHUNKS):
        load_feat(i).wait()
    per_tile = TILE // FETCH_ROWS

    def build(s):
        mine = jnp.full((FETCH_ROWS, WIDTH), (owner_ref[s] == me).astype(F32)).astype(BF16)
        for t in range(BLOCK // TILE):
            tile = feat_ref[tiles_ref[s, t]]
            for i in range(per_tile):
                at = slice(i * FETCH_ROWS, (i + 1) * FETCH_ROWS)
                masked[s, t * per_tile + i] = tile[at] * mine

    def pair_of(ref):
        return (
            Chunks(ref, 1, pl.ds(0, FETCH_CUT)),
            Chunks(ref, NQ // NZ, pl.ds(FETCH_CUT, FETCH_REST)),
        )

    def flows_of(kinds, parts, totals, scratch):
        flows = []
        for i, (first, second, _, _) in enumerate(kinds):
            mine = scratch[i * FLOW_SCRATCH : (i + 1) * FLOW_SCRATCH]
            flows.append(Flow(chip, core, first, second, parts[i], totals[i], mine))
        return Flows(*flows)

    fetch = flows_of(FETCH_FLOWS, pair_of(masked), pair_of(blocks), scratch)
    build(1 - core)
    await_greetings()
    fetch.start_a()
    build(core)
    fetch.a_to_b()

    def norms_of(i, carry):
        rows = feat_ref[pl.ds(i * CHUNK_TILES, CHUNK_TILES)].reshape(CHUNK, WIDTH)
        along_ref[i] = jnp.broadcast_to(along_lanes(column_norms(rows)), (8, CHUNK))
        return carry

    lax.fori_loop(0, CHUNKS, norms_of, 0)
    fetch.b_to_c()
    for load in loads:
        load.wait()
    weighted_ref[...] = (res_ref[...] - RIDGE * coef_ref[...]).astype(BF16)
    fetch.c_to_e()
    fetch.e_to_f()

    def block_rows(s):
        return blocks[s].reshape(BLOCK, WIDTH)

    def set_norm(s):
        norm_ref[s] = jnp.broadcast_to(column_norms(block_rows(s)), (BLOCK, 128))

    sides = [core] * CHUNKS + [1 - core] * CHUNKS
    units = len(sides)

    def cross_of(unit):
        i = unit % CHUNKS
        feat = feat_ref[i * CHUNK_TILES : (i + 1) * CHUNK_TILES].reshape(CHUNK, WIDTH)
        return dot_nt(block_rows(sides[unit]), feat)

    set_norm(core)
    cross = cross_of(0)
    for unit in range(units):
        i = unit % CHUNKS
        if unit == CHUNKS - 1:
            fetch.finish()
            set_norm(1 - core)
        later = cross_of(unit + 1) if unit + 1 < units else None
        slab = kernel_of(cross, norm_ref[sides[unit]][:, 0:1], along_ref[i][0:1, :]).astype(BF16)
        at = pl.ds(pl.multiple_of(sides[unit] * BLOCK, BLOCK), BLOCK)
        slab_ref[at, i * CHUNK : (i + 1) * CHUNK] = slab
        cross = later

    def share(half):
        at = [pl.ds(pl.multiple_of(s * BLOCK + half * HALF, HALF), HALF) for s in range(STEPS)]
        for s in range(STEPS):
            term = dot(slab_ref[at[s], :], weighted_ref[...]).reshape(NZ, HALF // NZ, TARGETS)
            grad_part[half, :, :, s * TARGETS : (s + 1) * TARGETS] = term
        term = dot_nt(slab_ref[at[0], :], slab_ref[BLOCK:, :])
        product_part[half] = term.reshape(product_part.shape[1:])

    sums = flows_of(
        SUM_FLOWS,
        (Chunks(product_part), Chunks(grad_part)),
        (Chunks(product_sum), Chunks(grad_sum)),
        scratch[2 * FLOW_SCRATCH :],
    )
    share(1 - core)
    sums.start_a()
    share(core)
    sums.a_to_b()

    def block_kernel(a, b):
        cross = dot_nt(block_rows(a), block_rows(b))
        return kernel_of(cross, norm_ref[a][:, 0:1], along_lanes(norm_ref[b][:, 0:1]))

    row = lax.broadcasted_iota(jnp.int32, (BLOCK, BLOCK), 0)
    lane = lax.broadcasted_iota(jnp.int32, (BLOCK, BLOCK), 1)
    inv[core] = block_kernel(core, core) + jnp.where(row == lane, RIDGE, 0.0)
    between[...] = block_kernel(0, 1).astype(BF16)
    fetch.drain_scatter()
    fetch.drain_gather()

    def spread(k, tile):
        at = pl.ds(pl.multiple_of(k * TILE, TILE), TILE)
        inside = lax.div(lax.broadcasted_iota(jnp.int32, (TILE, BLOCK), 1), TILE) == k
        lead = wide_dot(tile, inv[core, at, :])
        lead = jnp.where(inside, jnp.concatenate([tile] * (BLOCK // TILE), axis=1), lead)
        column = inv[core, :, at]
        inv[core, :, at] = jnp.zeros_like(column)
        inv[core] -= wide_dot(column, lead)
        inv[core, at, :] = lead

    stages = {(1, 0): sums.b_to_c, (2, 4): sums.c_to_e}

    def look(k, part):
        for (at_k, at_part), stage in stages.items():
            if at_part == part:
                pl.when(k == at_k)(stage)

    def step(k, carry):
        at = pl.ds(pl.multiple_of(k * TILE, TILE), TILE)
        for part in range(4):
            tile = inv[core, at, at]
            for panel in range(part * PANELS // 4, (part + 1) * PANELS // 4):
                tile = eliminate(tile, panel)
            inv[core, at, at] = tile
            look(k, part)
        spread(k, inv[core, at, at])
        look(k, 4)
        return carry

    lax.fori_loop(0, BLOCK // TILE, step, 0)

    def swap(side):
        return remote(inv.at[core], inv.at[side], swap_sem, 0, (chip, 1 - core))

    def split(s):
        for i, third in enumerate(split3(inv[s])):
            thirds[s, i] = third

    swap(core).start()
    split(core)
    swap(1 - core).wait_recv()
    split(1 - core)
    sums.drain_scatter()
    sums.e_to_f()
    sums.flows[1].finish()

    both = [[thirds[s, i] for i in range(3)] for s in range(STEPS)]
    grads = jnp.transpose(grad_sum[...].reshape(BLOCK, STEPS * TARGETS))
    first = product(split3(grads[:TARGETS]), both[0]) * step_size
    first_low = first.astype(BF16)
    past = sum(stacked_dot(split3(first), between[...]))
    sums.flows[0].finish()
    slab_product = product_sum[...].reshape(BLOCK, BLOCK)
    shift = sum(dot(first_low, third) for third in split3(slab_product))
    gradient = grads[TARGETS:] - shift - RIDGE * past
    second = product(split3(gradient), both[1]) * step_size
    for s, update in enumerate((first, second)):
        update_ref[s] = update
        low_ref[:, s * BLOCK : (s + 1) * BLOCK] = update.astype(BF16)

    swap(core).wait_send()
    sums.drain_gather()


def updates_of(step_size, block_owner, block_tiles, features, residual, coefficients):
    hbm = pl.BlockSpec(memory_space=pltpu.HBM)
    tiled = features.reshape(-1, TILE, WIDTH)
    slab_shape = (STEPS * BLOCK, ROWS_DEV)
    fetch_shape = (STEPS, NQ, FETCH_ROWS, WIDTH)
    product_shape = (2, NQ, HALF // NQ, BLOCK)
    grad_shape = (2, NZ, HALF // NZ, STEPS * TARGETS)
    flows = []
    for kind in FETCH_FLOWS:
        flows += flow_scratch(*kind, BF16)
    for kind in SUM_FLOWS:
        flows += flow_scratch(*kind, F32)
    return pl.pallas_call(
        functools.partial(update_kernel, step_size),
        out_shape=(
            pltpu.VMEM((STEPS, TARGETS, BLOCK), F32),
            pltpu.VMEM((TARGETS, STEPS * BLOCK), BF16),
            pltpu.VMEM(slab_shape, BF16),
            pltpu.VMEM(residual.shape, F32),
            pltpu.VMEM(coefficients.shape, F32),
        ),
        in_specs=[smem(), smem(), hbm, hbm, hbm],
        out_specs=(vmem(),) * 5,
        scratch_shapes=[
            pltpu.VMEM(tiled.shape, BF16),
            pltpu.VMEM(residual.shape, BF16),
            pltpu.VMEM((CHUNKS, 8, CHUNK), F32),
            pltpu.SemaphoreType.DMA((CHUNKS,)),
            pltpu.SemaphoreType.DMA((2,)),
            pltpu.VMEM(fetch_shape, BF16),
            pltpu.VMEM(fetch_shape, BF16),
            pltpu.VMEM((STEPS, BLOCK, 128), F32),
            pltpu.VMEM(product_shape, F32),
            pltpu.VMEM(product_shape, F32),
            pltpu.VMEM(grad_shape, F32),
            pltpu.VMEM(grad_shape, F32),
            pltpu.VMEM((STEPS, BLOCK, BLOCK), F32),
            pltpu.VMEM((STEPS, 3, BLOCK, BLOCK), BF16),
            pltpu.VMEM((BLOCK, BLOCK), BF16),
            pltpu.SemaphoreType.DMA((2, 1)),
            *flows,
        ],
        compiler_params=pltpu.CompilerParams(
            collective_id=0, has_side_effects=True, vmem_limit_bytes=48 << 20
        ),
        name="updates",
    )(block_owner, block_tiles, tiled, residual, coefficients)


ROWS_STEP = 512


def final_kernel(
    owner_ref,
    tiles_ref,
    update_ref,
    low_ref,
    slab_ref,
    res_ref,
    coef_ref,
    res_hbm,
    coef_hbm,
    res_new,
    coef_new,
    res_sem,
    coef_sem,
):
    me = lax.axis_index("rows") * lax.axis_size("sub") + lax.axis_index("sub")
    coef_new[...] = coef_ref[...]
    for s in range(STEPS):

        @pl.when(owner_ref[s] == me)
        def _():
            for t in range(BLOCK // TILE):
                at = pl.ds(pl.multiple_of(tiles_ref[s, t] * TILE, TILE), TILE)
                coef_new[at, :] += jnp.transpose(update_ref[s, :, t * TILE : (t + 1) * TILE])

    coef_copy = pltpu.make_async_copy(coef_new, coef_hbm, coef_sem)
    coef_copy.start()
    copies = []
    for i in range(res_ref.shape[0] // ROWS_STEP):
        here = pl.ds(i * ROWS_STEP, ROWS_STEP)
        res_new[here, :] = res_ref[here, :] - jnp.transpose(dot(low_ref[...], slab_ref[:, here]))
        copies.append(
            pltpu.make_async_copy(res_new.at[here, :], res_hbm.at[here, :], res_sem.at[i])
        )
        copies[-1].start()
    for copy in copies + [coef_copy]:
        copy.wait()


def final(owner, tiles, updates, low, slabs, residual, coefficients):
    rows = residual.shape[0]
    anywhere = pl.BlockSpec(memory_space=pl.ANY)
    return pl.pallas_call(
        final_kernel,
        out_shape=(
            jax.ShapeDtypeStruct(residual.shape, F32),
            jax.ShapeDtypeStruct(coefficients.shape, F32),
        ),
        in_specs=[smem(), smem(), vmem(), vmem(), vmem(), vmem(), vmem()],
        out_specs=(anywhere, anywhere),
        scratch_shapes=[
            pltpu.VMEM(residual.shape, F32),
            pltpu.VMEM(coefficients.shape, F32),
            pltpu.SemaphoreType.DMA((rows // ROWS_STEP,)),
            pltpu.SemaphoreType.DMA,
        ],
        compiler_params=pltpu.CompilerParams(vmem_limit_bytes=24 << 20),
        name="final",
    )(owner, tiles, updates, low, slabs, residual, coefficients)


def local(features, residual, coefficients, block_owner, block_tiles):
    devices = lax.axis_size("rows") * lax.axis_size("sub")
    step_size = 1.0 / math.sqrt(features.shape[0] * devices)
    results = updates_of(
        step_size, block_owner, block_tiles, features, residual, coefficients
    )
    return final(block_owner, block_tiles, *results)


def solution(mesh):
    in_specs = (
        P(("rows", "sub"), None),
        P(("rows", "sub"), None),
        P(("rows", "sub"), None),
        P(),
        P(),
    )
    out_specs = (P(("rows", "sub"), None), P(("rows", "sub"), None))
    return jax.shard_map(local, mesh=mesh, in_specs=in_specs, out_specs=out_specs, check_vma=False)
```

```python
import functools
import math

import jax
import jax.numpy as jnp
from jax import lax
from jax.experimental import pallas as pl
from jax.experimental.pallas import tpu as pltpu
from jax.sharding import PartitionSpec as P

MESH = pl.DeviceIdType.MESH
F32 = jnp.float32
BF16 = jnp.bfloat16

BLOCK = 512
TILE = 128
STEPS = 2
RIDGE = 0.5
WIDTH = 512
TARGETS = 128
NX, NY, NZ = 4, 4, 8
NQ = NX * NY
CHUNK = 1024
ROWS_DEV = 4096
VMEM_BYTES = 64 << 20


def vmem():
    return pl.BlockSpec(memory_space=pltpu.VMEM)


def smem():
    return pl.BlockSpec(memory_space=pltpu.SMEM)


def dot(a, b, precision=None):
    return jnp.dot(a, b, precision=precision, preferred_element_type=F32)


def dot_nt(a, b, precision=None):
    return lax.dot_general(
        a, b, (((1,), (1,)), ((), ())), precision=precision, preferred_element_type=F32
    )


def place():
    across, within = lax.axis_index("rows"), lax.axis_index("sub")
    core = lax.rem(across, 2)
    y = lax.rem(lax.div(across, 2), NY)
    z = lax.div(across, 2 * NY) * 2 + lax.rem(within, 2)
    x = lax.div(within, 2)
    return (x, y, z), core


def device(chip, core):
    x, y, z = chip
    return (lax.div(z, 2) * (2 * NY) + y * 2 + core, x * 2 + lax.rem(z, 2))


SIZES = (NX, NY, NZ)


def moved(chip, step):
    return tuple(
        lax.rem(c + (s + size) % size, size) if s % size else c
        for c, s, size in zip(chip, step, SIZES)
    )


def back(step):
    return tuple(-s for s in step)


def hops(step):
    return sum(min(s, size - s) for s, size in zip(step, SIZES))


COLUMN_STEPS = sorted(
    [(i, j, 0) for i in range(NX) for j in range(NY) if i or j], key=lambda s: -hops(s)
)
GROUP_STEPS = (2, 1, 3, 0)


class Columns:
    size = NX * NY
    steps = COLUMN_STEPS
    groups = [[i for i, s in enumerate(COLUMN_STEPS) if s[0] == dx] for dx in GROUP_STEPS]
    members = NY

    @staticmethod
    def number(chip):
        return chip[0] * NY + chip[1]

    @staticmethod
    def group_start(chip, j):
        return moved(chip, (-GROUP_STEPS[j], 0, 0))[0] * NY


class Planes:
    size = NZ
    steps = sorted([(0, 0, k) for k in range(1, NZ)], key=lambda s: -hops(s))

    groups = [list(range(NZ - 1))]
    members = NZ

    @staticmethod
    def number(chip):
        return chip[2]

    @staticmethod
    def group_start(chip, j):
        return 0


def greet(chip, core):
    barrier = pltpu.get_barrier_semaphore()
    others = [(moved(chip, step), core) for step in Columns.steps + Planes.steps]
    others.append((chip, 1 - core))
    for there, side in others:
        pl.semaphore_signal(barrier, inc=1, device_id=device(there, side), device_id_type=MESH)


def await_greetings():
    pl.semaphore_wait(pltpu.get_barrier_semaphore(), len(Columns.steps) + len(Planes.steps) + 1)


def remote(source, target, sems, i, where):
    return pltpu.make_async_remote_copy(
        src_ref=source,
        dst_ref=target,
        send_sem=sems.at[0, i],
        recv_sem=sems.at[1, i],
        device_id=device(*where),
        device_id_type=MESH,
    )


class Chunks:
    def __init__(self, ref, per=1, lanes=None):
        self.ref, self.per, self.lanes = ref, per, lanes

    def some(self, side, index):
        if self.lanes is None:
            return self.ref.at[side, index]
        return self.ref.at[side, index, :, self.lanes]

    def one(self, side, chunk):
        return self.some(side, chunk if self.per == 1 else pl.ds(self.per * chunk, self.per))

    def run(self, side, start, count):
        return self.some(side, pl.ds(self.per * start, self.per * count))


class Flow:
    def __init__(self, chip, core, first, second, part, total, scratch):
        self.chip, self.core, self.first, self.second = chip, core, first, second
        self.part, self.total = part, total
        self.recv_a, self.half, self.recv_b, self.recv_c = scratch[:4]
        self.sem_a, self.sem_b, self.sem_c, self.sem_e, self.sem_f = scratch[4:]
        self.steps = first.steps + [(0, 0, 0)]
        self.last = len(first.steps)
        self.mate = (chip, 1 - core)
        self.chunk = first.number(chip)
        self.slot = second.number(chip)

    def ahead(self, i):
        there = moved(self.chip, self.steps[i])
        return (there, self.core), self.first.number(there)

    def behind(self, i):
        return self.first.number(moved(self.chip, back(self.steps[i])))

    def a_copy(self):
        part = self.part.run(1 - self.core, 0, self.first.size)
        return remote(part, self.recv_a.at[0], self.sem_a, 0, self.mate)

    def b_copy(self, i):
        return remote(self.half.at[i], self.recv_b.at[i], self.sem_b, i, self.ahead(i)[0])

    def c_copy(self, i, slot):
        there = moved(self.chip, self.second.steps[i])
        mine, target = self.recv_c.at[self.slot], self.recv_c.at[slot]
        return remote(mine, target, self.sem_c, i, (there, self.core))

    def e_copy(self, i, chunk):
        mine, target = self.total.one(self.core, self.chunk), self.total.one(self.core, chunk)
        return remote(mine, target, self.sem_e, i, self.ahead(i)[0])

    def f_copy(self, j, side):
        start, count = self.first.group_start(self.chip, j), self.first.members
        mine, target = self.total.run(self.core, start, count), self.total.run(side, start, count)
        return remote(mine, target, self.sem_f, j, self.mate)

    def a_to_b(self, i):
        if i == 0:
            self.a_copy().wait_recv()
        chunk = self.ahead(i)[1]
        other = Chunks(self.recv_a, self.part.per).one(0, chunk)
        self.half[i] = self.part.one(self.core, chunk)[...] + other[...]
        if i < self.last:
            self.b_copy(i).start()

    def b_to_c(self):
        chunk = self.half[self.last]
        for i in reversed(range(self.last)):
            self.b_copy(i).wait_recv()
            chunk = chunk + self.recv_b[i]
        self.recv_c[self.slot] = chunk
        for i in range(len(self.second.steps)):
            self.c_copy(i, self.slot).start()

    def c_to_e(self):
        for i in range(len(self.second.steps)):
            source = moved(self.chip, back(self.second.steps[i]))
            self.c_copy(i, self.second.number(source)).wait_recv()
        chunk = self.recv_c[0]
        for i in range(1, self.second.size):
            chunk = chunk + self.recv_c[i]
        self.total.one(self.core, self.chunk)[...] = chunk
        for i in range(self.last):
            self.e_copy(i, self.chunk).start()

    def e_to_f(self, j):
        for i in self.first.groups[j]:
            self.e_copy(i, self.behind(i)).wait_recv()
        self.f_copy(j, self.core).start()

    def finish(self):
        for j in range(len(self.first.groups)):
            self.f_copy(j, 1 - self.core).wait_recv()

    def drain_scatter(self):
        self.a_copy().wait_send()
        for i in range(self.last):
            self.b_copy(i).wait_send()
        for i in range(len(self.second.steps)):
            self.c_copy(i, self.slot).wait_send()

    def drain_gather(self):
        for i in range(self.last):
            self.e_copy(i, self.chunk).wait_send()
        for j in range(len(self.first.groups)):
            self.f_copy(j, self.core).wait_send()


def flow_scratch(first, second, half, shape, dtype):
    def pair(n):
        return pltpu.SemaphoreType.DMA((2, n))

    n1, n2 = len(first.steps), len(second.steps)
    return [
        pltpu.VMEM((1, *half), dtype),
        pltpu.VMEM((first.size, *shape), dtype),
        pltpu.VMEM((n1, *shape), dtype),
        pltpu.VMEM((second.size, *shape), dtype),
        pair(1),
        pair(n1),
        pair(n2),
        pair(n1),
        pair(len(first.groups)),
    ]


FLOW_SCRATCH = 9


class Flows:
    def __init__(self, *flows):
        self.flows = flows

    def in_turn(self, count, call):
        most = max(count(flow) for flow in self.flows)
        for i in range(most):
            for flow in self.flows:
                if i < count(flow):
                    call(flow, i)

    def start_a(self):
        for flow in self.flows:
            flow.a_copy().start()

    def a_to_b(self):
        self.in_turn(lambda f: f.first.size, lambda f, i: f.a_to_b(i))

    def b_to_c(self):
        for flow in reversed(self.flows):
            flow.b_to_c()

    def c_to_e(self):
        for flow in self.flows:
            flow.c_to_e()

    def e_to_f(self):
        self.in_turn(lambda f: len(f.first.groups), lambda f, j: f.e_to_f(j))

    def finish(self):
        for flow in self.flows:
            flow.finish()

    def drain_scatter(self):
        for flow in self.flows:
            flow.drain_scatter()

    def drain_gather(self):
        for flow in self.flows:
            flow.drain_gather()


PANEL = 16
PANELS = TILE // PANEL


def split3(wide):
    high = wide.astype(BF16)
    rest = wide - high.astype(F32)
    middle = rest.astype(BF16)
    low = (rest - middle.astype(F32)).astype(BF16)
    return high, middle, low


LEFT_THIRDS = (0, 0, 1, 0, 2, 1)
RIGHT_THIRDS = (0, 1, 0, 2, 0, 1)


def wide_dot(left, right):
    left, right = split3(left), split3(right)
    return dot(
        jnp.concatenate([left[i] for i in LEFT_THIRDS], axis=1),
        jnp.concatenate([right[i] for i in RIGHT_THIRDS], axis=0),
    )


def eliminate(a, panel):
    n, first = TILE, panel * PANEL
    mine = slice(first, first + PANEL)
    row = lax.broadcasted_iota(jnp.int32, (PANEL, n), 0)
    lane = lax.broadcasted_iota(jnp.int32, (PANEL, n), 1)
    square = [
        jnp.broadcast_to(a[mine, first + j : first + j + 1], (PANEL, n)) for j in range(PANEL)
    ]
    rows = jnp.where(
        (lane >= first) & (lane < first + PANEL),
        jnp.where(lane - first == row, 1.0, 0.0),
        a[mine],
    )
    for k in range(PANEL):
        inverse = 1.0 / square[k][k : k + 1]
        column = jnp.where(row == k, square[k] - 1.0, square[k])
        for j in range(k + 1, PANEL):
            square[j] = square[j] - column * (square[j][k : k + 1] * inverse)
        rows = rows - column * (rows[k : k + 1] * inverse)
    lane_all = lax.broadcasted_iota(jnp.int32, (n, n), 1)
    inside = (lane_all >= first) & (lane_all < first + PANEL)
    columns = jnp.where(inside, a, 0.0)
    if first:
        columns = pltpu.roll(columns, n - first, 1)
    left = [third.astype(F32) for third in split3(columns)]
    right = split3(rows)
    packed = left[0]
    for i, t in enumerate(LEFT_THIRDS[1:]):
        packed = packed + pltpu.roll(left[t], PANEL * (i + 1), 1)
    below = [right[t] for t in RIGHT_THIRDS]
    below.append(jnp.zeros((n - PANEL * len(below), n), BF16))
    change = dot(packed.astype(BF16), jnp.concatenate(below, axis=0))
    a = jnp.where(inside, 0.0, a) - change
    pieces = [a[:first], rows, a[first + PANEL :]]
    return jnp.concatenate([piece for piece in pieces if piece.shape[0]], axis=0)


def stacked_dot(thirds, right):
    rows = thirds[0].shape[0]
    whole = dot(jnp.concatenate(thirds, axis=0), right)
    return [whole[i * rows : (i + 1) * rows] for i in range(len(thirds))]


def product(left, right):
    high = stacked_dot(left, right[0])
    middle = stacked_dot(left[:2], right[1])
    low = dot(left[0], right[2])
    return high[0] + ((high[1] + middle[0]) + (high[2] + middle[1] + low))


LOG2E_SCALED = math.log2(math.e) / WIDTH


def column_norms(rows):
    wide = rows.astype(F32)
    return jnp.sum(wide * wide, axis=1, keepdims=True) * LOG2E_SCALED


def along_lanes(column):
    return jnp.transpose(jnp.broadcast_to(column, (column.shape[0], 128)))[0:1, :]


def kernel_of(cross, column, lane_row):
    return jnp.exp2((2.0 * LOG2E_SCALED) * cross - lane_row - column)


FETCH_ROWS = BLOCK // NQ
FETCH_CUT = 384
FETCH_REST = WIDTH - FETCH_CUT
HALF = BLOCK // 2
FETCH_FLOWS = (
    (Columns, Planes, (NQ, FETCH_ROWS, FETCH_CUT), (FETCH_ROWS, FETCH_CUT)),
    (Planes, Columns, (NQ, FETCH_ROWS, FETCH_REST), (NQ // NZ, FETCH_ROWS, FETCH_REST)),
)
SUM_FLOWS = (
    (Columns, Planes, (NQ, HALF // NQ, BLOCK), (HALF // NQ, BLOCK)),
    (Planes, Columns, (NZ, HALF // NZ, STEPS * TARGETS), (HALF // NZ, STEPS * TARGETS)),
)
CHUNKS = ROWS_DEV // CHUNK
CHUNK_TILES = CHUNK // TILE


def update_kernel(
    step_size,
    owner_ref,
    tiles_ref,
    feat_hbm,
    res_hbm,
    coef_hbm,
    update_ref,
    low_ref,
    slab_ref,
    res_ref,
    coef_ref,
    feat_ref,
    weighted_ref,
    along_ref,
    feat_sem,
    load_sem,
    masked,
    blocks,
    norm_ref,
    product_part,
    product_sum,
    grad_part,
    grad_sum,
    inv,
    thirds,
    between,
    swap_sem,
    *scratch,
):
    def load_feat(i):
        at = pl.ds(i * CHUNK_TILES, CHUNK_TILES)
        return pltpu.make_async_copy(feat_hbm.at[at], feat_ref.at[at], feat_sem.at[i])

    for i in range(CHUNKS):
        load_feat(i).start()
    loads = [
        pltpu.make_async_copy(source, target, load_sem.at[i])
        for i, (source, target) in enumerate([(res_hbm, res_ref), (coef_hbm, coef_ref)])
    ]
    chip, core = place()
    greet(chip, core)
    for load in loads:
        load.start()

    me = lax.axis_index("rows") * lax.axis_size("sub") + lax.axis_index("sub")
    for i in range(CHUNKS):
        load_feat(i).wait()
    per_tile = TILE // FETCH_ROWS

    def build(s):
        mine = jnp.full((FETCH_ROWS, WIDTH), (owner_ref[s] == me).astype(F32)).astype(BF16)
        for t in range(BLOCK // TILE):
            tile = feat_ref[tiles_ref[s, t]]
            for i in range(per_tile):
                at = slice(i * FETCH_ROWS, (i + 1) * FETCH_ROWS)
                masked[s, t * per_tile + i] = tile[at] * mine

    def pair_of(ref):
        return (
            Chunks(ref, 1, pl.ds(0, FETCH_CUT)),
            Chunks(ref, NQ // NZ, pl.ds(FETCH_CUT, FETCH_REST)),
        )

    def flows_of(kinds, parts, totals, scratch):
        flows = []
        for i, (first, second, _, _) in enumerate(kinds):
            mine = scratch[i * FLOW_SCRATCH : (i + 1) * FLOW_SCRATCH]
            flows.append(Flow(chip, core, first, second, parts[i], totals[i], mine))
        return Flows(*flows)

    fetch = flows_of(FETCH_FLOWS, pair_of(masked), pair_of(blocks), scratch)
    build(1 - core)
    await_greetings()
    fetch.start_a()
    build(core)
    fetch.a_to_b()

    def norms_of(i, carry):
        rows = feat_ref[pl.ds(i * CHUNK_TILES, CHUNK_TILES)].reshape(CHUNK, WIDTH)
        along_ref[i] = jnp.broadcast_to(along_lanes(column_norms(rows)), (8, CHUNK))
        return carry

    lax.fori_loop(0, CHUNKS, norms_of, 0)
    fetch.b_to_c()
    for load in loads:
        load.wait()
    weighted_ref[...] = (res_ref[...] - RIDGE * coef_ref[...]).astype(BF16)
    fetch.c_to_e()
    fetch.e_to_f()

    def block_rows(s):
        return blocks[s].reshape(BLOCK, WIDTH)

    def set_norm(s):
        norm_ref[s] = jnp.broadcast_to(column_norms(block_rows(s)), (BLOCK, 128))

    sides = [core] * CHUNKS + [1 - core] * CHUNKS
    units = len(sides)

    def cross_of(unit):
        i = unit % CHUNKS
        feat = feat_ref[i * CHUNK_TILES : (i + 1) * CHUNK_TILES].reshape(CHUNK, WIDTH)
        return dot_nt(block_rows(sides[unit]), feat)

    set_norm(core)
    cross = cross_of(0)
    for unit in range(units):
        i = unit % CHUNKS
        if unit == CHUNKS - 1:
            fetch.finish()
            set_norm(1 - core)
        later = cross_of(unit + 1) if unit + 1 < units else None
        slab = kernel_of(cross, norm_ref[sides[unit]][:, 0:1], along_ref[i][0:1, :]).astype(BF16)
        at = pl.ds(pl.multiple_of(sides[unit] * BLOCK, BLOCK), BLOCK)
        slab_ref[at, i * CHUNK : (i + 1) * CHUNK] = slab
        cross = later

    def share(half):
        at = [pl.ds(pl.multiple_of(s * BLOCK + half * HALF, HALF), HALF) for s in range(STEPS)]
        for s in range(STEPS):
            term = dot(slab_ref[at[s], :], weighted_ref[...]).reshape(NZ, HALF // NZ, TARGETS)
            grad_part[half, :, :, s * TARGETS : (s + 1) * TARGETS] = term
        term = dot_nt(slab_ref[at[0], :], slab_ref[BLOCK:, :])
        product_part[half] = term.reshape(product_part.shape[1:])

    sums = flows_of(
        SUM_FLOWS,
        (Chunks(product_part), Chunks(grad_part)),
        (Chunks(product_sum), Chunks(grad_sum)),
        scratch[2 * FLOW_SCRATCH :],
    )
    share(1 - core)
    sums.start_a()
    share(core)
    sums.a_to_b()

    def block_kernel(a, b):
        cross = dot_nt(block_rows(a), block_rows(b))
        return kernel_of(cross, norm_ref[a][:, 0:1], along_lanes(norm_ref[b][:, 0:1]))

    row = lax.broadcasted_iota(jnp.int32, (BLOCK, BLOCK), 0)
    lane = lax.broadcasted_iota(jnp.int32, (BLOCK, BLOCK), 1)
    inv[core] = block_kernel(core, core) + jnp.where(row == lane, RIDGE, 0.0)
    between[...] = block_kernel(0, 1).astype(BF16)
    fetch.drain_scatter()
    fetch.drain_gather()

    def spread(k, tile):
        at = pl.ds(pl.multiple_of(k * TILE, TILE), TILE)
        inside = lax.div(lax.broadcasted_iota(jnp.int32, (TILE, BLOCK), 1), TILE) == k
        lead = wide_dot(tile, inv[core, at, :])
        lead = jnp.where(inside, jnp.concatenate([tile] * (BLOCK // TILE), axis=1), lead)
        column = inv[core, :, at]
        inv[core, :, at] = jnp.zeros_like(column)
        inv[core] -= wide_dot(column, lead)
        inv[core, at, :] = lead

    stages = {(1, 0): sums.b_to_c, (2, 4): sums.c_to_e}

    def look(k, part):
        for (at_k, at_part), stage in stages.items():
            if at_part == part:
                pl.when(k == at_k)(stage)

    def step(k, carry):
        at = pl.ds(pl.multiple_of(k * TILE, TILE), TILE)
        for part in range(4):
            tile = inv[core, at, at]
            for panel in range(part * PANELS // 4, (part + 1) * PANELS // 4):
                tile = eliminate(tile, panel)
            inv[core, at, at] = tile
            look(k, part)
        spread(k, inv[core, at, at])
        look(k, 4)
        return carry

    lax.fori_loop(0, BLOCK // TILE, step, 0)

    def swap(side):
        return remote(inv.at[core], inv.at[side], swap_sem, 0, (chip, 1 - core))

    def split(s):
        for i, third in enumerate(split3(inv[s])):
            thirds[s, i] = third

    swap(core).start()
    split(core)
    swap(1 - core).wait_recv()
    split(1 - core)
    sums.drain_scatter()
    sums.e_to_f()
    sums.flows[1].finish()

    both = [[thirds[s, i] for i in range(3)] for s in range(STEPS)]
    grads = jnp.transpose(grad_sum[...].reshape(BLOCK, STEPS * TARGETS))
    first = product(split3(grads[:TARGETS]), both[0]) * step_size
    first_low = first.astype(BF16)
    past = sum(stacked_dot(split3(first), between[...]))
    sums.flows[0].finish()
    slab_product = product_sum[...].reshape(BLOCK, BLOCK)
    shift = sum(dot(first_low, third) for third in split3(slab_product))
    gradient = grads[TARGETS:] - shift - RIDGE * past
    second = product(split3(gradient), both[1]) * step_size
    for s, update in enumerate((first, second)):
        update_ref[s] = update
        low_ref[:, s * BLOCK : (s + 1) * BLOCK] = update.astype(BF16)

    swap(core).wait_send()
    sums.drain_gather()


def updates_of(step_size, block_owner, block_tiles, features, residual, coefficients):
    hbm = pl.BlockSpec(memory_space=pltpu.HBM)
    tiled = features.reshape(-1, TILE, WIDTH)
    slab_shape = (STEPS * BLOCK, ROWS_DEV)
    fetch_shape = (STEPS, NQ, FETCH_ROWS, WIDTH)
    product_shape = (2, NQ, HALF // NQ, BLOCK)
    grad_shape = (2, NZ, HALF // NZ, STEPS * TARGETS)
    flows = []
    for kind in FETCH_FLOWS:
        flows += flow_scratch(*kind, BF16)
    for kind in SUM_FLOWS:
        flows += flow_scratch(*kind, F32)
    return pl.pallas_call(
        functools.partial(update_kernel, step_size),
        out_shape=(
            pltpu.VMEM((STEPS, TARGETS, BLOCK), F32),
            pltpu.VMEM((TARGETS, STEPS * BLOCK), BF16),
            pltpu.VMEM(slab_shape, BF16),
            pltpu.VMEM(residual.shape, F32),
            pltpu.VMEM(coefficients.shape, F32),
        ),
        in_specs=[smem(), smem(), hbm, hbm, hbm],
        out_specs=(vmem(),) * 5,
        scratch_shapes=[
            pltpu.VMEM(tiled.shape, BF16),
            pltpu.VMEM(residual.shape, BF16),
            pltpu.VMEM((CHUNKS, 8, CHUNK), F32),
            pltpu.SemaphoreType.DMA((CHUNKS,)),
            pltpu.SemaphoreType.DMA((2,)),
            pltpu.VMEM(fetch_shape, BF16),
            pltpu.VMEM(fetch_shape, BF16),
            pltpu.VMEM((STEPS, BLOCK, 128), F32),
            pltpu.VMEM(product_shape, F32),
            pltpu.VMEM(product_shape, F32),
            pltpu.VMEM(grad_shape, F32),
            pltpu.VMEM(grad_shape, F32),
            pltpu.VMEM((STEPS, BLOCK, BLOCK), F32),
            pltpu.VMEM((STEPS, 3, BLOCK, BLOCK), BF16),
            pltpu.VMEM((BLOCK, BLOCK), BF16),
            pltpu.SemaphoreType.DMA((2, 1)),
            *flows,
        ],
        compiler_params=pltpu.CompilerParams(
            collective_id=0, has_side_effects=True, vmem_limit_bytes=48 << 20
        ),
        name="updates",
    )(block_owner, block_tiles, tiled, residual, coefficients)


ROWS_STEP = 512


def final_kernel(
    owner_ref,
    tiles_ref,
    update_ref,
    low_ref,
    slab_ref,
    res_ref,
    coef_ref,
    res_hbm,
    coef_hbm,
    res_new,
    coef_new,
    res_sem,
    coef_sem,
):
    me = lax.axis_index("rows") * lax.axis_size("sub") + lax.axis_index("sub")
    owns = (owner_ref[0] == me) | (owner_ref[1] == me)

    @pl.when(jnp.logical_not(owns))
    def _():
        pltpu.make_async_copy(coef_ref, coef_hbm, coef_sem).start()

    @pl.when(owns)
    def _():
        coef_new[...] = coef_ref[...]

    for s in range(STEPS):

        @pl.when(owner_ref[s] == me)
        def _():
            for t in range(BLOCK // TILE):
                at = pl.ds(pl.multiple_of(tiles_ref[s, t] * TILE, TILE), TILE)
                coef_new[at, :] += jnp.transpose(update_ref[s, :, t * TILE : (t + 1) * TILE])

    coef_copy = pltpu.make_async_copy(coef_new, coef_hbm, coef_sem)

    @pl.when(owns)
    def _():
        coef_copy.start()

    copies = []
    for i in range(res_ref.shape[0] // ROWS_STEP):
        here = pl.ds(i * ROWS_STEP, ROWS_STEP)
        res_new[here, :] = res_ref[here, :] - jnp.transpose(dot(low_ref[...], slab_ref[:, here]))
        copies.append(
            pltpu.make_async_copy(res_new.at[here, :], res_hbm.at[here, :], res_sem.at[i])
        )
        copies[-1].start()
    for copy in copies + [coef_copy]:
        copy.wait()


def final(owner, tiles, updates, low, slabs, residual, coefficients):
    rows = residual.shape[0]
    anywhere = pl.BlockSpec(memory_space=pl.ANY)
    return pl.pallas_call(
        final_kernel,
        out_shape=(
            jax.ShapeDtypeStruct(residual.shape, F32),
            jax.ShapeDtypeStruct(coefficients.shape, F32),
        ),
        in_specs=[smem(), smem(), vmem(), vmem(), vmem(), vmem(), vmem()],
        out_specs=(anywhere, anywhere),
        scratch_shapes=[
            pltpu.VMEM(residual.shape, F32),
            pltpu.VMEM(coefficients.shape, F32),
            pltpu.SemaphoreType.DMA((rows // ROWS_STEP,)),
            pltpu.SemaphoreType.DMA,
        ],
        compiler_params=pltpu.CompilerParams(vmem_limit_bytes=24 << 20),
        name="final",
    )(owner, tiles, updates, low, slabs, residual, coefficients)


def local(features, residual, coefficients, block_owner, block_tiles):
    devices = lax.axis_size("rows") * lax.axis_size("sub")
    step_size = 1.0 / math.sqrt(features.shape[0] * devices)
    results = updates_of(
        step_size, block_owner, block_tiles, features, residual, coefficients
    )
    return final(block_owner, block_tiles, *results)


def solution(mesh):
    in_specs = (
        P(("rows", "sub"), None),
        P(("rows", "sub"), None),
        P(("rows", "sub"), None),
        P(),
        P(),
    )
    out_specs = (P(("rows", "sub"), None), P(("rows", "sub"), None))
    return jax.shard_map(local, mesh=mesh, in_specs=in_specs, out_specs=out_specs, check_vma=False)
```
